32 devices in a mesh: rows: 16 (over z, y, x), seq: 2 (over core).
Axes of the slice: x: 2, y: 2, z: 4, core: 2. Of those that a mesh axis runs over, the one named last changes fastest.
Arguments:
- tokens: bfloat16 [16, 256, 768], P('rows', 'seq'), may hold values from -6 to 6
- marks: int32 [16, 256], P('rows', 'seq'), may hold values from 0 to 1, as said below
- norm_gain: float32 [768], replicated, may hold values from 0.5 to 1.5
- in_weight: bfloat16 [768, 3072], replicated, may hold values from -0.21875 to 0.21875
- conv_weight: float32 [4, 1536], replicated, may hold values from -3 to 3
- conv_bias: float32 [1536], replicated, may hold values from -3 to 3
- x_weight: bfloat16 [80, 1536], replicated, may hold values from -0.15625 to 0.15625
- dt_weight: bfloat16 [48, 1536], replicated, may hold values from -0.875 to 0.875
- dt_bias: float32 [1536], replicated, may hold values from -6.9 to -2.3
- a_log: float32 [16, 1536], replicated, may hold values from 0 to 2.77
- skip: float32 [1536], replicated, may hold values from 0.5 to 1.5
- out_weight: bfloat16 [1536, 768], replicated, may hold values from -0.4375 to 0.4375
- cotangent: bfloat16 [16, 256, 768], P('rows', 'seq'), may hold values from -6 to 6
Outputs:
- output: bfloat16 [16, 256, 768], P('rows', 'seq')
- grad_tokens: bfloat16 [16, 256, 768], P('rows', 'seq')
- grad_gain: float32 [768], replicated
- grad_in: float32 [768, 3072], replicated
- grad_conv: float32 [4, 1536], replicated
- grad_conv_bias: float32 [1536], replicated
- grad_x: float32 [80, 1536], replicated
- grad_dt: float32 [48, 1536], replicated
- grad_dt_bias: float32 [1536], replicated
- grad_a_log: float32 [16, 1536], replicated
- grad_skip: float32 [1536], replicated
- grad_out: float32 [1536, 768], replicated
The draws below stay inside these ranges and needn't reach their ends.
Inputs may be any that keep to these rules, and one draw needn't show every extreme that they name: `marks`: in every row, one to three positions among 1 to 63 hold 1 (at least one), and zero to three among the last 64 positions; all other entries are 0.
All inputs are finite; a program needn't handle non-finite values.
Results may differ from the reference program's by a relative error of at most 0.012.
The reference program's roundings to bfloat16 on the way count: a program that leaves them out, or rounds other values in their place, can miss the bound.
Values may be sent and summed in bfloat16 or wider, within the bound.
A program may use at most 128 MiB of HBM per device.

```python
import jax
import jax.numpy as jnp
from jax import lax

D = 768
E = 1536
NS = 16
RANK = 48
CONV = 4
LEN = 256
GROUP = 128
ROWS = 16


def draw_marks(key, part):
    key = jax.random.fold_in(key, 11)
    first_key, last_key, pick_key = jax.random.split(key, 3)
    quarter = LEN // 4
    early = jax.random.randint(first_key, (ROWS, 3), 1, quarter)
    late = jax.random.randint(last_key, (ROWS, 3), LEN - quarter, LEN)
    active = jax.random.randint(pick_key, (ROWS, 6), 0, 2)
    active = active.at[:, 0].set(1)
    spots = jnp.concatenate([early, late], axis=1)
    places = jnp.arange(LEN, dtype=jnp.int32)
    hits = (places[None, None, :] == spots[:, :, None]) & (active[:, :, None] == 1)
    return jnp.any(hits, axis=1).astype(jnp.int32)


def level_of(key, shape, shards, smallest, largest):
    factor_of = 1.0
    for dim, blocks in shards:
        heights = jax.random.uniform(jax.random.fold_in(jax.random.fold_in(key, 6), dim), (blocks,), jnp.float32, smallest / len(shards), largest / len(shards))
        factor_of = factor_of * jnp.repeat(jnp.exp(heights), shape[dim] // blocks).reshape((-1,) + (1,) * (len(shape) - 1 - dim))
    return factor_of


def gaussian(own_key, shape, scale, most, cuts=(), kind=jnp.bfloat16):
    array = scale * jax.random.normal(own_key, shape, jnp.float32)
    if cuts:
        array = array * level_of(own_key, shape, cuts, -0.22, 0.18)
    return jnp.clip(array, -most, most).astype(kind)


def setup_inputs(seed: int = 0) -> dict:
    seeds = jax.random.split(jax.random.key(seed), 14)
    tokens = gaussian(seeds[0], (ROWS, LEN, D), 1.0, 6.0, ((0, 16), (1, 2)))
    marks = draw_marks(jax.random.fold_in(seeds[13], 71), 0)
    norm_gain = jnp.clip(1.0 + 0.1 * jax.random.normal(seeds[2], (D,), jnp.float32), 0.5, 1.5)
    in_weight = gaussian(seeds[3], (D, 2 * E), D ** -0.5, 0.21875)
    conv_weight = gaussian(seeds[4], (CONV, E), 0.5, 3.0, (), jnp.float32)
    conv_bias = gaussian(seeds[5], (E,), 0.5, 3.0, (), jnp.float32)
    x_weight = gaussian(seeds[6], (RANK + 2 * NS, E), E ** -0.5, 0.15625)
    dt_weight = gaussian(seeds[7], (RANK, E), RANK ** -0.5, 0.875)
    dt_bias = jnp.clip(jax.random.uniform(seeds[8], (E,), jnp.float32, -6.9, -2.3), -6.9, -2.3)
    a_log = jnp.clip(jax.random.uniform(seeds[9], (NS, E), jnp.float32, 0.0, 2.77), 0.0, 2.77)
    skip = jnp.clip(jax.random.uniform(seeds[10], (E,), jnp.float32, 0.5, 1.5), 0.5, 1.5)
    out_weight = gaussian(seeds[11], (E, D), (E // 8) ** -0.5, 0.4375)
    cotangent = gaussian(seeds[12], (ROWS, LEN, D), 1.0, 6.0, ((0, 16), (1, 2)))
    return dict(tokens=tokens, marks=marks, norm_gain=norm_gain, in_weight=in_weight, conv_weight=conv_weight, conv_bias=conv_bias, x_weight=x_weight, dt_weight=dt_weight, dt_bias=dt_bias, a_log=a_log, skip=skip, out_weight=out_weight, cotangent=cotangent)


@jax.custom_vjp
def low(v):
    return lax.optimization_barrier(v.astype(jnp.bfloat16)).astype(jnp.float32)

@jax.custom_vjp
def low_back(v):
    return v

def low_keep(v):
    return (low(v), None)

def low_pass(kept, grad):
    return (grad,)

def back_keep(v):
    return (v, None)

def back_low(kept, grad):
    return (low(grad),)
low.defvjp(low_keep, low_pass)
low_back.defvjp(back_keep, back_low)
epsilon = 1e-05
highest = lax.Precision.HIGHEST

def mix_states(h_start, decay, inflow, c_rows):

    def step(state, item):
        factor, source, reader = item
        state = factor * state + source
        return (state, lax.optimization_barrier(jnp.sum(state * reader[:, None], axis=0)))
    return lax.scan(step, h_start, (decay, inflow, c_rows))

def row_forward(row, marks, gain, w_in, conv_w, conv_b, w_x, w_dt, dt_b, a_log, skip, w_out):
    length = row.shape[0]
    scale = lax.rsqrt(lax.optimization_barrier(jnp.mean(row * row, axis=-1, keepdims=True)) + epsilon)
    normed = low(row * scale * gain)
    both = low_back(jnp.dot(normed, w_in, precision=highest))
    inner = low(both[:, :E])
    gate = both[:, E:]
    segment = jnp.cumsum(marks, dtype=jnp.int32)
    conv = conv_b + conv_w[CONV - 1] * inner
    for shift_by in range(1, CONV):
        earlier = jnp.concatenate([jnp.zeros((shift_by, E), inner.dtype), inner[:length - shift_by]], axis=0)
        seg_before = jnp.concatenate([jnp.zeros((shift_by,), jnp.int32), segment[:length - shift_by]])
        same = (seg_before == segment).astype(inner.dtype)
        conv = conv + conv_w[CONV - 1 - shift_by] * earlier * same[:, None]
    act = jax.nn.silu(conv)
    proj = low_back(jnp.dot(w_x, low(act).T, precision=highest))
    rank_part = low(proj[:RANK])
    pre = low_back(jnp.dot(rank_part.T, w_dt, precision=highest)) + dt_b
    delta = jax.nn.softplus(pre)
    b_rows = proj[RANK:RANK + NS].T
    c_rows = proj[RANK + NS:].T
    a_neg = -jnp.exp(a_log)
    keep = (1 - marks).astype(delta.dtype)
    blocks = length // GROUP

    def one_block(state, pieces):
        d_b, x_b, b_b, c_b, k_b = pieces
        decay = jnp.exp(d_b[:, None, :] * a_neg[None]) * k_b[:, None, None]
        inflow = (d_b * x_b)[:, None, :] * b_b[:, :, None]
        return mix_states(state, decay, inflow, c_b)
    pieces = (delta.reshape(blocks, GROUP, E), act.reshape(blocks, GROUP, E), b_rows.reshape(blocks, GROUP, NS), c_rows.reshape(blocks, GROUP, NS), keep.reshape(blocks, GROUP))
    _, mixed = lax.scan(jax.checkpoint(one_block), jnp.zeros((NS, E), delta.dtype), pieces)
    y_values = mixed.reshape(length, E) + skip * act
    y_values = low(low_back(y_values))
    gated = y_values * jax.nn.silu(gate)
    return row + jnp.dot(low(gated), w_out, precision=highest)

def reference(tokens, marks, norm_gain, in_weight, conv_weight, conv_bias, x_weight, dt_weight, dt_bias, a_log, skip, out_weight, cotangent):
    wide = jnp.float32

    def forward(rows_in, gain, w_in, conv_w, conv_b, w_x, w_dt, dt_b, logs, gains, w_out):

        def one(carry, item):
            row, row_marks = item
            result = jax.checkpoint(row_forward)(row, row_marks, gain, w_in, conv_w, conv_b, w_x, w_dt, dt_b, logs, gains, w_out)
            return (carry, result)
        _, result = lax.scan(one, jnp.zeros((), wide), (rows_in, marks))
        return result
    output, pull = jax.vjp(forward, tokens.astype(wide), norm_gain, in_weight.astype(wide), conv_weight, conv_bias, x_weight.astype(wide), dt_weight.astype(wide), dt_bias, a_log, skip, out_weight.astype(wide))
    grads = pull(cotangent.astype(wide))
    return (output.astype(jnp.bfloat16), grads[0].astype(jnp.bfloat16), grads[1], grads[2], grads[3], grads[4], grads[5], grads[6], grads[7], grads[8], grads[9], grads[10])
```

```python
import jax
import jax.numpy as jnp
from jax import lax
from jax.experimental import pallas as pl
from jax.experimental.pallas import tpu as pltpu
from jax.sharding import PartitionSpec as P

f32 = jnp.float32
bf16 = jnp.bfloat16
EPS = 1e-05
LOG2E = 1.4426950408889634
LN2 = 0.6931471805599453
LANES = 128
STEP = 16
PLANE = 4
DEPTH = 4
TEAM = PLANE * DEPTH
MESH = pl.DeviceIdType.MESH
NN = (((1,), (0,)), ((), ()))
NT = (((1,), (1,)), ((), ()))
TN = (((0,), (0,)), ((), ()))


def mm(a, b, dims=NN):
    return lax.dot_general(a, b, dims, preferred_element_type=f32)


def lane_tiles(width, size):
    return [slice(j, j + size) for j in range(0, width, size)]


def body_kernel(
    tok, marks, gain, win, cw, cb, xw, dtw, dtb, alog, skip, wout, cot,
    out, gtok, gin, gout, small,
    win_i, win_g, wo, nfull, gfull, nh, gh, mk, mcol,
    inner, gate, dgated, act, dsilu, actl, ddec, u, ul, sig, dyf, dyl, du, s1, sq,
    pp, pq, pp2, pq2, hs, bt, ct, cbd, bbd, gbuf, qbuf, mc, mb,
    gt, dgl, dpl, dil, dconv, dn, dnr, outp, outr,
    fac, pf, pown, pb, zr, res, sm, smb, fs, zs, ress,
    ls, ss, rs,
):
    row, core = lax.axis_index("rows"), lax.axis_index("seq")
    other = 1 - core
    team = row - row % TEAM
    px, py, pz = row % 2, (row // 2) % 2, (row // PLANE) % DEPTH
    tl, d = tok.shape
    t = 2 * tl
    w = wo.shape[0]
    states = alog.shape[0]
    rank = dtw.shape[0]
    nproj = xw.shape[0]
    half = w // 2
    zrows = half // DEPTH
    chunks = t // STEP
    tiles = w // LANES
    mine = pl.multiple_of(core * tl, tl)
    theirs = pl.multiple_of(other * tl, tl)
    chan = pl.multiple_of(core * w, w)
    halves = lane_tiles(w, half)
    pending = []

    def plane_peer(s):
        x, y = s % 2, s // 2
        qx, qy = px + x - 2 * x * px, py + y - 2 * y * py
        return team + pz * PLANE + qy * 2 + qx, qx, qy

    def z_peer(s):
        return (pz + s) % DEPTH

    def send(k, src, dst, to_row, to_core):
        copy = pltpu.make_async_remote_copy(
            src_ref=src,
            dst_ref=dst,
            send_sem=ss.at[k],
            recv_sem=rs.at[k],
            device_id=(to_row, to_core),
            device_id_type=MESH,
        )
        copy.start()
        pending.append(copy)
        return copy

    def at_half(index):
        return pl.ds(pl.multiple_of(index * half, half), half)

    ids = iter(range(10_000))

    loads = [
        pltpu.make_async_copy(win.at[:, pl.ds(chan, w)], win_i, ls.at[0]),
        pltpu.make_async_copy(
            win.at[:, pl.ds(pl.multiple_of(2 * w + core * w, w), w)], win_g, ls.at[1]
        ),
        pltpu.make_async_copy(wout.at[pl.ds(chan, w), :], wo, ls.at[2]),
    ]
    for copy in loads:
        copy.start()

    gain_row = gain[...]
    unit = 2 * STEP

    def norm_block(b, carry):
        at = pl.multiple_of(b * unit, unit)
        rows = tok[pl.ds(at, unit), :].astype(f32)
        scale = lax.rsqrt(jnp.mean(rows * rows, axis=-1, keepdims=True) + EPS)
        nfull[pl.ds(mine + at, unit), :] = (rows * scale * gain_row).astype(bf16)
        gfull[pl.ds(mine + at, unit), :] = cot[pl.ds(at, unit), :]
        return carry

    lax.fori_loop(0, tl // unit, norm_block, 0)
    mk[:, pl.ds(mine, tl)] = jnp.broadcast_to(marks[...].astype(f32), (8, tl))

    barrier = pltpu.get_barrier_semaphore()
    partners = [(row, other)]
    partners += [(plane_peer(s)[0], core) for s in range(1, PLANE)]
    partners += [(team + z_peer(s) * PLANE + py * 2 + px, core) for s in range(1, DEPTH)]
    for partner in partners:
        pl.semaphore_signal(barrier, inc=1, device_id=partner, device_id_type=MESH)
    pl.semaphore_wait(barrier, len(partners))

    twin = []
    for ref in (nfull, gfull):
        part = ref.at[pl.ds(mine, tl), :]
        twin.append(send(next(ids), part, part, row, other))
    part = mk.at[:, pl.ds(mine, tl)]
    twin.append(send(next(ids), part, part, row, other))
    early = []
    for s in range(1, PLANE):
        peer, qx, qy = plane_peer(s)
        for full, dest in ((nfull, nh), (gfull, gh)):
            early.append(
                (
                    s,
                    dest,
                    send(
                        next(ids),
                        full.at[pl.ds(mine, tl), at_half(qy)],
                        dest.at[s - 1, pl.ds(mine, tl), :],
                        peer,
                        core,
                    ),
                )
            )

    inner[0:8, :] = jnp.zeros((8, w), f32)
    dconv[t : t + 8, :] = jnp.zeros((8, w), f32)
    mcol[t : t + 8, :] = jnp.zeros((8, LANES), f32)
    hs[0:states, :] = jnp.zeros((states, w), bf16)
    sm[...] = jnp.zeros(sm.shape, f32)

    for copy in loads:
        copy.wait()
    for copy in twin:
        copy.wait_recv()

    for sl in lane_tiles(w, 2 * LANES):
        inner[8 : 8 + t, sl] = mm(nfull[...], win_i[:, sl]).astype(bf16).astype(f32)

    lane = lax.broadcasted_iota(jnp.int32, (8, t), 1)
    mark = mk[...]
    keep = jnp.where(lane == 0, 0.0, 1.0 - mark)
    mask2 = keep * pltpu.roll(keep, 1, 1)
    mask3 = mask2 * pltpu.roll(keep, 2, 1)
    line = lax.broadcasted_iota(jnp.int32, (LANES, t), 0)

    def spread(v):
        return jnp.broadcast_to(v[0:1, :], (LANES, t))

    stacked = jnp.where(line == 0, spread(keep), 0.0)
    stacked = jnp.where(line == 1, spread(mask2), stacked)
    stacked = jnp.where(line == 2, spread(mask3), stacked)
    stacked = jnp.where(line == 3, spread(mark), stacked)
    mcol[0:t, :] = stacked.T

    cw_own = cw[:, pl.ds(chan, w)]
    cb_own = cb[:, pl.ds(chan, w)]
    taps = cw.shape[0]

    def conv_block(b, carry):
        at = pl.multiple_of(b * STEP, STEP)
        view = inner.at[pl.ds(at, STEP + 8)]
        masks = mcol[pl.ds(at, STEP), :]
        for sl in halves:
            total = cb_own[:, sl] + cw_own[taps - 1 : taps, sl] * view[8 : 8 + STEP, sl]
            for j in range(1, taps):
                tap = cw_own[taps - 1 - j : taps - j, sl]
                total = total + tap * view[8 - j : 8 - j + STEP, sl] * masks[:, j - 1 : j]
            sg = 1.0 / (1.0 + jnp.exp(-total))
            value = total * sg
            act[pl.ds(at, STEP), sl] = value
            actl[pl.ds(at, STEP), sl] = value.astype(bf16)
            dsilu[pl.ds(at, STEP), sl] = sg * (1.0 + total * (1.0 - sg))
        return carry

    lax.fori_loop(0, chunks, conv_block, 0)
    xw_own = xw[:, pl.ds(chan, w)]
    pp[:, 0:nproj] = mm(actl[...], xw_own, NT)
    proj_copy = send(next(ids), pp, pq, row, other)

    for sl in lane_tiles(w, 2 * LANES):
        gate[:, sl] = mm(nfull[...], win_g[:, sl])
        dgated[:, sl] = mm(gfull[...], wo[sl, :], NT)

    def dy_block(b, carry):
        at = pl.ds(pl.multiple_of(b * STEP, STEP), STEP)
        for sl in halves:
            g = gate[at, sl]
            low = (dgated[at, sl] * (g / (1.0 + jnp.exp(-g)))).astype(bf16)
            dyl[at, sl] = low
            dyf[at, sl] = low.astype(f32)
        return carry

    lax.fori_loop(0, chunks, dy_block, 0)

    relays = []
    for s, dest, copy in early:
        copy.wait_recv()
        part = dest.at[s - 1, pl.ds(mine, tl), :]
        relays.append(send(next(ids), part, part, row, other))

    proj_copy.wait_recv()
    proj = pp[...] + pq[...]
    turned = proj.T
    for k in range(chunks):
        cols = slice(k * STEP, (k + 1) * STEP)
        bt[k, :, 0:STEP] = turned[rank : rank + states, cols]
        ct[k, :, 0:STEP] = turned[rank + states : rank + 2 * states, cols]
    rank_low = proj[:, 0:rank].astype(bf16)
    rank_turned = turned[0:rank, :].astype(bf16)
    dtw_own = dtw[:, pl.ds(chan, w)]
    dtb_own = dtb[:, pl.ds(chan, w)]
    for sl in lane_tiles(w, 2 * LANES):
        sig[:, sl] = mm(rank_low, dtw_own[:, sl]) + dtb_own[:, sl]

    def delta_block(b, carry):
        at = pl.ds(pl.multiple_of(b * STEP, STEP), STEP)
        marked = mcol[at, :][:, 3:4] > 0.5
        for sl in halves:
            pre = sig[at, sl]
            e = jnp.exp(-jnp.abs(pre))
            one = 1.0 + e
            log1p = jnp.where(one == 1.0, e, jnp.log(one) * (e / (one - 1.0)))
            delta = jnp.maximum(pre, 0.0) + log1p
            sig[at, sl] = jnp.where(pre >= 0.0, 1.0, e) / one
            inflow = delta * act[at, sl]
            u[at, sl] = inflow
            ul[at, sl] = inflow.astype(bf16)
            s1[at, sl] = delta
            ddec[at, sl] = jnp.where(marked, 1e30, delta)
        return carry

    lax.fori_loop(0, chunks, delta_block, 0)

    span = STEP * states
    pick = (
        lax.broadcasted_iota(jnp.int32, (states, span), 0)
        == lax.broadcasted_iota(jnp.int32, (states, span), 1) % states
    ).astype(bf16)
    diag = (
        lax.broadcasted_iota(jnp.int32, (t, span), 0) % STEP
        == lax.broadcasted_iota(jnp.int32, (t, span), 1) // states
    )
    ones_diag = diag[0:STEP].astype(bf16)
    b_low = proj[:, rank : rank + states].astype(bf16)
    c_low = proj[:, rank + states : rank + 2 * states].astype(bf16)
    bbd[...] = jnp.where(diag, mm(b_low, pick), 0.0).astype(bf16)
    cbd[...] = jnp.where(diag, mm(c_low, pick), 0.0).astype(bf16)

    rates = [-jnp.exp(alog[:, pl.ds(chan + j * LANES, LANES)]) * LOG2E for j in range(tiles)]
    zeros = tuple(jnp.zeros((states, LANES), f32) for _ in range(tiles))

    def scan_chunk(k, state):
        base = pl.multiple_of(k * STEP, STEP)
        b_here = bt[k]
        dec, flow = ddec.at[pl.ds(base, STEP)], u.at[pl.ds(base, STEP)]
        state = list(state)
        for i in range(STEP):
            b_wide = jnp.broadcast_to(b_here[:, i : i + 1], (states, LANES))
            for j in range(tiles):
                sl = slice(j * LANES, (j + 1) * LANES)
                decay = jnp.exp2(dec[i : i + 1, sl] * rates[j])
                state[j] = decay * state[j] + flow[i : i + 1, sl] * b_wide
                hs[pl.ds(pl.multiple_of((base + i + 1) * states, states), states), sl] = state[
                    j
                ].astype(bf16)
        kept = hs[pl.ds(pl.multiple_of((base + 1) * states, states), span), :]
        du[pl.ds(base, STEP), :] = mm(cbd[pl.ds(base, STEP), :], kept)
        return tuple(state)

    lax.fori_loop(0, chunks, scan_chunk, zeros)

    skip_own = skip[:, pl.ds(chan, w)]

    def gated_block(b, carry):
        at = pl.ds(pl.multiple_of(b * STEP, STEP), STEP)
        for sl in halves:
            y = (du[at, sl] + skip_own[:, sl] * act[at, sl]).astype(bf16).astype(f32)
            g = gate[at, sl]
            sg = 1.0 / (1.0 + jnp.exp(-g))
            gt[at, sl] = (y * (g * sg)).astype(bf16)
            dgl[at, sl] = (dgated[at, sl] * y * (sg * (1.0 + g * (1.0 - sg)))).astype(bf16)
        return carry

    lax.fori_loop(0, chunks, gated_block, 0)

    def send_factors(n, source):
        copies = []
        for s in range(1, PLANE):
            peer, qx, qy = plane_peer(s)
            copies.append(
                send(next(ids), source.at[:, at_half(qx)], fac.at[n, s - 1], peer, core)
            )
        return copies

    fac_out = send_factors(0, gt)
    fac_gate = send_factors(1, dgl)

    for sl in lane_tiles(d, 2 * LANES):
        outp[:, sl] = mm(gt[...], wo[:, sl])
    out_copy = send(next(ids), outp.at[pl.ds(theirs, tl), :], outr, row, other)
    for sl in lane_tiles(d, 2 * LANES):
        dn[:, sl] = mm(dgl[...], win_g[sl, :], NT)

    def at_shard(n, z):
        first = px if n == 0 else py
        second = py if n == 0 else px
        return (
            pl.ds(pl.multiple_of(first * half + z * zrows, zrows), zrows),
            at_half(second),
        )

    def partial_sum(n, source, copies):
        for copy in copies:
            copy.wait_recv()
        for sl in lane_tiles(half, LANES):
            if n == 0:
                lefts = [source[:, at_half(px)][:, sl]] + [fac[0, s, :, sl] for s in range(PLANE - 1)]
                rights = [gfull[:, at_half(py)]] + [gh[s] for s in range(PLANE - 1)]
            else:
                lefts = [nfull[:, at_half(py)][:, sl]] + [nh[s, :, sl] for s in range(PLANE - 1)]
                rights = [source[:, at_half(px)]] + [fac[n, s] for s in range(PLANE - 1)]
            total = mm(lefts[0], rights[0], TN)
            for a, b in zip(lefts[1:], rights[1:]):
                total = total + mm(a, b, TN)
            pf[sl, :] = total
            pb[n, sl, :] = total.astype(bf16)
        pown[n] = pf[pl.ds(pl.multiple_of(pz * zrows, zrows), zrows), :]
        copies = []
        for s in range(1, DEPTH):
            to = z_peer(s)
            copies.append(
                send(
                    next(ids),
                    pb.at[n, pl.ds(pl.multiple_of(to * zrows, zrows), zrows), :],
                    zr.at[n, s - 1],
                    team + to * PLANE + py * 2 + px,
                    core,
                )
            )
        return copies

    def to_plane(n, z):
        rows, cols = at_shard(n, z)
        part = res.at[n, rows, cols]
        return [send(next(ids), part, part, plane_peer(s)[0], core) for s in range(1, PLANE)]

    def total_sum(n, copies):
        for copy in copies:
            copy.wait_recv()
        total = pown[n]
        for s in range(DEPTH - 1):
            total = total + zr[n, s].astype(f32)
        rows, cols = at_shard(n, pz)
        res[n, rows, cols] = total.astype(bf16)
        part = res.at[n, rows, cols]
        along = [
            send(next(ids), part, part, team + z_peer(s) * PLANE + py * 2 + px, core)
            for s in range(1, DEPTH)
        ]
        return along, to_plane(n, pz)

    def pass_on(n, along, across):
        for s in range(1, DEPTH):
            along[s - 1].wait_recv()
            across = across + to_plane(n, (pz + DEPTH - s) % DEPTH)
        return across

    def place_of(n):
        if n == 0:
            return gout.at[pl.ds(chan, w), :]
        return gin.at[:, pl.ds(pl.multiple_of((2 - n) * 2 * w + core * w, w), w)]

    locals_ = []

    def finish(n, across):
        for copy in across:
            copy.wait_recv()
        copy = pltpu.make_async_copy(res.at[n], place_of(n), ls.at[3 + n])
        copy.start()
        locals_.append(copy)
        return send(next(ids), res.at[n], place_of(n), row, other)

    def back_chunk(kk, carry):
        k = chunks - 1 - kk
        base = pl.multiple_of(k * STEP, STEP)
        c_here = ct[k]
        dec, dys = ddec.at[pl.ds(base, STEP)], dyf.at[pl.ds(base, STEP)]
        flow, acc = list(carry[0]), list(carry[1])
        for i in reversed(range(STEP)):
            c_wide = jnp.broadcast_to(c_here[:, i : i + 1], (states, LANES))
            line_at = slice(i * states, (i + 1) * states)
            for j in range(tiles):
                sl = slice(j * LANES, (j + 1) * LANES)
                rate = dec[i : i + 1, sl]
                g = c_wide * dys[i : i + 1, sl] + flow[j]
                gbuf[line_at, sl] = g.astype(bf16)
                flow[j] = g * jnp.exp2(rate * rates[j])
                before = hs[pl.ds(pl.multiple_of((base + i) * states, states), states), sl]
                q = flow[j] * before.astype(f32)
                acc[j] = acc[j] + q * rate
                qbuf[line_at, sl] = (q * rates[j]).astype(bf16)
        rows = pl.ds(base, STEP)
        kept = hs[pl.ds(pl.multiple_of((base + 1) * states, states), span), :]
        du[rows, :] = mm(bbd[rows, :], gbuf[...])
        sq[rows, :] = mm(ones_diag, qbuf[...])
        mc[rows, :] = mm(dyl[rows, :], kept, NT)
        mb[rows, :] = mm(ul[rows, :], gbuf[...], NT)
        return tuple(flow), tuple(acc)

    out_copy.wait_recv()

    def out_block(b, carry):
        at = pl.multiple_of(b * STEP, STEP)
        rows = pl.ds(at, STEP)
        total = outp[pl.ds(mine + at, STEP), :] + outr[rows, :]
        out[rows, :] = (tok[rows, :].astype(f32) + total).astype(bf16)
        return carry

    lax.fori_loop(0, tl // STEP, out_block, 0)

    marks_at = [chunks * p // 16 for p in (0, 4, 8, 11, 14, 16)]
    carry = (zeros, zeros)
    carry = lax.fori_loop(marks_at[0], marks_at[1], back_chunk, carry)
    for copy in relays:
        copy.wait_recv()
    z_out = partial_sum(0, gt, fac_out)
    carry = lax.fori_loop(marks_at[1], marks_at[2], back_chunk, carry)
    z_gate = partial_sum(1, dgl, fac_gate)
    carry = lax.fori_loop(marks_at[2], marks_at[3], back_chunk, carry)
    a_out = total_sum(0, z_out)
    carry = lax.fori_loop(marks_at[3], marks_at[4], back_chunk, carry)
    a_gate = total_sum(1, z_gate)
    c_out = pass_on(0, *a_out)
    carry = lax.fori_loop(marks_at[4], marks_at[5], back_chunk, carry)
    acc = carry[1]

    def fold(m):
        v = jnp.where(diag, m[...], 0.0)
        high = v.astype(bf16)
        rest = (v - high.astype(f32)).astype(bf16)
        return mm(high, pick, NT) + mm(rest, pick, NT)

    def dpre_block(b, carry):
        at = pl.ds(pl.multiple_of(b * STEP, STEP), STEP)
        sums, gains = [], []
        for n, sl in enumerate(halves):
            flow, value, dy = du[at, sl], act[at, sl], dyf[at, sl]
            dpre = (sq[at, sl] * LN2 + flow * value) * sig[at, sl]
            dpl[at, sl] = dpre.astype(bf16)
            du[at, sl] = flow * s1[at, sl] + skip_own[:, sl] * dy
            both = dy * value
            sums.append(carry[0][n] + dpre[0:8] + dpre[8:16])
            gains.append(carry[1][n] + both[0:8] + both[8:16])
        return tuple(sums), tuple(gains)

    none = tuple(jnp.zeros((8, half), f32) for _ in halves)
    sums, gains = lax.fori_loop(0, chunks, dpre_block, (none, none))
    first = nproj + rank + states
    line_conv, line_cb, line_dtb, line_skip, line_gain = (
        first,
        first + taps,
        first + taps + 1,
        first + taps + 2,
        first + taps + 3,
    )
    for n, sl in enumerate(halves):
        sm[line_dtb : line_dtb + 1, sl] = jnp.sum(sums[n], axis=0, keepdims=True)
        sm[line_skip : line_skip + 1, sl] = jnp.sum(gains[n], axis=0, keepdims=True)
    for j in range(tiles):
        sl = slice(j * LANES, (j + 1) * LANES)
        sm[nproj + rank : first, sl] = acc[j] * rates[j] * LN2

    pp2[:, 0:rank] = mm(dpl[...], dtw_own, NT)
    pp2[:, rank : rank + states] = fold(mb)
    pp2[:, rank + states : nproj] = fold(mc)
    dproj_copy = send(next(ids), pp2, pq2, row, other)
    for sl in lane_tiles(w, 2 * LANES):
        sm[nproj : nproj + rank, sl] = mm(rank_turned, dpl[:, sl])
    c_gate = pass_on(1, *a_gate)
    dproj_copy.wait_recv()
    dproj = pp2[...] + pq2[...]
    dproj_low = dproj[:, 0:nproj].astype(bf16)
    dproj_turned = dproj.T[0:nproj, :].astype(bf16)
    for sl in lane_tiles(w, 2 * LANES):
        sq[:, sl] = mm(dproj_low, xw_own[:, sl])

    def dconv_block(b, carry):
        at = pl.multiple_of(b * STEP, STEP)
        view = inner.at[pl.ds(at, STEP + 8)]
        rows = pl.ds(at, STEP)
        masks = mcol[rows, :]
        sums = [list(v) for v in carry]
        for n, sl in enumerate(halves):
            grad = (du[rows, sl] + sq[rows, sl]) * dsilu[rows, sl]
            dconv[rows, sl] = grad
            terms = [grad, grad * view[8 : 8 + STEP, sl]]
            for j in range(1, taps):
                terms.append(grad * masks[:, j - 1 : j] * view[8 - j : 8 - j + STEP, sl])
            for m, term in enumerate(terms):
                sums[m][n] = sums[m][n] + term[0:8] + term[8:16]
        return tuple(tuple(v) for v in sums)

    sums = lax.fori_loop(0, chunks, dconv_block, (none,) * (taps + 1))
    for n, sl in enumerate(halves):
        sm[line_cb : line_cb + 1, sl] = jnp.sum(sums[0][n], axis=0, keepdims=True)
        for j in range(taps):
            at = line_conv + taps - 1 - j
            sm[at : at + 1, sl] = jnp.sum(sums[1 + j][n], axis=0, keepdims=True)

    def dinner_block(b, carry):
        at = pl.multiple_of(b * STEP, STEP)
        view = dconv.at[pl.ds(at, STEP + 8)]
        masks = mcol.at[pl.ds(at, STEP + 8)]
        for sl in halves:
            total = cw_own[taps - 1 : taps, sl] * view[0:STEP, sl]
            for j in range(1, taps):
                tap = cw_own[taps - 1 - j : taps - j, sl]
                total = total + tap * view[j : j + STEP, sl] * masks[j : j + STEP, j - 1 : j]
            dil[pl.ds(at, STEP), sl] = total.astype(bf16)
        return carry

    lax.fori_loop(0, chunks, dinner_block, 0)
    fac_in = send_factors(2, dil)
    for sl in lane_tiles(d, 2 * LANES):
        dn[:, sl] = dn[:, sl] + mm(dil[...], win_i[sl, :], NT)
    dn_copy = send(next(ids), dn.at[pl.ds(theirs, tl), :], dnr, row, other)
    for sl in lane_tiles(w, 2 * LANES):
        sm[0:nproj, sl] = mm(dproj_turned, actl[:, sl])
    twin_out = finish(0, c_out)
    dn_copy.wait_recv()

    def norm_back(b, carry):
        at = pl.multiple_of(b * STEP, STEP)
        rows = pl.ds(at, STEP)
        values = tok[rows, :].astype(f32)
        scale = lax.rsqrt(jnp.mean(values * values, axis=-1, keepdims=True) + EPS)
        unit_rows = values * scale
        grad = dn[pl.ds(mine + at, STEP), :] + dnr[rows, :]
        inside = grad * gain_row
        mean = jnp.mean(inside * unit_rows, axis=-1, keepdims=True)
        both = grad * unit_rows
        gtok[rows, :] = (cot[rows, :].astype(f32) + scale * (inside - unit_rows * mean)).astype(bf16)
        return carry + both[0:8] + both[8:16]

    total = lax.fori_loop(0, tl // STEP, norm_back, jnp.zeros((8, d), f32))
    sm[line_gain : line_gain + 1, :] = jnp.sum(total, axis=0, keepdims=True)
    smb[...] = sm[...].astype(bf16)

    srows = smb.shape[0] // 2
    small_at = pl.ds(pl.multiple_of(py * srows, srows), srows)
    over_plane = []
    for s in range(1, PLANE):
        peer, qx, qy = plane_peer(s)
        over_plane.append(
            send(
                next(ids),
                smb.at[pl.ds(pl.multiple_of(qy * srows, srows), srows), at_half(qx)],
                fs.at[s - 1],
                peer,
                core,
            )
        )

    z_in = partial_sum(2, dil, fac_in)
    for copy in over_plane:
        copy.wait_recv()
    total = sm[small_at, at_half(px)]
    for s in range(PLANE - 1):
        total = total + fs[s].astype(f32)
    zs[pz] = total.astype(bf16)
    over_z = [
        send(next(ids), zs.at[pz], zs.at[pz], team + z_peer(s) * PLANE + py * 2 + px, core)
        for s in range(1, DEPTH)
    ]
    a_in = total_sum(2, z_in)
    for copy in over_z:
        copy.wait_recv()
    total = zs[0].astype(f32)
    for s in range(1, DEPTH):
        total = total + zs[s].astype(f32)
    ress[small_at, at_half(px)] = total.astype(bf16)
    part = ress.at[small_at, at_half(px)]
    small_across = [send(next(ids), part, part, plane_peer(s)[0], core) for s in range(1, PLANE)]
    twin_gate = finish(1, c_gate)
    c_in = pass_on(2, *a_in)
    for copy in small_across:
        copy.wait_recv()
    small_copy = pltpu.make_async_copy(ress, small.at[:, pl.ds(chan, w)], ls.at[6])
    small_copy.start()
    locals_.append(small_copy)
    twin_small = send(next(ids), ress, small.at[:, pl.ds(chan, w)], row, other)
    twin_in = finish(2, c_in)
    for copy in (twin_out, twin_gate, twin_small, twin_in):
        copy.wait_recv()
    for copy in locals_:
        copy.wait()
    for copy in pending:
        copy.wait_send()


def wide_kernel(gin, gout, small, gin_f, gout_f, *rows):
    gin_f[...] = gin[...].astype(f32)
    gout_f[...] = gout[...].astype(f32)

    @pl.when(pl.program_id(0) == 0)
    def _():
        whole = small[...].astype(f32)
        first = 0
        for ref in rows[:-1]:
            count = ref.shape[0]
            ref[...] = whole[first : first + count, :]
            first += count
        width = rows[-1].shape[1]
        line = whole[first : first + 1, :]
        rows[-1][...] = line[:, 0:width] + line[:, width : 2 * width]


def local(
    tokens, marks, norm_gain, in_weight, conv_weight, conv_bias, x_weight, dt_weight,
    dt_bias, a_log, skip, out_weight, cotangent,
):
    tl, d = tokens.shape[1:]
    e = out_weight.shape[0]
    w = e // lax.axis_size("seq")
    t = tl * lax.axis_size("seq")
    states, rank, nproj, taps = a_log.shape[0], dt_weight.shape[0], x_weight.shape[0], conv_weight.shape[0]
    half, chunks, span = w // 2, t // STEP, STEP * states
    zrows = half // DEPTH
    lines = -(-(nproj + rank + states + taps + 4) // 32) * 32
    vmem = pl.BlockSpec(memory_space=pltpu.VMEM)
    anywhere = pl.BlockSpec(memory_space=pl.ANY)
    wide = pltpu.VMEM((t, w), f32)
    low = pltpu.VMEM((t, w), bf16)
    scratch = [
        pltpu.VMEM((d, w), bf16), pltpu.VMEM((d, w), bf16), pltpu.VMEM((w, d), bf16),
        pltpu.VMEM((t, d), bf16), pltpu.VMEM((t, d), bf16),
        pltpu.VMEM((PLANE - 1, t, half), bf16), pltpu.VMEM((PLANE - 1, t, half), bf16),
        pltpu.VMEM((8, t), f32), pltpu.VMEM((t + 8, LANES), f32),
        pltpu.VMEM((t + 8, w), f32), wide, wide, wide, wide, low, wide, wide, low, wide, wide, low,
        wide, wide, wide,
        pltpu.VMEM((t, LANES), f32), pltpu.VMEM((t, LANES), f32),
        pltpu.VMEM((t, LANES), f32), pltpu.VMEM((t, LANES), f32),
        pltpu.VMEM(((t + 1) * states, w), bf16),
        pltpu.VMEM((chunks, states, LANES), f32), pltpu.VMEM((chunks, states, LANES), f32),
        pltpu.VMEM((t, span), bf16), pltpu.VMEM((t, span), bf16),
        pltpu.VMEM((span, w), bf16), pltpu.VMEM((span, w), bf16),
        pltpu.VMEM((t, span), f32), pltpu.VMEM((t, span), f32),
        low, low, low, low, pltpu.VMEM((t + 8, w), f32),
        pltpu.VMEM((t, d), f32), pltpu.VMEM((tl, d), f32),
        pltpu.VMEM((t, d), f32), pltpu.VMEM((tl, d), f32),
        pltpu.VMEM((3, PLANE - 1, t, half), bf16), pltpu.VMEM((half, half), f32),
        pltpu.VMEM((3, zrows, half), f32), pltpu.VMEM((3, half, half), bf16),
        pltpu.VMEM((3, DEPTH - 1, zrows, half), bf16), pltpu.VMEM((3, w, d), bf16),
        pltpu.VMEM((lines, w), f32), pltpu.VMEM((lines, w), bf16),
        pltpu.VMEM((PLANE - 1, lines // 2, half), bf16), pltpu.VMEM((DEPTH, lines // 2, half), bf16),
        pltpu.VMEM((lines, w), bf16),
        pltpu.SemaphoreType.DMA((8,)),
        pltpu.SemaphoreType.DMA((112,)), pltpu.SemaphoreType.DMA((112,)),
    ]
    output, grad_tokens, gin, gout, small = pl.pallas_call(
        body_kernel,
        out_shape=[
            jax.ShapeDtypeStruct((tl, d), bf16),
            jax.ShapeDtypeStruct((tl, d), bf16),
            jax.ShapeDtypeStruct((d, 2 * e), bf16),
            jax.ShapeDtypeStruct((e, d), bf16),
            jax.ShapeDtypeStruct((lines, e), bf16),
        ],
        in_specs=[vmem, vmem, vmem, anywhere] + [vmem] * 7 + [anywhere, vmem],
        out_specs=[vmem, vmem, anywhere, anywhere, anywhere],
        scratch_shapes=scratch,
        compiler_params=pltpu.CompilerParams(
            collective_id=0, has_side_effects=True, vmem_limit_bytes=60 * 2**20
        ),
        name="block",
    )(
        tokens.reshape(tl, d), marks.reshape(1, tl), norm_gain.reshape(1, d), in_weight, conv_weight,
        conv_bias.reshape(1, e), x_weight, dt_weight, dt_bias.reshape(1, e), a_log,
        skip.reshape(1, e), out_weight, cotangent.reshape(tl, d),
    )

    steps = 8
    shapes = [(nproj, e), (rank, e), (states, e), (taps, e), (1, e), (1, e), (1, e), (1, d)]
    once = [pl.BlockSpec(s, lambda i: (0, 0)) for s in shapes]
    gin_spec = pl.BlockSpec((d // steps, 2 * e), lambda i: (i, 0))
    gout_spec = pl.BlockSpec((e // steps, d), lambda i: (i, 0))
    grads = pl.pallas_call(
        wide_kernel,
        grid=(steps,),
        out_shape=[jax.ShapeDtypeStruct(s, f32) for s in [(d, 2 * e), (e, d)] + shapes],
        in_specs=[gin_spec, gout_spec, pl.BlockSpec((lines, e), lambda i: (0, 0))],
        out_specs=[gin_spec, gout_spec] + once,
        compiler_params=pltpu.CompilerParams(vmem_limit_bytes=32 * 2**20),
        name="widen",
    )(gin, gout, small)
    rows = lax.axis_size("rows")
    if rows > TEAM:
        grads = [v * (1.0 / TEAM) for v in lax.psum(grads, "rows")]
    grad_in, grad_out, grad_x, grad_dt, grad_log, grad_conv, g_cb, g_dtb, g_skip, g_gain = grads
    return (
        output[None], grad_tokens[None], g_gain.reshape(d), grad_in, grad_conv, g_cb.reshape(e), grad_x,
        grad_dt, g_dtb.reshape(e), grad_log, g_skip.reshape(e), grad_out,
    )


def solution(mesh):
    split = P("rows", "seq", None)
    whole = P()
    in_specs = (split, P("rows", "seq")) + (whole,) * 10 + (split,)
    out_specs = (split, split) + (whole,) * 10
    return jax.shard_map(local, mesh=mesh, in_specs=in_specs, out_specs=out_specs, check_vma=False)
```

```python
import functools

import jax
import jax.numpy as jnp
from jax import lax
from jax.experimental import pallas as pl
from jax.experimental.pallas import tpu as pltpu
from jax.sharding import PartitionSpec as P

f32 = jnp.float32
bf16 = jnp.bfloat16
EPS = 1e-05
LANES = 128
STEP = 16
PLANE = 4
DEPTH = 4
TEAM = PLANE * DEPTH
MESH = pl.DeviceIdType.MESH
NN = (((1,), (0,)), ((), ()))
NT = (((1,), (1,)), ((), ()))


def mm(a, b, dims=NN):
    return lax.dot_general(a, b, dims, preferred_element_type=f32)


def lane_tiles(width, size):
    return [slice(j, j + size) for j in range(0, width, size)]


def body_kernel(
    tok, marks, gain, win, cw, cb, xw, dtw, dtb, alog, skip, wout, cot,
    out, gtok, gin, gout, small,
    win_i, win_g, wo, ng, ngh, mk, mcol, lines,
    inner, gate, dgated, act, dsilu, actl, ddec, u, sig, dyf, du, s1, sq,
    pp, pq, pp2, pq2, tsc, even, odd, bt, ct, cbd, bbd, ga, gb, qa, qb, ba, bb, ca, cc, dbt, dct,
    gt, dgl, dpl, dil, turn, dconv, dn, dnr, outp, outr,
    fac, pw, pown, pb, zr, res, sm, smb, smf, sfac, szr, sres, sown, sfin,
    ls, ss, rs,
):
    row, core = lax.axis_index("rows"), lax.axis_index("seq")
    other = 1 - core
    team = row - row % TEAM
    px, py, pz = row % 2, (row // 2) % 2, (row // PLANE) % DEPTH
    tl, d = tok.shape
    t = 2 * tl
    w = wo.shape[0]
    states = alog.shape[0]
    rank = dtw.shape[0]
    nproj = xw.shape[0]
    half = w // 2
    quarter = w // PLANE
    zrows = quarter // DEPTH
    place = row % PLANE
    chunks = t // STEP
    tiles = w // LANES
    mine = pl.multiple_of(core * tl, tl)
    theirs = pl.multiple_of(other * tl, tl)
    chan = pl.multiple_of(core * w, w)
    halves = lane_tiles(w, half)
    pending = []

    def plane_place(s):
        x, y = s % 2, s // 2
        return (py + y - 2 * y * py) * 2 + px + x - 2 * x * px

    def plane_row(s):
        return team + pz * PLANE + plane_place(s)

    def z_place(s):
        return (pz + s) % DEPTH

    def z_row(s):
        return team + z_place(s) * PLANE + place

    def send(k, src, dst, to_row, to_core):
        copy = pltpu.make_async_remote_copy(
            src_ref=src,
            dst_ref=dst,
            send_sem=ss.at[k],
            recv_sem=rs.at[k],
            device_id=(to_row, to_core),
            device_id_type=MESH,
        )
        copy.start()
        pending.append(copy)
        return copy

    def block(index, size):
        return pl.ds(pl.multiple_of(index * size, size), size)

    ids = iter(range(10_000))

    loads = [
        pltpu.make_async_copy(win.at[:, pl.ds(chan, w)], win_i, ls.at[0]),
        pltpu.make_async_copy(
            win.at[:, pl.ds(pl.multiple_of(2 * w + core * w, w), w)], win_g, ls.at[1]
        ),
        pltpu.make_async_copy(wout.at[pl.ds(chan, w), :], wo, ls.at[2]),
    ]
    for copy in loads:
        copy.start()

    for n, ref in enumerate((gain, cb, dtb, skip)):
        count = ref.shape[0]
        lines[n : n + 1, 0:count] = ref[...].reshape(1, count)
    gain_row = lines[0:1, 0:d]
    unit = 2 * STEP

    def norm_block(b, carry):
        at = pl.multiple_of(b * unit, unit)
        rows = tok[pl.ds(at, unit), :].astype(f32)
        scale = lax.rsqrt(jnp.mean(rows * rows, axis=-1, keepdims=True) + EPS)
        ng[0, pl.ds(mine + at, unit), :] = (rows * scale * gain_row).astype(bf16)
        ng[1, pl.ds(mine + at, unit), :] = cot[pl.ds(at, unit), :]
        return carry

    lax.fori_loop(0, tl // unit, norm_block, 0)
    mk[:, pl.ds(mine, tl)] = jnp.broadcast_to(marks[...].astype(f32), (8, tl))

    barrier = pltpu.get_barrier_semaphore()
    partners = [(row, other)]
    partners += [(plane_row(s), core) for s in range(1, PLANE)]
    partners += [(z_row(s), core) for s in range(1, DEPTH)]
    for partner in partners:
        pl.semaphore_signal(barrier, inc=1, device_id=partner, device_id_type=MESH)
    pl.semaphore_wait(barrier, len(partners))

    own_rows = ng.at[:, pl.ds(mine, tl), :]
    twin = [send(next(ids), own_rows, own_rows, row, other)]
    part = mk.at[:, pl.ds(mine, tl)]
    twin.append(send(next(ids), part, part, row, other))
    early = [
        send(next(ids), own_rows, ngh.at[s - 1, :, pl.ds(mine, tl), :], plane_row(s), core)
        for s in (1, 2)
    ]

    inner[0:8, :] = jnp.zeros((8, w), f32)
    dconv[t : t + 8, :] = jnp.zeros((8, w), f32)
    mcol[t : t + 8, :] = jnp.zeros((8, LANES), f32)
    odd[0:states, :] = jnp.zeros((states, w), bf16)
    tsc[...] = jnp.zeros(tsc.shape, f32)
    smb[...] = jnp.zeros(smb.shape, bf16)
    for ref in (ga, qa, ba, ca):
        ref[...] = jnp.zeros(ref.shape, bf16)
    sm[...] = jnp.zeros(sm.shape, f32)

    for copy in loads:
        copy.wait()
    for copy in twin:
        copy.wait_recv()

    for sl in lane_tiles(w, 2 * LANES):
        inner[8 : 8 + t, sl] = mm(ng[0], win_i[:, sl]).astype(bf16).astype(f32)

    lane = lax.broadcasted_iota(jnp.int32, (8, t), 1)
    mark = mk[...]
    keep = jnp.where(lane == 0, 0.0, 1.0 - mark)
    mask2 = keep * pltpu.roll(keep, 1, 1)
    mask3 = mask2 * pltpu.roll(keep, 2, 1)
    line = lax.broadcasted_iota(jnp.int32, (LANES, t), 0)

    def spread(v):
        return jnp.broadcast_to(v[0:1, :], (LANES, t))

    stacked = jnp.where(line == 0, spread(keep), 0.0)
    stacked = jnp.where(line == 1, spread(mask2), stacked)
    stacked = jnp.where(line == 2, spread(mask3), stacked)
    stacked = jnp.where(line == 3, spread(mark), stacked)
    mcol[0:t, :] = stacked.T

    cw_own = cw[:, pl.ds(chan, w)]
    cb_own = lines[1:2, pl.ds(chan, w)]
    taps = cw.shape[0]

    def conv_block(b, carry):
        at = pl.multiple_of(b * STEP, STEP)
        view = inner.at[pl.ds(at, STEP + 8)]
        masks = mcol[pl.ds(at, STEP), :]
        for sl in halves:
            total = cb_own[:, sl] + cw_own[taps - 1 : taps, sl] * view[8 : 8 + STEP, sl]
            for j in range(1, taps):
                tap = cw_own[taps - 1 - j : taps - j, sl]
                total = total + tap * view[8 - j : 8 - j + STEP, sl] * masks[:, j - 1 : j]
            sg = 1.0 / (1.0 + jnp.exp(-total))
            value = total * sg
            act[pl.ds(at, STEP), sl] = value
            actl[pl.ds(at, STEP), sl] = value.astype(bf16)
            dsilu[pl.ds(at, STEP), sl] = sg * (1.0 + total * (1.0 - sg))
        return carry

    lax.fori_loop(0, chunks, conv_block, 0)
    xw_own = xw[:, pl.ds(chan, w)]
    pp[:, 0:nproj] = mm(actl[...], xw_own, NT)
    proj_copy = send(next(ids), pp, pq, row, other)

    for sl in lane_tiles(w, 2 * LANES):
        gate[:, sl] = mm(ng[0], win_g[:, sl])
        dgated[:, sl] = mm(ng[1], wo[sl, :], NT)

    def dy_block(b, carry):
        at = pl.ds(pl.multiple_of(b * STEP, STEP), STEP)
        for sl in halves:
            g = gate[at, sl]
            low = (dgated[at, sl] * (g / (1.0 + jnp.exp(-g)))).astype(bf16)
            dyf[at, sl] = low.astype(f32)
        return carry

    lax.fori_loop(0, chunks, dy_block, 0)

    across, relays = [], []
    for s in (1, 2):
        early[s - 1].wait_recv()
        piece = pl.ds(pl.multiple_of(mine + (s - 1) * (tl // 2), tl // 2), tl // 2)
        across.append(
            send(next(ids), ngh.at[s - 1, :, piece, :], ngh.at[2, :, piece, :], plane_row(3 - s), core)
        )
        part = ngh.at[s - 1, :, pl.ds(mine, tl), :]
        relays.append(send(next(ids), part, part, row, other))

    proj_copy.wait_recv()
    proj = pp[...] + pq[...]
    turned = proj.T
    for k in range(chunks):
        cols = slice(k * STEP, (k + 1) * STEP)
        bt[k, :, 0:STEP] = turned[rank : rank + states, cols]
        ct[k, :, 0:STEP] = turned[rank + states : rank + 2 * states, cols]
    rank_low = proj[:, 0:rank].astype(bf16)
    rank_turned = turned[0:rank, :].astype(bf16)
    dtw_own = dtw[:, pl.ds(chan, w)]
    dtb_own = lines[2:3, pl.ds(chan, w)]
    for sl in lane_tiles(w, 2 * LANES):
        sig[:, sl] = mm(rank_low, dtw_own[:, sl]) + dtb_own[:, sl]

    def delta_block(b, carry):
        at = pl.ds(pl.multiple_of(b * STEP, STEP), STEP)
        marked = mcol[at, :][:, 3:4] > 0.5
        for sl in halves:
            pre = sig[at, sl]
            e = jnp.exp(-jnp.abs(pre))
            one = 1.0 + e
            log1p = jnp.where(one == 1.0, e, jnp.log(one) * (e / (one - 1.0)))
            delta = jnp.maximum(pre, 0.0) + log1p
            sig[at, sl] = jnp.where(pre >= 0.0, 1.0, e) / one
            inflow = delta * act[at, sl]
            u[at, sl] = inflow
            s1[at, sl] = delta
            ddec[at, sl] = jnp.where(marked, 1e30, delta)
        return carry

    lax.fori_loop(0, chunks, delta_block, 0)

    span = STEP * states
    pick = (
        lax.broadcasted_iota(jnp.int32, (states, span), 0)
        == lax.broadcasted_iota(jnp.int32, (states, span), 1) % states
    ).astype(bf16)
    diag = (
        lax.broadcasted_iota(jnp.int32, (t, span), 0) % STEP
        == lax.broadcasted_iota(jnp.int32, (t, span), 1) // states
    )
    ones_diag = diag[0:STEP].astype(bf16)
    b_low = proj[:, rank : rank + states].astype(bf16)
    c_low = proj[:, rank + states : rank + 2 * states].astype(bf16)
    bbd[...] = jnp.where(diag, mm(b_low, pick), 0.0).astype(bf16)
    cbd[...] = jnp.where(diag, mm(c_low, pick), 0.0).astype(bf16)

    rates = [-jnp.exp(alog[:, pl.ds(chan + j * LANES, LANES)]) for j in range(tiles)]
    zeros = tuple(jnp.zeros((states, LANES), f32) for _ in range(tiles))
    tile = [slice(j * LANES, (j + 1) * LANES) for j in range(tiles)]

    def even_at(m):
        return pl.multiple_of(m * span, span)

    def odd_at(m):
        return pl.multiple_of(states + m * span, states)

    def state_block(ref, first, i):
        return ref.at[pl.ds(pl.multiple_of(first + i * states, states), states)]

    def scan_chunk(k, state, kept, first):
        rows = pl.ds(pl.multiple_of(k * STEP, STEP), STEP)
        b_here, dec, flow = bt[k], ddec.at[rows], u.at[rows]
        state = list(state)
        for i in range(STEP):
            b_wide = jnp.broadcast_to(b_here[:, i : i + 1], (states, LANES))
            dest = state_block(kept, first, i)
            for j, sl in enumerate(tile):
                decay = jnp.exp(dec[i : i + 1, sl] * rates[j])
                state[j] = decay * state[j] + flow[i : i + 1, sl] * b_wide
                dest[:, sl] = state[j].astype(bf16)
        return state

    def read_chunk(k, kept, first):
        rows = pl.ds(pl.multiple_of(k * STEP, STEP), STEP)
        du[rows, :] = mm(cbd[rows, :], kept[pl.ds(pl.multiple_of(first, states), span), :])

    def scan_pair(m, state):
        read_chunk(jnp.maximum(2 * m - 1, 0), odd, odd_at(jnp.maximum(m - 1, 0)))
        state = scan_chunk(2 * m, state, even, even_at(m))
        read_chunk(2 * m, even, even_at(m))
        return tuple(scan_chunk(2 * m + 1, state, odd, odd_at(m)))

    pairs = chunks // 2
    odd[pl.ds(states, span), :] = jnp.zeros((span, w), bf16)
    final = lax.fori_loop(0, pairs, scan_pair, zeros)
    read_chunk(chunks - 1, odd, odd_at(pairs - 1))

    skip_own = lines[3:4, pl.ds(chan, w)]

    def gated_block(b, carry):
        at = pl.ds(pl.multiple_of(b * STEP, STEP), STEP)
        for sl in halves:
            y = (du[at, sl] + skip_own[:, sl] * act[at, sl]).astype(bf16).astype(f32)
            g = gate[at, sl]
            sg = 1.0 / (1.0 + jnp.exp(-g))
            gt[at, sl] = (y * (g * sg)).astype(bf16)
            dgl[at, sl] = (dgated[at, sl] * y * (sg * (1.0 + g * (1.0 - sg)))).astype(bf16)
        return carry

    lax.fori_loop(0, chunks, gated_block, 0)

    def send_factors(n, source):
        for sl in tile:
            turn[n, sl, :] = source[:, sl].T
        return [
            send(
                next(ids),
                turn.at[n, block(plane_place(s), quarter), :],
                fac.at[n, s - 1],
                plane_row(s),
                core,
            )
            for s in range(1, PLANE)
        ]

    def partial_sum(n, copies):
        for copy in copies:
            copy.wait_recv()
        kind = 1 if n == 0 else 0
        lefts = [turn[n, block(place, quarter), :]] + [fac[n, s] for s in range(PLANE - 1)]
        for sl in lane_tiles(d, 2 * LANES):
            total = mm(lefts[0], ng[kind, :, sl])
            for s in range(PLANE - 1):
                total = total + mm(lefts[s + 1], ngh[s, kind, :, sl])
            pw[:, sl] = total
            pb[n, :, sl] = total.astype(bf16)
        pown[n] = pw[block(pz, zrows), :]
        return [
            send(next(ids), pb.at[n, block(z_place(s), zrows), :], zr.at[n, s - 1], z_row(s), core)
            for s in range(1, DEPTH)
        ]

    def shard(n, where, z):
        return res.at[n, pl.ds(pl.multiple_of(where * quarter + z * zrows, zrows), zrows), :]

    def to_neighbours(part):
        return [send(next(ids), part, part, plane_row(s), core) for s in (1, 2)]

    def total_sum(n, copies):
        for copy in copies:
            copy.wait_recv()
        total = pown[n]
        for s in range(DEPTH - 1):
            total = total + zr[n, s].astype(f32)
        part = shard(n, place, pz)
        part[...] = total.astype(bf16)
        along = [send(next(ids), part, part, z_row(s), core) for s in range(1, DEPTH)]
        return {"n": n, "along": along, "near": [to_neighbours(part)], "far": []}

    def pass_on(state, s):
        state["along"][s - 1].wait_recv()
        part = shard(state["n"], place, (pz + DEPTH - s) % DEPTH)
        state["near"].append(to_neighbours(part))

    def pass_across(state, s):
        for q in (1, 2):
            state["near"][s][q - 1].wait_recv()
        q = 1 + s % 2
        part = shard(state["n"], plane_place(q), (pz + DEPTH - s) % DEPTH)
        state["far"].append(send(next(ids), part, part, plane_row(3 - q), core))

    def place_of(n):
        if n == 0:
            return gout.at[pl.ds(chan, w), :]
        return gin.at[pl.ds(pl.multiple_of((2 - n) * 2 * w + core * w, w), w), :]

    locals_ = []

    def finish(state):
        n = state["n"]
        for copy in state["far"]:
            copy.wait_recv()
        copy = pltpu.make_async_copy(res.at[n], place_of(n), ls.at[3 + n])
        copy.start()
        locals_.append(copy)
        return send(next(ids), res.at[n], place_of(n), row, other)

    fac_out = send_factors(0, gt)
    fac_gate = send_factors(1, dgl)
    for s in (1, 2):
        across[s - 1].wait_recv()
        piece = pl.ds(pl.multiple_of(mine + (s - 1) * (tl // 2), tl // 2), tl // 2)
        part = ngh.at[2, :, piece, :]
        relays.append(send(next(ids), part, part, row, other))

    for sl in lane_tiles(d, 2 * LANES):
        outp[:, sl] = mm(gt[...], wo[:, sl])
    out_copy = send(next(ids), outp.at[pl.ds(theirs, tl), :], outr, row, other)
    for sl in lane_tiles(d, 2 * LANES):
        dn[:, sl] = mm(dgl[...], win_g[sl, :], NT)

    def back_chunk(k, carry, kept, first, before, last, gbuf, qbuf, bbuf, cbuf):
        base = pl.multiple_of(k * STEP, STEP)
        rows = pl.ds(base, STEP)
        c_here, dec, dys, inflow = ct[k], ddec.at[rows], dyf.at[rows], u.at[rows]
        dys_before = dyf.at[pl.ds(pl.multiple_of(jnp.maximum(base - STEP, 0), STEP), STEP)]
        flow, acc = list(carry[0]), list(carry[1])
        for i in reversed(range(STEP)):
            c_wide = jnp.broadcast_to(c_here[:, i : i + 1], (states, LANES))
            at = slice(i * states, (i + 1) * states)
            old = state_block(kept, first, i - 1) if i else state_block(before, last, 0)
            dy_old = dys_before[STEP - 1 : STEP, :] if i == 0 else dys[i - 1 : i, :]
            for_b = for_c = None
            for j, sl in enumerate(tile):
                rate = dec[i : i + 1, sl]
                g = c_wide * dys[i : i + 1, sl] + flow[j]
                gbuf[at, sl] = g.astype(bf16)
                flow[j] = g * jnp.exp(rate * rates[j])
                h_old = old[:, sl].astype(f32)
                q = flow[j] * h_old
                acc[j] = acc[j] + q * rate
                qbuf[at, sl] = (q * rates[j]).astype(bf16)
                term_b, term_c = g * inflow[i : i + 1, sl], h_old * dy_old[:, sl]
                for_b = term_b if for_b is None else for_b + term_b
                for_c = term_c if for_c is None else for_c + term_c
            bbuf[at, :] = for_b.astype(bf16)
            cbuf[at, :] = for_c.astype(bf16)
        return flow, acc

    lane_of = lax.broadcasted_iota(jnp.int32, (states, LANES), 1)
    ones = jnp.ones((LANES, LANES), bf16)

    def back_sums(k, gbuf, qbuf, bbuf, cbuf):
        rows = pl.ds(pl.multiple_of(k * STEP, STEP), STEP)
        for parts, dest in ((bbuf, dbt), (cbuf, dct)):
            summed = mm(parts[...], ones)
            value = jnp.zeros((states, LANES), f32)
            for i in range(STEP):
                value = jnp.where(lane_of == i, summed[i * states : (i + 1) * states, :], value)
            dest[k] = value
        du[rows, :] = mm(bbd[rows, :], gbuf[...])
        sq[rows, :] = mm(ones_diag, qbuf[...])

    even_bufs, odd_bufs = (ga, qa, ba, ca), (gb, qb, bb, cc)

    def back_pair(mm_, carry):
        m = pairs - 1 - mm_
        back_sums(jnp.minimum(2 * m + 2, chunks - 1), *even_bufs)
        carry = back_chunk(2 * m + 1, carry, odd, odd_at(m), even, even_at(m) + span - states, *odd_bufs)
        back_sums(2 * m + 1, *odd_bufs)
        flow, acc = back_chunk(2 * m, carry, even, even_at(m), odd, even_at(m), *even_bufs)
        return tuple(flow), tuple(acc)

    def out_block(b, carry):
        at = pl.multiple_of(b * STEP, STEP)
        rows = pl.ds(at, STEP)
        total = outp[pl.ds(mine + at, STEP), :] + outr[rows, :]
        out[rows, :] = (tok[rows, :].astype(f32) + total).astype(bf16)
        return carry

    stops = [pairs * p // 8 for p in (0, 2, 4, 6, 8)]
    carry = (zeros, zeros)
    carry = lax.fori_loop(stops[0], stops[1], back_pair, carry)
    out_copy.wait_recv()
    lax.fori_loop(0, tl // STEP, out_block, 0)
    carry = lax.fori_loop(stops[1], stops[2], back_pair, carry)
    for copy in relays:
        copy.wait_recv()
    z_out = partial_sum(0, fac_out)
    carry = lax.fori_loop(stops[2], stops[3], back_pair, carry)
    z_gate = partial_sum(1, fac_gate)
    carry = lax.fori_loop(stops[3], stops[4], back_pair, carry)
    back_sums(0, *even_bufs)
    acc = carry[1]
    g_out = total_sum(0, z_out)

    def dpre_block(b, carry):
        at = pl.ds(pl.multiple_of(b * STEP, STEP), STEP)
        sums, gains = [], []
        for n, sl in enumerate(halves):
            flow, value, dy = du[at, sl], act[at, sl], dyf[at, sl]
            dpre = (sq[at, sl] + flow * value) * sig[at, sl]
            dpl[at, sl] = dpre.astype(bf16)
            du[at, sl] = flow * s1[at, sl] + skip_own[:, sl] * dy
            both = dy * value
            sums.append(carry[0][n] + dpre[0:8] + dpre[8:16])
            gains.append(carry[1][n] + both[0:8] + both[8:16])
        return tuple(sums), tuple(gains)

    none = tuple(jnp.zeros((8, half), f32) for _ in halves)
    sums, gains = lax.fori_loop(0, chunks, dpre_block, (none, none))
    first = nproj + rank + states
    line_conv, line_cb, line_dtb, line_skip, line_gain = (
        first,
        first + taps,
        first + taps + 1,
        first + taps + 2,
        first + taps + 3,
    )
    for n, sl in enumerate(halves):
        sm[line_dtb : line_dtb + 1, sl] = jnp.sum(sums[n], axis=0, keepdims=True)
        sm[line_skip : line_skip + 1, sl] = jnp.sum(gains[n], axis=0, keepdims=True)
    for j in range(tiles):
        sl = slice(j * LANES, (j + 1) * LANES)
        sm[nproj + rank : first, sl] = acc[j] * rates[j]

    late = sum(dyf[t - 1 : t, sl] * final[j] for j, sl in enumerate(tile))
    for k in range(chunks):
        cols = slice(k * STEP, (k + 1) * STEP)
        tsc[rank : rank + states, cols] = dbt[k][:, 0:STEP]
        tsc[rank + states : nproj, cols] = dct[k][:, 0:STEP]
    shifted = pltpu.roll(tsc[rank + states : nproj, :], t - 1, 1)
    at_end = lax.broadcasted_iota(jnp.int32, (states, t), 1) == t - 1
    tsc[rank + states : nproj, :] = jnp.where(
        at_end, jnp.sum(late, axis=1, keepdims=True), shifted
    )
    pp2[...] = tsc[...].T
    pp2[:, 0:rank] = mm(dpl[...], dtw_own, NT)
    dproj_copy = send(next(ids), pp2, pq2, row, other)
    for sl in lane_tiles(w, 2 * LANES):
        sm[nproj : nproj + rank, sl] = mm(rank_turned, dpl[:, sl])
    g_gate = total_sum(1, z_gate)
    pass_on(g_out, 1)
    dproj_copy.wait_recv()
    dproj = pp2[...] + pq2[...]
    dproj_low = dproj[:, 0:nproj].astype(bf16)
    dproj_turned = dproj.T[0:nproj, :].astype(bf16)
    for sl in lane_tiles(w, 2 * LANES):
        sq[:, sl] = mm(dproj_low, xw_own[:, sl])

    def dconv_block(b, carry):
        at = pl.multiple_of(b * STEP, STEP)
        view = inner.at[pl.ds(at, STEP + 8)]
        rows = pl.ds(at, STEP)
        masks = mcol[rows, :]
        sums = [list(v) for v in carry]
        for n, sl in enumerate(halves):
            grad = (du[rows, sl] + sq[rows, sl]) * dsilu[rows, sl]
            dconv[rows, sl] = grad
            terms = [grad, grad * view[8 : 8 + STEP, sl]]
            for j in range(1, taps):
                terms.append(grad * masks[:, j - 1 : j] * view[8 - j : 8 - j + STEP, sl])
            for m, term in enumerate(terms):
                sums[m][n] = sums[m][n] + term[0:8] + term[8:16]
        return tuple(tuple(v) for v in sums)

    sums = lax.fori_loop(0, chunks, dconv_block, (none,) * (taps + 1))
    for n, sl in enumerate(halves):
        sm[line_cb : line_cb + 1, sl] = jnp.sum(sums[0][n], axis=0, keepdims=True)
        for j in range(taps):
            at = line_conv + taps - 1 - j
            sm[at : at + 1, sl] = jnp.sum(sums[1 + j][n], axis=0, keepdims=True)

    def dinner_block(b, carry):
        at = pl.multiple_of(b * STEP, STEP)
        view = dconv.at[pl.ds(at, STEP + 8)]
        masks = mcol.at[pl.ds(at, STEP + 8)]
        for sl in halves:
            total = cw_own[taps - 1 : taps, sl] * view[0:STEP, sl]
            for j in range(1, taps):
                tap = cw_own[taps - 1 - j : taps - j, sl]
                total = total + tap * view[j : j + STEP, sl] * masks[j : j + STEP, j - 1 : j]
            dil[pl.ds(at, STEP), sl] = total.astype(bf16)
        return carry

    lax.fori_loop(0, chunks, dinner_block, 0)
    fac_in = send_factors(2, dil)
    for sl in lane_tiles(d, 2 * LANES):
        dn[:, sl] = dn[:, sl] + mm(dil[...], win_i[sl, :], NT)
    dn_copy = send(next(ids), dn.at[pl.ds(theirs, tl), :], dnr, row, other)
    for sl in lane_tiles(w, 2 * LANES):
        sm[0:nproj, sl] = mm(dproj_turned, actl[:, sl])
    pass_on(g_out, 2)
    pass_on(g_out, 3)
    for s in (0, 1):
        pass_across(g_out, s)
    dn_copy.wait_recv()

    def norm_back(b, carry):
        at = pl.multiple_of(b * STEP, STEP)
        rows = pl.ds(at, STEP)
        values = tok[rows, :].astype(f32)
        scale = lax.rsqrt(jnp.mean(values * values, axis=-1, keepdims=True) + EPS)
        unit_rows = values * scale
        grad = dn[pl.ds(mine + at, STEP), :] + dnr[rows, :]
        inside = grad * gain_row
        mean = jnp.mean(inside * unit_rows, axis=-1, keepdims=True)
        both = grad * unit_rows
        gtok[rows, :] = (cot[rows, :].astype(f32) + scale * (inside - unit_rows * mean)).astype(bf16)
        return carry + both[0:8] + both[8:16]

    total = lax.fori_loop(0, tl // STEP, norm_back, jnp.zeros((8, d), f32))
    sm[line_gain : line_gain + 1, :] = jnp.sum(total, axis=0, keepdims=True)
    count = sm.shape[0]
    for j, sl in enumerate(tile):
        smb[j * count : (j + 1) * count, :] = sm[:, sl].astype(bf16)
        smf[j * count : (j + 1) * count, :] = sm[:, sl]
    smf[tiles * count :, :] = jnp.zeros((smf.shape[0] - tiles * count, LANES), f32)

    squarter = smb.shape[0] // PLANE
    szrows = squarter // DEPTH
    over_plane = [
        send(
            next(ids), smb.at[block(plane_place(s), squarter), :], sfac.at[s - 1], plane_row(s), core
        )
        for s in range(1, PLANE)
    ]
    for s in (1, 2, 3):
        pass_on(g_gate, s)
    z_in = partial_sum(2, fac_in)
    for s in (2, 3):
        pass_across(g_out, s)
    for copy in over_plane:
        copy.wait_recv()
    total = smf[block(place, squarter), :]
    for s in range(PLANE - 1):
        total = total + sfac[s].astype(f32)
    smf[block(place, squarter), :] = total
    smb_sum = sres.at[block(place, squarter), :]
    smb_sum[...] = total.astype(bf16)
    over_z = [
        send(
            next(ids),
            sres.at[pl.ds(pl.multiple_of(place * squarter + z_place(s) * szrows, szrows), szrows), :],
            szr.at[s - 1],
            z_row(s),
            core,
        )
        for s in range(1, DEPTH)
    ]
    for s in (0, 1, 2, 3):
        pass_across(g_gate, s)
    twin_out = finish(g_out)
    g_in = total_sum(2, z_in)
    for copy in over_z:
        copy.wait_recv()
    own_small = pl.ds(pl.multiple_of(place * squarter + pz * szrows, szrows), szrows)
    total = smf[own_small, :]
    for s in range(DEPTH - 1):
        total = total + szr[s].astype(f32)
    sown[...] = total.astype(bf16)
    small_along = [
        send(next(ids), sown, sfin.at[own_small, :], z_row(s), core) for s in range(1, DEPTH)
    ]
    sfin[own_small, :] = sown[...]
    twin_gate = finish(g_gate)
    for s in (1, 2, 3):
        pass_on(g_in, s)
    for copy in small_along:
        copy.wait_recv()
    part = sfin.at[block(place, squarter), :]
    small_near = [send(next(ids), part, part, plane_row(s), core) for s in range(1, PLANE)]
    for s in (0, 1, 2, 3):
        pass_across(g_in, s)
    for copy in small_near:
        copy.wait_recv()
    small_place = small.at[block(core, smb.shape[0]), :]
    small_copy = pltpu.make_async_copy(sfin, small_place, ls.at[6])
    small_copy.start()
    locals_.append(small_copy)
    twin_small = send(next(ids), sfin, small_place, row, other)
    twin_in = finish(g_in)
    for copy in (twin_out, twin_gate, twin_small, twin_in):
        copy.wait_recv()
    for copy in locals_:
        copy.wait()
    for copy in pending:
        copy.wait_send()


def wide_kernel(tiles, gin, gout, small, gin_f, gout_f, *rows):
    gin_f[...] = gin[...].T.astype(f32)
    gout_f[...] = gout[...].astype(f32)

    @pl.when(pl.program_id(0) == 0)
    def _():
        cores = rows[0].shape[1] // (tiles * LANES)
        stride = small.shape[0] // cores
        matrices = [ref for ref in rows if len(ref.shape) == 2]
        vectors = [ref for ref in rows if len(ref.shape) == 1]
        count = sum(ref.shape[0] for ref in matrices) + len(vectors)
        pad = -(-count // 32) * 32
        last = [None] * tiles
        for n in range(cores * tiles):
            first = (n // tiles) * stride + (n % tiles) * pad
            value = small[first : first + pad, :].astype(f32)
            cols = slice(n * LANES, (n + 1) * LANES)
            at = 0
            for ref in matrices:
                ref[:, cols] = value[at : at + ref.shape[0], :]
                at += ref.shape[0]
            for ref in vectors[:-1]:
                ref[cols] = value[at : at + 1, :].reshape(LANES)
                at += 1
            piece = value[at : at + 1, :]
            j = n % tiles
            last[j] = piece if last[j] is None else last[j] + piece
        for j in range(tiles):
            vectors[-1][j * LANES : (j + 1) * LANES] = last[j].reshape(LANES)


def local(
    tokens, marks, norm_gain, in_weight, conv_weight, conv_bias, x_weight, dt_weight,
    dt_bias, a_log, skip, out_weight, cotangent,
):
    tl, d = tokens.shape[1:]
    e = out_weight.shape[0]
    w = e // lax.axis_size("seq")
    t = tl * lax.axis_size("seq")
    states, rank, nproj, taps = a_log.shape[0], dt_weight.shape[0], x_weight.shape[0], conv_weight.shape[0]
    chunks, span, tiles = t // STEP, STEP * states, w // LANES
    quarter = w // PLANE
    zrows = quarter // DEPTH
    lines = -(-(nproj + rank + states + taps + 4) // 32) * 32
    slines = -(-lines * tiles // (16 * TEAM)) * 16 * TEAM
    vmem = pl.BlockSpec(memory_space=pltpu.VMEM)
    anywhere = pl.BlockSpec(memory_space=pl.ANY)
    wide = pltpu.VMEM((t, w), f32)
    low = pltpu.VMEM((t, w), bf16)
    one = pltpu.VMEM((t, LANES), f32)
    scratch = [
        pltpu.VMEM((d, w), bf16), pltpu.VMEM((d, w), bf16), pltpu.VMEM((w, d), bf16),
        pltpu.VMEM((2, t, d), bf16), pltpu.VMEM((PLANE - 1, 2, t, d), bf16),
        pltpu.VMEM((8, t), f32), pltpu.VMEM((t + 8, LANES), f32), pltpu.VMEM((8, e), f32),
        pltpu.VMEM((t + 8, w), f32), wide, wide, wide, wide, low, wide, wide, wide, wide, wide, wide, wide,
        one, one, one, one, pltpu.VMEM((LANES, t), f32),
        pltpu.VMEM((t * states // 2, w), bf16), pltpu.VMEM((t * states // 2 + states, w), bf16),
        pltpu.VMEM((chunks, states, LANES), f32), pltpu.VMEM((chunks, states, LANES), f32),
        pltpu.VMEM((t, span), bf16), pltpu.VMEM((t, span), bf16),
        *[pltpu.VMEM((span, w), bf16)] * 4, *[pltpu.VMEM((span, LANES), bf16)] * 4,
        *[pltpu.VMEM((chunks, states, LANES), f32)] * 2,
        low, low, low, low, pltpu.VMEM((3, w, t), bf16), pltpu.VMEM((t + 8, w), f32),
        pltpu.VMEM((t, d), f32), pltpu.VMEM((tl, d), f32),
        pltpu.VMEM((t, d), f32), pltpu.VMEM((tl, d), f32),
        pltpu.VMEM((3, PLANE - 1, quarter, t), bf16), pltpu.VMEM((quarter, d), f32),
        pltpu.VMEM((3, zrows, d), f32), pltpu.VMEM((3, quarter, d), bf16),
        pltpu.VMEM((3, DEPTH - 1, zrows, d), bf16), pltpu.VMEM((3, w, d), bf16),
        pltpu.VMEM((lines, w), f32), pltpu.VMEM((slines, LANES), bf16), pltpu.VMEM((slines, LANES), f32),
        pltpu.VMEM((PLANE - 1, slines // PLANE, LANES), bf16),
        pltpu.VMEM((DEPTH - 1, slines // TEAM, LANES), bf16),
        pltpu.VMEM((slines, LANES), bf16), pltpu.VMEM((slines // TEAM, LANES), bf16),
        pltpu.VMEM((slines, LANES), bf16),
        pltpu.SemaphoreType.DMA((8,)),
        pltpu.SemaphoreType.DMA((112,)), pltpu.SemaphoreType.DMA((112,)),
    ]
    cores = e // w
    output, grad_tokens, gin, gout, small = pl.pallas_call(
        body_kernel,
        out_shape=[
            jax.ShapeDtypeStruct((tl, d), bf16),
            jax.ShapeDtypeStruct((tl, d), bf16),
            jax.ShapeDtypeStruct((2 * e, d), bf16),
            jax.ShapeDtypeStruct((e, d), bf16),
            jax.ShapeDtypeStruct((cores * slines, LANES), bf16),
        ],
        in_specs=[vmem, vmem, vmem, anywhere] + [vmem] * 7 + [anywhere, vmem],
        out_specs=[vmem, vmem, anywhere, anywhere, anywhere],
        scratch_shapes=scratch,
        compiler_params=pltpu.CompilerParams(
            collective_id=0, has_side_effects=True, vmem_limit_bytes=60 * 2**20
        ),
        name="block",
    )(
        tokens.reshape(tl, d), marks.reshape(1, tl), norm_gain, in_weight, conv_weight,
        conv_bias, x_weight, dt_weight, dt_bias, a_log, skip, out_weight, cotangent.reshape(tl, d),
    )

    steps = 8
    shapes = [(nproj, e), (rank, e), (states, e), (taps, e), (e,), (e,), (e,), (d,)]
    once = [pl.BlockSpec(s, functools.partial(lambda k, i: (0,) * k, len(s))) for s in shapes]
    gout_spec = pl.BlockSpec((e // steps, d), lambda i: (i, 0))
    grads = pl.pallas_call(
        functools.partial(wide_kernel, tiles),
        grid=(steps,),
        out_shape=[jax.ShapeDtypeStruct(s, f32) for s in [(d, 2 * e), (e, d)] + shapes],
        in_specs=[
            pl.BlockSpec((2 * e // steps, d), lambda i: (i, 0)),
            gout_spec,
            pl.BlockSpec((cores * slines, LANES), lambda i: (0, 0)),
        ],
        out_specs=[pl.BlockSpec((d, 2 * e // steps), lambda i: (0, i)), gout_spec] + once,
        compiler_params=pltpu.CompilerParams(vmem_limit_bytes=60 * 2**20),
        name="widen",
    )(gin, gout, small)
    rows = lax.axis_size("rows")
    if rows > TEAM:
        grads = [v * (1.0 / TEAM) for v in lax.psum(grads, "rows")]
    grad_in, grad_out, grad_x, grad_dt, grad_log, grad_conv, g_cb, g_dtb, g_skip, g_gain = grads
    return (
        output[None], grad_tokens[None], g_gain, grad_in, grad_conv, g_cb, grad_x, grad_dt, g_dtb, grad_log,
        g_skip, grad_out,
    )


def solution(mesh):
    split = P("rows", "seq", None)
    whole = P()
    in_specs = (split, P("rows", "seq")) + (whole,) * 10 + (split,)
    out_specs = (split, split) + (whole,) * 10
    return jax.shard_map(local, mesh=mesh, in_specs=in_specs, out_specs=out_specs, check_vma=False)
```

```python
import functools

import jax
import jax.numpy as jnp
from jax import lax
from jax.experimental import pallas as pl
from jax.experimental.pallas import tpu as pltpu
from jax.sharding import PartitionSpec as P

f32 = jnp.float32
bf16 = jnp.bfloat16
EPS = 1e-05
LANES = 128
STEP = 16
PLANE = 4
DEPTH = 4
TEAM = PLANE * DEPTH
MESH = pl.DeviceIdType.MESH
NN = (((1,), (0,)), ((), ()))
NT = (((1,), (1,)), ((), ()))


def mm(a, b, dims=NN):
    return lax.dot_general(a, b, dims, preferred_element_type=f32)


def lane_tiles(width, size):
    return [slice(j, j + size) for j in range(0, width, size)]


def body_kernel(
    tok, marks, gain_in, win, cw_in, cb_in, xw_in, dtw_in, dtb_in, alog_in, skip_in, wout, cot,
    out, gtok, gout, ggate, gmix,
    win_i, win_g, wo, gain, cw, cb, xw, dtw, dtb, alog, skip, mkraw, ng, ngh, mk, mcol, lines,
    inner, gate, dgated, act, dsilu, actl, ddec, u, sig, dyf, du, s1, sq,
    pp, pq, pp2, pq2, tsc, even, odd, bt, ct, cbd, bbd, ga, gb, qa, qb, ba, bb, ca, cc, dbt, dct, lastc, tot,
    gt, dgl, dpl, dil, turn, dconv, dn, dnr, outp, outr,
    fac, pw, pown, pb, zr, sm, smb, sms, sfac, spb, szr,
    ls, ss, rs,
):
    row, core = lax.axis_index("rows"), lax.axis_index("seq")
    other = 1 - core
    team = row - row % TEAM
    px, py, pz = row % 2, (row // 2) % 2, (row // PLANE) % DEPTH
    tl, d = out.shape
    t = 2 * tl
    w = wo.shape[0]
    states = alog.shape[0]
    rank = dtw.shape[0]
    nproj = xw.shape[0]
    half = w // 2
    quarter = w // PLANE
    zrows = quarter // DEPTH
    extra, packed = smb.shape[0] // TEAM, smb.shape[1]
    place = row % PLANE
    chunks = t // STEP
    tiles = w // LANES
    mine = pl.multiple_of(core * tl, tl)
    theirs = pl.multiple_of(other * tl, tl)
    chan = pl.multiple_of(core * w, w)
    halves = lane_tiles(w, half)
    pending = []

    def flip(low, high, s):
        a, b = s % 2, s // 2
        return (high + b - 2 * b * high) * 2 + low + a - 2 * a * low

    plane_place = [flip(px, py, s) for s in range(PLANE)]
    plane_row = [team + pz * PLANE + plane_place[s] for s in range(PLANE)]
    z_place = [flip(pz % 2, pz // 2, s) for s in range(DEPTH)]
    z_row = [team + z_place[s] * PLANE + place for s in range(DEPTH)]
    ids = iter(range(10_000))

    class Send:
        def __init__(self, refs, to_row, to_core):
            self.refs, self.to, self.k = refs, (to_row, to_core), next(ids)
            self.copy().start()
            pending.append(self)

        def copy(self):
            src, dst = self.refs()
            return pltpu.make_async_remote_copy(
                src_ref=src,
                dst_ref=dst,
                send_sem=ss.at[self.k],
                recv_sem=rs.at[self.k],
                device_id=self.to,
                device_id_type=MESH,
            )

        def wait_recv(self):
            self.copy().wait_recv()

        def wait_send(self):
            self.copy().wait_send()

    def block(index, size):
        return pl.ds(pl.multiple_of(index * size, size), size)

    own = pl.ds(chan, w)
    sources = [
        (tok, ng.at[2, pl.ds(mine, tl), :]),
        (marks, mkraw.at[0:1]),
        (gain_in, gain),
        (win.at[:, own], win_i),
        (cw_in.at[:, own], cw),
        (cb_in, cb),
        (cot, ng.at[1, pl.ds(mine, tl), :]),
        (xw_in.at[:, own], xw),
        (win.at[:, pl.ds(pl.multiple_of(2 * w + core * w, w), w)], win_g),
        (wout.at[own, :], wo),
        (dtw_in.at[:, own], dtw),
        (dtb_in, dtb),
        (skip_in, skip),
        (alog_in.at[:, own], alog),
    ]
    loads = [pltpu.make_async_copy(src, dst, ls.at[n]) for n, (src, dst) in enumerate(sources)]
    for copy in loads:
        copy.start()

    barrier = pltpu.get_barrier_semaphore()
    partners = [(row, other)]
    partners += [(plane_row[s], core) for s in range(1, PLANE)]
    partners += [(z_row[s], core) for s in range(1, DEPTH)]
    for partner in partners:
        pl.semaphore_signal(barrier, inc=1, device_id=partner, device_id_type=MESH)
    pl.semaphore_wait(barrier, len(partners))

    def pair_to(ref):
        return lambda: (ref(), ref())

    def own_rows(kind):
        return ng.at[kind, pl.ds(mine, tl), :]

    def slot(s, kind, first=0, count=tl):
        return ngh.at[s - 1, kind, pl.ds(pl.multiple_of(mine + first, count), count), :]

    twin = [
        Send(lambda n=n, ref=ref: (ref, ng.at[n, pl.ds(mine, tl), :]), row, other)
        for n, ref in ((2, tok), (1, cot))
    ]
    twin.append(Send(lambda: (marks, mkraw.at[1:2]), row, other))
    early, across, relays = {}, {}, {0: [], 1: []}
    piece = tl // 2

    def share(kind):
        early[kind] = [
            Send(lambda s=s: (cot if kind else own_rows(kind), slot(s, kind)), plane_row[s], core)
            for s in (1, 2)
        ]

    def share_on(kind):
        across[kind] = []
        for s in (1, 2):
            early[kind][s - 1].wait_recv()
            first = (s - 1) * piece
            refs = lambda s=s, first=first: (slot(s, kind, first, piece), slot(3, kind, first, piece))
            across[kind].append(Send(refs, plane_row[3 - s], core))
            relays[kind].append(Send(pair_to(lambda s=s: slot(s, kind)), row, other))

    def share_end(kind):
        for s in (1, 2):
            across[kind][s - 1].wait_recv()
            refs = pair_to(lambda first=(s - 1) * piece: slot(3, kind, first, piece))
            relays[kind].append(Send(refs, row, other))

    share(1)

    for copy in loads[:3]:
        copy.wait()
    count = gain.shape[0]
    lines[0:1, 0:count] = gain[...].reshape(1, count)
    unit = 2 * STEP

    def norm_rows(first):
        gain_row = lines[0:1, 0:d]

        def norm_block(b, carry):
            at = pl.ds(pl.multiple_of(first + b * unit, unit), unit)
            rows = ng[2, at, :].astype(f32)
            scale = lax.rsqrt(jnp.mean(rows * rows, axis=-1, keepdims=True) + EPS)
            ng[0, at, :] = (rows * scale * gain_row).astype(bf16)
            return carry

        lax.fori_loop(0, tl // unit, norm_block, 0)

    norm_rows(mine)
    share(0)

    inner[0:8, :] = jnp.zeros((8, w), f32)
    dconv[t : t + 8, :] = jnp.zeros((8, w), f32)
    mcol[t : t + 8, :] = jnp.zeros((8, LANES), f32)
    odd[0:states, :] = jnp.zeros((states, w), bf16)
    tsc[...] = jnp.zeros(tsc.shape, f32)
    tot[...] = jnp.zeros(tot.shape, f32)
    smb[...] = jnp.zeros(smb.shape, bf16)
    sms[...] = jnp.zeros(sms.shape, f32)
    for ref in (ga, qa, ba, ca):
        ref[...] = jnp.zeros(ref.shape, bf16)
    sm[...] = jnp.zeros(sm.shape, f32)

    for copy in twin:
        copy.wait_recv()
    norm_rows(theirs)
    own_marks, twin_marks = mkraw[0:1, :].astype(f32), mkraw[1:2, :].astype(f32)
    mk[:, pl.ds(mine, tl)] = jnp.broadcast_to(own_marks, (8, tl))
    mk[:, pl.ds(theirs, tl)] = jnp.broadcast_to(twin_marks, (8, tl))
    for copy in loads[3:7]:
        copy.wait()

    for sl in lane_tiles(w, 2 * LANES):
        inner[8 : 8 + t, sl] = mm(ng[0], win_i[:, sl]).astype(bf16).astype(f32)

    lane = lax.broadcasted_iota(jnp.int32, (8, t), 1)
    mark = mk[...]
    keep = jnp.where(lane == 0, 0.0, 1.0 - mark)
    mask2 = keep * pltpu.roll(keep, 1, 1)
    mask3 = mask2 * pltpu.roll(keep, 2, 1)
    line = lax.broadcasted_iota(jnp.int32, (LANES, t), 0)

    def spread(v):
        return jnp.broadcast_to(v[0:1, :], (LANES, t))

    stacked = jnp.where(line == 0, spread(keep), 0.0)
    stacked = jnp.where(line == 1, spread(mask2), stacked)
    stacked = jnp.where(line == 2, spread(mask3), stacked)
    stacked = jnp.where(line == 3, spread(mark), stacked)
    mcol[0:t, :] = stacked.T

    for copy in loads[7:]:
        copy.wait()
    for n, ref in enumerate((gain, cb, dtb, skip)):
        count = ref.shape[0]
        lines[n : n + 1, 0:count] = ref[...].reshape(1, count)
    cw_own = cw[...]
    cb_own = lines[1:2, pl.ds(chan, w)]
    taps = cw.shape[0]

    def conv_block(b, carry):
        at = pl.multiple_of(b * STEP, STEP)
        view = inner.at[pl.ds(at, STEP + 8)]
        masks = mcol[pl.ds(at, STEP), :]
        for sl in halves:
            total = cb_own[:, sl] + cw_own[taps - 1 : taps, sl] * view[8 : 8 + STEP, sl]
            for j in range(1, taps):
                tap = cw_own[taps - 1 - j : taps - j, sl]
                total = total + tap * view[8 - j : 8 - j + STEP, sl] * masks[:, j - 1 : j]
            sg = 1.0 / (1.0 + jnp.exp(-total))
            value = total * sg
            act[pl.ds(at, STEP), sl] = value
            actl[pl.ds(at, STEP), sl] = value.astype(bf16)
            dsilu[pl.ds(at, STEP), sl] = sg * (1.0 + total * (1.0 - sg))
        return carry

    lax.fori_loop(0, chunks, conv_block, 0)
    xw_own = xw[...]
    pp[:, 0:nproj] = mm(actl[...], xw_own, NT)
    proj_copy = Send(lambda: (pp, pq), row, other)

    for sl in lane_tiles(w, 2 * LANES):
        gate[:, sl] = mm(ng[0], win_g[:, sl])
        dgated[:, sl] = mm(ng[1], wo[sl, :], NT)

    def dy_block(b, carry):
        at = pl.ds(pl.multiple_of(b * STEP, STEP), STEP)
        for sl in halves:
            g = gate[at, sl]
            low = (dgated[at, sl] * (g / (1.0 + jnp.exp(-g)))).astype(bf16)
            dyf[at, sl] = low.astype(f32)
        return carry

    lax.fori_loop(0, chunks, dy_block, 0)

    share_on(1)

    proj_copy.wait_recv()
    proj = pp[...] + pq[...]
    turned = proj.T
    for k in range(chunks):
        cols = slice(k * STEP, (k + 1) * STEP)
        bt[k, :, 0:STEP] = turned[rank : rank + states, cols]
        ct[k, :, 0:STEP] = turned[rank + states : rank + 2 * states, cols]
    rank_low = proj[:, 0:rank].astype(bf16)
    rank_turned = turned[0:rank, :].astype(bf16)
    dtw_own = dtw[...]
    dtb_own = lines[2:3, pl.ds(chan, w)]
    for sl in lane_tiles(w, 2 * LANES):
        sig[:, sl] = mm(rank_low, dtw_own[:, sl]) + dtb_own[:, sl]

    def delta_block(b, carry):
        at = pl.ds(pl.multiple_of(b * STEP, STEP), STEP)
        marked = mcol[at, :][:, 3:4] > 0.5
        for sl in halves:
            pre = sig[at, sl]
            e = jnp.exp(-jnp.abs(pre))
            one = 1.0 + e
            log1p = jnp.where(one == 1.0, e, jnp.log(one) * (e / (one - 1.0)))
            delta = jnp.maximum(pre, 0.0) + log1p
            sig[at, sl] = jnp.where(pre >= 0.0, 1.0, e) / one
            inflow = delta * act[at, sl]
            u[at, sl] = inflow
            s1[at, sl] = delta
            ddec[at, sl] = jnp.where(marked, 1e30, delta)
        return carry

    lax.fori_loop(0, chunks, delta_block, 0)

    span = STEP * states
    pick = (
        lax.broadcasted_iota(jnp.int32, (states, span), 0)
        == lax.broadcasted_iota(jnp.int32, (states, span), 1) % states
    ).astype(bf16)
    diag = (
        lax.broadcasted_iota(jnp.int32, (t, span), 0) % STEP
        == lax.broadcasted_iota(jnp.int32, (t, span), 1) // states
    )
    ones_diag = diag[0:STEP].astype(bf16)
    b_low = proj[:, rank : rank + states].astype(bf16)
    c_low = proj[:, rank + states : rank + 2 * states].astype(bf16)
    bbd[...] = jnp.where(diag, mm(b_low, pick), 0.0).astype(bf16)
    cbd[...] = jnp.where(diag, mm(c_low, pick), 0.0).astype(bf16)

    rates = [-jnp.exp(alog[:, j * LANES : (j + 1) * LANES]) for j in range(tiles)]
    zeros = tuple(jnp.zeros((states, LANES), f32) for _ in range(tiles))
    tile = [slice(j * LANES, (j + 1) * LANES) for j in range(tiles)]

    def even_at(m):
        return pl.multiple_of(m * span, span)

    def odd_at(m):
        return pl.multiple_of(states + m * span, states)

    def state_block(ref, first, i):
        return ref.at[pl.ds(pl.multiple_of(first + i * states, states), states)]

    def scan_chunk(k, state, kept, first):
        rows = pl.ds(pl.multiple_of(k * STEP, STEP), STEP)
        b_here, dec, flow = bt[k], ddec.at[rows], u.at[rows]
        state = list(state)
        for i in range(STEP):
            b_wide = jnp.broadcast_to(b_here[:, i : i + 1], (states, LANES))
            dest = state_block(kept, first, i)
            for j, sl in enumerate(tile):
                decay = jnp.exp(dec[i : i + 1, sl] * rates[j])
                state[j] = decay * state[j] + flow[i : i + 1, sl] * b_wide
                dest[:, sl] = state[j].astype(bf16)
        return state

    def read_chunk(k, kept, first):
        rows = pl.ds(pl.multiple_of(k * STEP, STEP), STEP)
        du[rows, :] = mm(cbd[rows, :], kept[pl.ds(pl.multiple_of(first, states), span), :])


    def gated_block(b, carry):
        skip_own = lines[3:4, pl.ds(chan, w)]
        at = pl.ds(pl.multiple_of(b * STEP, STEP), STEP)
        for sl in halves:
            y = (du[at, sl] + skip_own[:, sl] * act[at, sl]).astype(bf16).astype(f32)
            g = gate[at, sl]
            sg = 1.0 / (1.0 + jnp.exp(-g))
            gt[at, sl] = (y * (g * sg)).astype(bf16)
            dgl[at, sl] = (dgated[at, sl] * y * (sg * (1.0 + g * (1.0 - sg)))).astype(bf16)
        return carry

    class Sum:
        def __init__(self, n, source):
            self.n, self.source, self.factors = n, source, []
            self.lines = zrows + (extra if n == 2 else 0)
            self.near, self.far, self.twin = [], [], []

        def send_factors(self, part):
            n, at = self.n, slice(part * tl, (part + 1) * tl)
            for sl in tile:
                turn[n, sl, at] = self.source[at, sl].T
            for s in range(1, PLANE):
                refs = lambda s=s: (
                    turn.at[n, block(plane_place[s], quarter), at],
                    fac.at[n, s - 1, :, at],
                )
                self.factors.append(Send(refs, plane_row[s], core))

        def rows(self, where, first, count):
            ref = (gout, ggate, gmix)[self.n]
            first = (core * PLANE + where) * DEPTH * self.lines + first
            return ref.at[pl.ds(pl.multiple_of(first, count), count), :]

        def shard(self, where, z):
            return self.rows(where, z * self.lines, self.lines)

        def partial(self):
            n = self.n
            for copy in self.factors:
                copy.wait_recv()
            kind = 1 if n == 0 else 0
            lefts = [turn[n, block(place, quarter), :]] + [fac[n, s] for s in range(PLANE - 1)]
            for sl in lane_tiles(d, 2 * LANES):
                total = mm(lefts[0], ng[kind, :, sl])
                for s in range(PLANE - 1):
                    total = total + mm(lefts[s + 1], ngh[s, kind, :, sl])
                pw[:, sl] = total
                pb[n, :, sl] = total.astype(bf16)
            pown[n] = pw[block(pz, zrows), :]
            self.depth = [
                Send(
                    lambda s=s: (pb.at[n, block(z_place[s], zrows), :], zr.at[n, s - 1]),
                    z_row[s],
                    core,
                )
                for s in range(1, DEPTH)
            ]

        def near_shard(self, z):
            part = pair_to(lambda: self.shard(place, z))
            self.near.append([Send(part, plane_row[s], core) for s in (1, 2)])

        def total(self):
            for copy in self.depth:
                copy.wait_recv()
            total = pown[self.n]
            for s in range(DEPTH - 1):
                total = total + zr[self.n, s].astype(f32)
            part = self.shard(place, pz)
            part[0:zrows, :] = total.astype(bf16)
            if self.n == 2:
                for copy in small_depth:
                    copy.wait_recv()
                total = sms[block(place * DEPTH + pz, extra), :]
                for s in range(DEPTH - 1):
                    total = total + szr[s].astype(f32)
                part[zrows:, 0:packed] = total.astype(bf16)
                part[zrows:, packed:] = jnp.zeros((extra, d - packed), bf16)
            own = pair_to(lambda: self.shard(place, pz))
            self.along = [Send(own, z_row[s], core) for s in (1, 2)]
            self.beyond = []
            self.near_shard(pz)

        def pass_on(self, s):
            if s < 3:
                self.along[s - 1].wait_recv()
                part = pair_to(lambda: self.shard(place, z_place[s]).at[:, halves[s - 1]])
                self.beyond.append(Send(part, z_row[3 - s], core))
            else:
                for copy in self.beyond:
                    copy.wait_recv()
            self.near_shard(z_place[s])
            if s == DEPTH - 1:
                self.to_twin(place)

        def pass_across(self, s):
            for copy in self.near[s]:
                copy.wait_recv()
            q = 1 + s % 2
            part = pair_to(lambda: self.shard(plane_place[q], z_place[s]))
            self.far.append(Send(part, plane_row[3 - q], core))
            if s == DEPTH - 1:
                for q in (1, 2):
                    self.to_twin(plane_place[q])

        def to_twin(self, where):
            self.twin.append(Send(pair_to(lambda: self.rows(where, 0, DEPTH * self.lines)), row, other))

        def finish(self):
            for copy in self.far:
                copy.wait_recv()
            self.to_twin(plane_place[3])

    sum_out, sum_gate, sum_in = Sum(0, gt), Sum(1, dgl), Sum(2, dil)

    def gated_half(part):
        lax.fori_loop(part * chunks // 2, (part + 1) * chunks // 2, gated_block, 0)
        sum_out.send_factors(part)

    pairs = chunks // 2
    odd[pl.ds(states, span), :] = jnp.zeros((span, w), bf16)

    def scan_pair(m, state):
        read_chunk(jnp.maximum(2 * m - 1, 0), odd, odd_at(jnp.maximum(m - 1, 0)))
        state = scan_chunk(2 * m, state, even, even_at(m))
        read_chunk(2 * m, even, even_at(m))
        state = scan_chunk(2 * m + 1, state, odd, odd_at(m))

        @pl.when(m == pairs // 2 - 1)
        def _():
            read_chunk(chunks // 2 - 1, odd, odd_at(pairs // 2 - 1))
            gated_half(0)
            share_on(0)

        return tuple(state)

    final = lax.fori_loop(0, pairs, scan_pair, zeros)
    read_chunk(chunks - 1, odd, odd_at(pairs - 1))
    gated_half(1)
    share_end(1)
    sum_gate.send_factors(0)
    sum_gate.send_factors(1)

    late = sum(dyf[t - 1 : t, sl] * final[j] for j, sl in enumerate(tile))
    lastc[...] = jnp.broadcast_to(jnp.sum(late, axis=1, keepdims=True), (states, LANES))

    def back_chunk(k, carry, kept, first, before, last, gbuf, qbuf, bbuf, cbuf):
        base = pl.multiple_of(k * STEP, STEP)
        rows = pl.ds(base, STEP)
        c_here, dec, dys, inflow = ct[k], ddec.at[rows], dyf.at[rows], u.at[rows]
        dys_before = dyf.at[pl.ds(pl.multiple_of(jnp.maximum(base - STEP, 0), STEP), STEP)]
        flow, acc = list(carry[0]), list(carry[1])
        for i in reversed(range(STEP)):
            c_wide = jnp.broadcast_to(c_here[:, i : i + 1], (states, LANES))
            at = slice(i * states, (i + 1) * states)
            old = state_block(kept, first, i - 1) if i else state_block(before, last, 0)
            dy_old = dys_before[STEP - 1 : STEP, :] if i == 0 else dys[i - 1 : i, :]
            for_b = for_c = None
            for j, sl in enumerate(tile):
                rate = dec[i : i + 1, sl]
                g = c_wide * dys[i : i + 1, sl] + flow[j]
                gbuf[at, sl] = g.astype(bf16)
                flow[j] = g * jnp.exp(rate * rates[j])
                h_old = old[:, sl].astype(f32)
                q = flow[j] * h_old
                acc[j] = acc[j] + q * rate
                qbuf[at, sl] = (q * rates[j]).astype(bf16)
                term_b, term_c = g * inflow[i : i + 1, sl], h_old * dy_old[:, sl]
                for_b = term_b if for_b is None else for_b + term_b
                for_c = term_c if for_c is None else for_c + term_c
            bbuf[at, :] = for_b.astype(bf16)
            cbuf[at, :] = for_c.astype(bf16)
        return flow, acc

    lane_of = lax.broadcasted_iota(jnp.int32, (states, LANES), 1)
    ones = jnp.ones((LANES, LANES), bf16)

    def back_sums(k, gbuf, qbuf, bbuf, cbuf):
        rows = pl.ds(pl.multiple_of(k * STEP, STEP), STEP)
        for parts, dest in ((bbuf, dbt), (cbuf, dct)):
            summed = mm(parts[...], ones)
            value = jnp.zeros((states, LANES), f32)
            for i in range(STEP):
                value = jnp.where(lane_of == i, summed[i * states : (i + 1) * states, :], value)
            dest[k] = value
        du[rows, :] = mm(bbd[rows, :], gbuf[...])
        sq[rows, :] = mm(ones_diag, qbuf[...])

    even_bufs, odd_bufs = (ga, qa, ba, ca), (gb, qb, bb, cc)

    def out_block(b, carry):
        at = pl.multiple_of(b * STEP, STEP)
        rows = pl.ds(at, STEP)
        total = outp[pl.ds(mine + at, STEP), :] + outr[rows, :]
        out[rows, :] = (ng[2, pl.ds(mine + at, STEP), :].astype(f32) + total).astype(bf16)
        return carry

    first = nproj + rank + states
    line_conv, line_cb, line_dtb, line_skip, line_gain = (
        first,
        first + taps,
        first + taps + 1,
        first + taps + 2,
        first + taps + 3,
    )
    tot_dtb, tot_skip, tot_conv = 0, 1, 2
    dproj_copies = {}

    def read_tot(n):
        return tuple(tot[n, :, sl] for sl in halves)

    def write_tot(n, values):
        for value, sl in zip(values, halves):
            tot[n, :, sl] = value

    def dpre_block(b, carry):
        at = pl.ds(pl.multiple_of(b * STEP, STEP), STEP)
        skip_own = lines[3:4, pl.ds(chan, w)]
        sums, gains = [], []
        for n, sl in enumerate(halves):
            flow, value, dy = du[at, sl], act[at, sl], dyf[at, sl]
            dpre = (sq[at, sl] + flow * value) * sig[at, sl]
            dpl[at, sl] = dpre.astype(bf16)
            s1[at, sl] = flow * s1[at, sl] + skip_own[:, sl] * dy
            both = dy * value
            sums.append(carry[0][n] + dpre[0:8] + dpre[8:16])
            gains.append(carry[1][n] + both[0:8] + both[8:16])
        return tuple(sums), tuple(gains)

    def projection_grads(part):
        at = slice(part * tl, (part + 1) * tl)
        span_of = (part * chunks // 2, (part + 1) * chunks // 2)
        sums, gains = lax.fori_loop(*span_of, dpre_block, (read_tot(tot_dtb), read_tot(tot_skip)))
        write_tot(tot_dtb, sums)
        write_tot(tot_skip, gains)
        for k in range(*span_of):
            cols = slice(k * STEP, (k + 1) * STEP)
            tsc[rank : rank + states, cols] = dbt[k][:, 0:STEP]
            tsc[rank + states : nproj, cols] = dct[k][:, 0:STEP]
        end = lastc[:, 0:1] if part else dct[chunks // 2][:, 0:1]
        shifted = pltpu.roll(tsc[rank + states : nproj, at], tl - 1, 1)
        at_end = lax.broadcasted_iota(jnp.int32, (states, tl), 1) == tl - 1
        tsc[rank + states : nproj, at] = jnp.where(at_end, end, shifted)
        pp2[at, :] = tsc[:, at].T
        pp2[at, 0:rank] = mm(dpl[at, :], dtw[...], NT)
        dproj_copies[part] = Send(lambda: (pp2.at[at, :], pq2.at[at, :]), row, other)

    def dconv_block(b, carry):
        at = pl.multiple_of(b * STEP, STEP)
        view = inner.at[pl.ds(at, STEP + 8)]
        rows = pl.ds(at, STEP)
        masks = mcol[rows, :]
        sums = [list(v) for v in carry]
        for n, sl in enumerate(halves):
            grad = (s1[rows, sl] + sq[rows, sl]) * dsilu[rows, sl]
            dconv[rows, sl] = grad
            terms = [grad, grad * view[8 : 8 + STEP, sl]]
            for j in range(1, taps):
                terms.append(grad * masks[:, j - 1 : j] * view[8 - j : 8 - j + STEP, sl])
            for m, term in enumerate(terms):
                sums[m][n] = sums[m][n] + term[0:8] + term[8:16]
        return tuple(tuple(v) for v in sums)

    def dinner_block(b, carry):
        at = pl.multiple_of(b * STEP, STEP)
        view = dconv.at[pl.ds(at, STEP + 8)]
        masks = mcol.at[pl.ds(at, STEP + 8)]
        cw_own = cw[...]
        for sl in halves:
            total = cw_own[taps - 1 : taps, sl] * view[0:STEP, sl]
            for j in range(1, taps):
                tap = cw_own[taps - 1 - j : taps - j, sl]
                total = total + tap * view[j : j + STEP, sl] * masks[j : j + STEP, j - 1 : j]
            dil[pl.ds(at, STEP), sl] = total.astype(bf16)
        return carry

    def inner_grads(part):
        at = slice(part * tl, (part + 1) * tl)
        span_of = (part * chunks // 2, (part + 1) * chunks // 2)
        dproj_copies[part].wait_recv()
        dproj = pp2[at, :] + pq2[at, :]
        pq2[at, :] = dproj
        dproj_low = dproj[:, 0:nproj].astype(bf16)
        for sl in lane_tiles(w, 2 * LANES):
            sq[at, sl] = mm(dproj_low, xw[:, sl])
        names = range(tot_conv, tot_conv + taps + 1)
        sums = lax.fori_loop(*span_of, dconv_block, tuple(read_tot(n) for n in names))
        for n, values in zip(names, sums):
            write_tot(n, values)
        lax.fori_loop(*span_of, dinner_block, 0)
        sum_in.send_factors(part)

    def late_half():
        back_sums(chunks // 2, *even_bufs)
        projection_grads(1)

    def out_sums():
        for copy in relays[1]:
            copy.wait_recv()
        sum_out.partial()

    def gate_sums():
        for copy in relays[0]:
            copy.wait_recv()
        sum_gate.partial()

    events = (
        (1, lambda: share_end(0)),
        (2, out_sums),
        (3, late_half),
        (5, gate_sums),
        (6, lambda: inner_grads(1)),
        (7, lambda: sum_out.total()),
    )

    def back_pair(step, carry):
        m = pairs - 1 - step
        back_sums(jnp.minimum(2 * m + 2, chunks - 1), *even_bufs)
        carry = back_chunk(2 * m + 1, carry, odd, odd_at(m), even, even_at(m) + span - states, *odd_bufs)
        back_sums(2 * m + 1, *odd_bufs)
        flow, acc = back_chunk(2 * m, carry, even, even_at(m), odd, even_at(m), *even_bufs)
        for when, event in events:
            pl.when(step == when * pairs // 8)(event)
        return tuple(flow), tuple(acc)

    carry = lax.fori_loop(0, pairs, back_pair, (zeros, zeros))
    back_sums(0, *even_bufs)
    for j, sl in enumerate(tile):
        sm[nproj + rank : first, sl] = carry[1][j] * rates[j]
    projection_grads(0)
    for sl in lane_tiles(d, 2 * LANES):
        dn[:, sl] = mm(dgl[...], win_g[sl, :], NT)
    inner_grads(0)
    sum_gate.total()
    sum_out.pass_on(1)
    sum_out.pass_on(2)
    for sl in lane_tiles(d, 2 * LANES):
        dn[:, sl] = dn[:, sl] + mm(dil[...], win_i[sl, :], NT)
    dn_copy = Send(lambda: (dn.at[pl.ds(theirs, tl), :], dnr), row, other)
    dproj_turned = pq2[...].T[0:nproj, :].astype(bf16)
    for sl in lane_tiles(w, 2 * LANES):
        sm[0:nproj, sl] = mm(dproj_turned, actl[:, sl])
        sm[nproj : nproj + rank, sl] = mm(rank_turned, dpl[:, sl])

    def put_line(line, n):
        for value, sl in zip(read_tot(n), halves):
            sm[line : line + 1, sl] = jnp.sum(value, axis=0, keepdims=True)

    put_line(line_dtb, tot_dtb)
    put_line(line_skip, tot_skip)
    put_line(line_cb, tot_conv)
    for j in range(taps):
        put_line(line_conv + taps - 1 - j, tot_conv + 1 + j)
    def gain_block(b, carry):
        rows = pl.ds(pl.multiple_of(b * STEP, STEP), STEP)
        values = ng[2, rows, :].astype(f32)
        scale = lax.rsqrt(jnp.mean(values * values, axis=-1, keepdims=True) + EPS)
        both = dn[rows, :] * (values * scale)
        return carry + both[0:8] + both[8:16]

    total = lax.fori_loop(0, chunks, gain_block, jnp.zeros((8, d), f32))
    sm[line_gain : line_gain + 1, :] = jnp.sum(total, axis=0, keepdims=True)
    across_tiles = packed // LANES
    for n in range(sm.shape[0] // 16 * tiles):
        to = slice(n // across_tiles * 16, n // across_tiles * 16 + 16)
        to_lanes = tile[n % across_tiles]
        value = sm[n // tiles * 16 : n // tiles * 16 + 16, tile[n % tiles]]
        smb[to, to_lanes] = value.astype(bf16)
        sms[to, to_lanes] = value
    srows = DEPTH * extra
    over_plane = [
        Send(
            lambda s=s: (smb.at[block(plane_place[s], srows), :], sfac.at[s - 1]),
            plane_row[s],
            core,
        )
        for s in range(1, PLANE)
    ]
    sum_in.partial()
    sum_out.pass_on(3)
    sum_gate.pass_on(1)
    sum_gate.pass_on(2)
    sum_out.pass_across(0)
    for copy in over_plane:
        copy.wait_recv()
    total = sms[block(place, srows), :]
    for s in range(PLANE - 1):
        total = total + sfac[s].astype(f32)
    sms[block(place, srows), :] = total
    spb[...] = total.astype(bf16)
    small_depth = [
        Send(lambda s=s: (spb.at[block(z_place[s], extra), :], szr.at[s - 1]), z_row[s], core)
        for s in range(1, DEPTH)
    ]
    sum_out.pass_across(1)
    sum_out.pass_across(2)
    sum_out.pass_across(3)
    sum_gate.pass_on(3)

    for sl in lane_tiles(d, 2 * LANES):
        outp[:, sl] = mm(gt[...], wo[:, sl])
    out_copy = Send(lambda: (outp.at[pl.ds(theirs, tl), :], outr), row, other)

    def norm_back(b, carry):
        at = pl.multiple_of(b * STEP, STEP)
        rows = pl.ds(at, STEP)
        values = ng[2, pl.ds(mine + at, STEP), :].astype(f32)
        scale = lax.rsqrt(jnp.mean(values * values, axis=-1, keepdims=True) + EPS)
        unit_rows = values * scale
        inside = (dn[pl.ds(mine + at, STEP), :] + dnr[rows, :]) * lines[0:1, 0:d]
        mean = jnp.mean(inside * unit_rows, axis=-1, keepdims=True)
        given = ng[1, pl.ds(mine + at, STEP), :].astype(f32)
        gtok[rows, :] = (given + scale * (inside - unit_rows * mean)).astype(bf16)
        return carry

    dn_copy.wait_recv()
    lax.fori_loop(0, tl // STEP, norm_back, 0)
    out_copy.wait_recv()
    lax.fori_loop(0, tl // STEP, out_block, 0)

    sum_in.total()
    sum_gate.pass_across(0)
    sum_gate.pass_across(1)
    sum_out.finish()
    sum_in.pass_on(1)
    sum_in.pass_on(2)
    sum_gate.pass_across(2)
    sum_gate.pass_across(3)
    sum_in.pass_on(3)
    sum_in.pass_across(0)
    sum_gate.finish()
    for s in (1, 2, 3):
        sum_in.pass_across(s)
    sum_in.finish()
    for copy in sum_out.twin + sum_gate.twin + sum_in.twin:
        copy.wait_recv()
    for copy in pending:
        copy.wait_send()


def wide_kernel(packed, output, grad_tokens, gout, ggate, gmix, *refs):
    out_o, out_t, gin_f, gout_f, *rows, wide_in, wide_out, value, sems = refs
    steps = wide_in.shape[0]
    cols, lines = wide_in.shape[2], wide_out.shape[1]
    copies = [
        pltpu.make_async_copy(output, out_o, sems.at[2, 0]),
        pltpu.make_async_copy(grad_tokens, out_t, sems.at[2, 1]),
    ]
    for copy in copies:
        copy.start()
    e, d = ggate.shape
    blocks = e // cols
    shards = 2 * TEAM
    zrows, stride = e // shards, gmix.shape[0] // shards
    per = shards // blocks

    def piece(n, first, last):
        return gmix[n * stride + first : n * stride + last, :]

    for i in range(steps):
        if i < blocks:
            turned = jnp.concatenate([piece(i * per + n, 0, zrows) for n in range(per)], axis=0).T
        else:
            turned = ggate[(i - blocks) * cols : (i - blocks + 1) * cols, :].T
        wide_in[i] = turned.astype(f32)
        at = slice(i * cols, (i + 1) * cols)
        copies.append(pltpu.make_async_copy(wide_in.at[i], gin_f.at[:, at], sems.at[0, i]))
        copies[-1].start()
        at = slice(i * lines, (i + 1) * lines)
        wide_out[i] = gout[at, :].astype(f32)
        copies.append(pltpu.make_async_copy(wide_out.at[i], gout_f.at[at, :], sems.at[1, i]))
        copies[-1].start()

    matrices = [ref for ref in rows if len(ref.shape) == 2]
    vectors = [ref for ref in rows if len(ref.shape) == 1]
    gain = 0.0
    tiles, across = d // LANES, packed // LANES
    for core in range(2):
        for n in range(value.shape[0] // 16 * tiles):
            first = (core * TEAM + n // across) * stride + zrows
            at_row, at_lane, lane = n // tiles * 16, n % tiles * LANES, n % across * LANES
            value[at_row : at_row + 16, at_lane : at_lane + LANES] = gmix[
                first : first + 16, lane : lane + LANES
            ].astype(f32)
        at_lanes = slice(core * d, (core + 1) * d)
        at = 0
        for ref in matrices:
            ref[:, at_lanes] = value[at : at + ref.shape[0], :]
            at += ref.shape[0]
        for ref in vectors[:-1]:
            ref[at_lanes] = value[at : at + 1, :].reshape(d)
            at += 1
        gain = gain + value[at : at + 1, :]
    vectors[-1][...] = gain.reshape(d)
    for copy in copies:
        copy.wait()


def local(
    tokens, marks, norm_gain, in_weight, conv_weight, conv_bias, x_weight, dt_weight,
    dt_bias, a_log, skip, out_weight, cotangent,
):
    tl, d = tokens.shape[1:]
    e = out_weight.shape[0]
    w = e // lax.axis_size("seq")
    t = tl * lax.axis_size("seq")
    states, rank, nproj, taps = a_log.shape[0], dt_weight.shape[0], x_weight.shape[0], conv_weight.shape[0]
    chunks, span = t // STEP, STEP * states
    quarter = w // PLANE
    zrows = quarter // DEPTH
    lines = -(-(nproj + rank + states + taps + 4) // 16) * 16
    packed = -(-(lines // 16) * (w // LANES) // TEAM) * LANES
    small = 16 * TEAM
    srows = zrows + 16
    vmem = pl.BlockSpec(memory_space=pltpu.VMEM)
    anywhere = pl.BlockSpec(memory_space=pl.ANY)
    wide = pltpu.VMEM((t, w), f32)
    low = pltpu.VMEM((t, w), bf16)
    one = pltpu.VMEM((t, LANES), f32)
    scratch = [
        pltpu.VMEM((d, w), bf16), pltpu.VMEM((d, w), bf16), pltpu.VMEM((w, d), bf16),
        pltpu.VMEM((d,), f32), pltpu.VMEM((taps, w), f32), pltpu.VMEM((e,), f32),
        pltpu.VMEM((nproj, w), bf16), pltpu.VMEM((rank, w), bf16), pltpu.VMEM((e,), f32),
        pltpu.VMEM((states, w), f32), pltpu.VMEM((e,), f32), pltpu.VMEM((8, tl), jnp.int32),
        pltpu.VMEM((3, t, d), bf16), pltpu.VMEM((PLANE - 1, 2, t, d), bf16),
        pltpu.VMEM((8, t), f32), pltpu.VMEM((t + 8, LANES), f32), pltpu.VMEM((8, e), f32),
        pltpu.VMEM((t + 8, w), f32), wide, wide, wide, wide, low, wide, wide, wide, wide, wide, wide, wide,
        one, one, one, one, pltpu.VMEM((LANES, t), f32),
        pltpu.VMEM((t * states // 2, w), bf16), pltpu.VMEM((t * states // 2 + states, w), bf16),
        pltpu.VMEM((chunks, states, LANES), f32), pltpu.VMEM((chunks, states, LANES), f32),
        pltpu.VMEM((t, span), bf16), pltpu.VMEM((t, span), bf16),
        *[pltpu.VMEM((span, w), bf16)] * 4, *[pltpu.VMEM((span, LANES), bf16)] * 4,
        *[pltpu.VMEM((chunks, states, LANES), f32)] * 2,
        pltpu.VMEM((states, LANES), f32), pltpu.VMEM((taps + 3, 8, w), f32),
        low, low, low, low, pltpu.VMEM((3, w, t), bf16), pltpu.VMEM((t + 8, w), f32),
        pltpu.VMEM((t, d), f32), pltpu.VMEM((tl, d), f32),
        pltpu.VMEM((t, d), f32), pltpu.VMEM((tl, d), f32),
        pltpu.VMEM((3, PLANE - 1, quarter, t), bf16), pltpu.VMEM((quarter, d), f32),
        pltpu.VMEM((3, zrows, d), f32), pltpu.VMEM((3, quarter, d), bf16),
        pltpu.VMEM((3, DEPTH - 1, zrows, d), bf16),
        pltpu.VMEM((lines, w), f32), pltpu.VMEM((small, packed), bf16), pltpu.VMEM((small, packed), f32),
        pltpu.VMEM((PLANE - 1, small // PLANE, packed), bf16), pltpu.VMEM((small // PLANE, packed), bf16),
        pltpu.VMEM((DEPTH - 1, 16, packed), bf16),
        pltpu.SemaphoreType.DMA((16,)),
        pltpu.SemaphoreType.DMA((128,)), pltpu.SemaphoreType.DMA((128,)),
    ]
    output, grad_tokens, gout, ggate, gmix = pl.pallas_call(
        body_kernel,
        out_shape=[
            pltpu.VMEM((tl, d), bf16),
            pltpu.VMEM((tl, d), bf16),
            pltpu.VMEM((e, d), bf16),
            pltpu.VMEM((e, d), bf16),
            pltpu.VMEM((2 * TEAM * srows, d), bf16),
        ],
        in_specs=[anywhere] * 13,
        out_specs=[vmem] * 5,
        scratch_shapes=scratch,
        compiler_params=pltpu.CompilerParams(
            collective_id=0, has_side_effects=True, vmem_limit_bytes=56 * 2**20
        ),
        name="block",
    )(
        tokens.reshape(tl, d), marks.reshape(1, tl), norm_gain, in_weight, conv_weight,
        conv_bias, x_weight, dt_weight, dt_bias, a_log, skip, out_weight, cotangent.reshape(tl, d),
    )

    steps = 8
    shapes = [(nproj, e), (rank, e), (states, e), (taps, e), (e,), (e,), (e,), (d,)]
    wide_shapes = [jax.ShapeDtypeStruct(s, f32) for s in [(d, 2 * e), (e, d)] + shapes]
    output, grad_tokens, *grads = pl.pallas_call(
        functools.partial(wide_kernel, packed),
        out_shape=[jax.ShapeDtypeStruct((tl, d), bf16)] * 2 + wide_shapes,
        in_specs=[vmem] * 5,
        out_specs=[anywhere] * 4 + [vmem] * len(shapes),
        scratch_shapes=[
            pltpu.VMEM((steps, d, 2 * e // steps), f32),
            pltpu.VMEM((steps, e // steps, d), f32),
            pltpu.VMEM((lines, w), f32),
            pltpu.SemaphoreType.DMA((3, steps)),
        ],
        compiler_params=pltpu.CompilerParams(vmem_limit_bytes=40 * 2**20),
        name="widen",
    )(output, grad_tokens, gout, ggate, gmix)
    rows = lax.axis_size("rows")
    if rows > TEAM:
        grads = [v * (1.0 / TEAM) for v in lax.psum(grads, "rows")]
    grad_in, grad_out, grad_x, grad_dt, grad_log, grad_conv, g_cb, g_dtb, g_skip, g_gain = grads
    return (
        output[None], grad_tokens[None], g_gain, grad_in, grad_conv, g_cb, grad_x, grad_dt, g_dtb, grad_log,
        g_skip, grad_out,
    )


def solution(mesh):
    split = P("rows", "seq", None)
    whole = P()
    in_specs = (split, P("rows", "seq")) + (whole,) * 10 + (split,)
    out_specs = (split, split) + (whole,) * 10
    return jax.shard_map(local, mesh=mesh, in_specs=in_specs, out_specs=out_specs, check_vma=False)
```

```python
import functools

import jax
import jax.numpy as jnp
from jax import lax
from jax.experimental import pallas as pl
from jax.experimental.pallas import tpu as pltpu
from jax.sharding import PartitionSpec as P

f32 = jnp.float32
bf16 = jnp.bfloat16
EPS = 1e-05
LANES = 128
STEP = 16
PLANE = 4
DEPTH = 4
TEAM = PLANE * DEPTH
MESH = pl.DeviceIdType.MESH
NN = (((1,), (0,)), ((), ()))
NT = (((1,), (1,)), ((), ()))


def mm(a, b, dims=NN):
    return lax.dot_general(a, b, dims, preferred_element_type=f32)


def lane_tiles(width, size):
    return [slice(j, j + size) for j in range(0, width, size)]


def body_kernel(
    tok, marks, gain_in, win, cw_in, cb_in, xw_in, dtw_in, dtb_in, alog_in, skip_in, wout, cot,
    out, gtok, gout, ggate, gmix,
    win_i, win_g, wo, gain, cw, cb, xw, dtw, dtb, alog, skip, mkraw, ng, ngh, mk, mcol, lines,
    inner, gate, dgated, act, dsilu, actl, ddec, u, sig, dyf, du, s1, sq,
    pp, pq, pp2, pq2, tsc, even, odd, bt, ct, cbd, bbd, ga, gb, qa, qb, ba, bb, ca, cc, dbt, dct, lastc, tot,
    gt, dgl, dpl, dil, turn, dconv, dn, dnr, outp, outr,
    fac, pw, pown, pb, zr, sm, smb, sms, sfac, spb, szr,
    ls, ss, rs,
):
    row, core = lax.axis_index("rows"), lax.axis_index("seq")
    other = 1 - core
    team = row - row % TEAM
    px, py, pz = row % 2, (row // 2) % 2, (row // PLANE) % DEPTH
    tl, d = out.shape
    t = 2 * tl
    w = wo.shape[0]
    states = alog.shape[0]
    rank = dtw.shape[0]
    nproj = xw.shape[0]
    half = w // 2
    quarter = w // PLANE
    zrows = quarter // DEPTH
    extra, packed = smb.shape[0] // TEAM, smb.shape[1]
    place = row % PLANE
    chunks = t // STEP
    tiles = w // LANES
    mine = pl.multiple_of(core * tl, tl)
    theirs = pl.multiple_of(other * tl, tl)
    chan = pl.multiple_of(core * w, w)
    halves = lane_tiles(w, half)
    pending = []

    def flip(low, high, s):
        a, b = s % 2, s // 2
        return (high + b - 2 * b * high) * 2 + low + a - 2 * a * low

    plane_place = [flip(px, py, s) for s in range(PLANE)]
    plane_row = [team + pz * PLANE + plane_place[s] for s in range(PLANE)]
    z_place = [flip(pz % 2, pz // 2, s) for s in range(DEPTH)]
    z_row = [team + z_place[s] * PLANE + place for s in range(DEPTH)]
    ids = iter(range(10_000))

    class Send:
        def __init__(self, refs, to_row, to_core):
            self.refs, self.to, self.k = refs, (to_row, to_core), next(ids)
            self.copy().start()
            pending.append(self)

        def copy(self):
            src, dst = self.refs()
            return pltpu.make_async_remote_copy(
                src_ref=src,
                dst_ref=dst,
                send_sem=ss.at[self.k],
                recv_sem=rs.at[self.k],
                device_id=self.to,
                device_id_type=MESH,
            )

        def wait_recv(self):
            self.copy().wait_recv()

        def wait_send(self):
            self.copy().wait_send()

    def block(index, size):
        return pl.ds(pl.multiple_of(index * size, size), size)

    own = pl.ds(chan, w)
    sources = [
        (tok, ng.at[2, pl.ds(mine, tl), :]),
        (marks, mkraw.at[0:1]),
        (gain_in, gain),
        (win.at[:, own], win_i),
        (cw_in.at[:, own], cw),
        (cb_in, cb),
        (cot, ng.at[1, pl.ds(mine, tl), :]),
        (xw_in.at[:, own], xw),
        (win.at[:, pl.ds(pl.multiple_of(2 * w + core * w, w), w)], win_g),
        (wout.at[own, :], wo),
        (dtw_in.at[:, own], dtw),
        (dtb_in, dtb),
        (skip_in, skip),
        (alog_in.at[:, own], alog),
    ]
    loads = [pltpu.make_async_copy(src, dst, ls.at[n]) for n, (src, dst) in enumerate(sources)]
    for copy in loads:
        copy.start()

    barrier = pltpu.get_barrier_semaphore()
    partners = [(row, other)]
    partners += [(plane_row[s], core) for s in range(1, PLANE)]
    partners += [(z_row[s], core) for s in range(1, DEPTH)]
    for partner in partners:
        pl.semaphore_signal(barrier, inc=1, device_id=partner, device_id_type=MESH)
    pl.semaphore_wait(barrier, len(partners))

    def pair_to(ref):
        return lambda: (ref(), ref())

    def own_rows(kind):
        return ng.at[kind, pl.ds(mine, tl), :]

    def slot(s, kind, first=0, count=tl):
        return ngh.at[s - 1, kind, pl.ds(pl.multiple_of(mine + first, count), count), :]

    twin = [
        Send(lambda n=n, ref=ref: (ref, ng.at[n, pl.ds(mine, tl), :]), row, other)
        for n, ref in ((2, tok), (1, cot))
    ]
    twin.append(Send(lambda: (marks, mkraw.at[1:2]), row, other))
    early, across, relays = {}, {}, {0: [], 1: []}
    piece = tl // 2

    def share(kind):
        early[kind] = [
            Send(lambda s=s: (cot if kind else own_rows(kind), slot(s, kind)), plane_row[s], core)
            for s in (1, 2)
        ]

    def share_on(kind):
        across[kind] = []
        for s in (1, 2):
            early[kind][s - 1].wait_recv()
            first = (s - 1) * piece
            refs = lambda s=s, first=first: (slot(s, kind, first, piece), slot(3, kind, first, piece))
            across[kind].append(Send(refs, plane_row[3 - s], core))
            relays[kind].append(Send(pair_to(lambda s=s: slot(s, kind)), row, other))

    def share_end(kind):
        for s in (1, 2):
            across[kind][s - 1].wait_recv()
            refs = pair_to(lambda first=(s - 1) * piece: slot(3, kind, first, piece))
            relays[kind].append(Send(refs, row, other))

    share(1)

    for copy in loads[:3]:
        copy.wait()
    count = gain.shape[0]
    lines[0:1, 0:count] = gain[...].reshape(1, count)
    unit = 2 * STEP

    def norm_rows(first):
        gain_row = lines[0:1, 0:d]

        def norm_block(b, carry):
            at = pl.ds(pl.multiple_of(first + b * unit, unit), unit)
            rows = ng[2, at, :].astype(f32)
            scale = lax.rsqrt(jnp.mean(rows * rows, axis=-1, keepdims=True) + EPS)
            ng[0, at, :] = (rows * scale * gain_row).astype(bf16)
            return carry

        lax.fori_loop(0, tl // unit, norm_block, 0, unroll=4)

    norm_rows(mine)
    share(0)

    inner[0:8, :] = jnp.zeros((8, w), f32)
    dconv[t : t + 8, :] = jnp.zeros((8, w), f32)
    mcol[t : t + 8, :] = jnp.zeros((8, LANES), f32)
    odd[0:states, :] = jnp.zeros((states, w), bf16)
    tsc[...] = jnp.zeros(tsc.shape, f32)
    tot[...] = jnp.zeros(tot.shape, f32)
    smb[...] = jnp.zeros(smb.shape, bf16)
    sms[...] = jnp.zeros(sms.shape, f32)
    for ref in (ga, qa, ba, ca):
        ref[...] = jnp.zeros(ref.shape, bf16)
    sm[...] = jnp.zeros(sm.shape, f32)

    for copy in twin:
        copy.wait_recv()
    norm_rows(theirs)
    own_marks, twin_marks = mkraw[0:1, :].astype(f32), mkraw[1:2, :].astype(f32)
    mk[:, pl.ds(mine, tl)] = jnp.broadcast_to(own_marks, (8, tl))
    mk[:, pl.ds(theirs, tl)] = jnp.broadcast_to(twin_marks, (8, tl))
    for copy in loads[3:7]:
        copy.wait()

    for sl in lane_tiles(w, 2 * LANES):
        inner[8 : 8 + t, sl] = mm(ng[0], win_i[:, sl]).astype(bf16).astype(f32)

    lane = lax.broadcasted_iota(jnp.int32, (8, t), 1)
    mark = mk[...]
    keep = jnp.where(lane == 0, 0.0, 1.0 - mark)
    mask2 = keep * pltpu.roll(keep, 1, 1)
    mask3 = mask2 * pltpu.roll(keep, 2, 1)
    line = lax.broadcasted_iota(jnp.int32, (LANES, t), 0)

    def spread(v):
        return jnp.broadcast_to(v[0:1, :], (LANES, t))

    stacked = jnp.where(line == 0, spread(keep), 0.0)
    stacked = jnp.where(line == 1, spread(mask2), stacked)
    stacked = jnp.where(line == 2, spread(mask3), stacked)
    stacked = jnp.where(line == 3, spread(mark), stacked)
    mcol[0:t, :] = stacked.T

    for copy in loads[7:]:
        copy.wait()
    for n, ref in enumerate((gain, cb, dtb, skip)):
        count = ref.shape[0]
        lines[n : n + 1, 0:count] = ref[...].reshape(1, count)
    cw_own = cw[...]
    cb_own = lines[1:2, pl.ds(chan, w)]
    taps = cw.shape[0]

    def conv_block(b, carry):
        at = pl.multiple_of(b * STEP, STEP)
        view = inner.at[pl.ds(at, STEP + 8)]
        masks = mcol[pl.ds(at, STEP), :]
        for sl in halves:
            total = cb_own[:, sl] + cw_own[taps - 1 : taps, sl] * view[8 : 8 + STEP, sl]
            for j in range(1, taps):
                tap = cw_own[taps - 1 - j : taps - j, sl]
                total = total + tap * view[8 - j : 8 - j + STEP, sl] * masks[:, j - 1 : j]
            sg = 1.0 / (1.0 + jnp.exp(-total))
            value = total * sg
            act[pl.ds(at, STEP), sl] = value
            actl[pl.ds(at, STEP), sl] = value.astype(bf16)
            dsilu[pl.ds(at, STEP), sl] = sg * (1.0 + total * (1.0 - sg))
        return carry

    lax.fori_loop(0, chunks, conv_block, 0, unroll=4)
    xw_own = xw[...]
    pp[:, 0:nproj] = mm(actl[...], xw_own, NT)
    proj_copy = Send(lambda: (pp, pq), row, other)

    for sl in lane_tiles(w, 2 * LANES):
        gate[:, sl] = mm(ng[0], win_g[:, sl])
        dgated[:, sl] = mm(ng[1], wo[sl, :], NT)

    def dy_block(b, carry):
        at = pl.ds(pl.multiple_of(b * STEP, STEP), STEP)
        for sl in halves:
            g = gate[at, sl]
            low = (dgated[at, sl] * (g / (1.0 + jnp.exp(-g)))).astype(bf16)
            dyf[at, sl] = low.astype(f32)
        return carry

    lax.fori_loop(0, chunks, dy_block, 0, unroll=4)

    share_on(1)

    proj_copy.wait_recv()
    proj = pp[...] + pq[...]
    turned = proj.T
    for k in range(chunks):
        cols = slice(k * STEP, (k + 1) * STEP)
        bt[k, :, 0:STEP] = turned[rank : rank + states, cols]
        ct[k, :, 0:STEP] = turned[rank + states : rank + 2 * states, cols]
    rank_low = proj[:, 0:rank].astype(bf16)
    rank_turned = turned[0:rank, :].astype(bf16)
    dtw_own = dtw[...]
    dtb_own = lines[2:3, pl.ds(chan, w)]
    for sl in lane_tiles(w, 2 * LANES):
        sig[:, sl] = mm(rank_low, dtw_own[:, sl]) + dtb_own[:, sl]

    def delta_block(b, carry):
        at = pl.ds(pl.multiple_of(b * STEP, STEP), STEP)
        marked = mcol[at, :][:, 3:4] > 0.5
        for sl in halves:
            pre = sig[at, sl]
            e = jnp.exp(-jnp.abs(pre))
            one = 1.0 + e
            log1p = jnp.where(one == 1.0, e, jnp.log(one) * (e / (one - 1.0)))
            delta = jnp.maximum(pre, 0.0) + log1p
            sig[at, sl] = jnp.where(pre >= 0.0, 1.0, e) / one
            inflow = delta * act[at, sl]
            u[at, sl] = inflow
            s1[at, sl] = delta
            ddec[at, sl] = jnp.where(marked, 1e30, delta)
        return carry

    lax.fori_loop(0, chunks, delta_block, 0, unroll=4)

    span = STEP * states
    pick = (
        lax.broadcasted_iota(jnp.int32, (states, span), 0)
        == lax.broadcasted_iota(jnp.int32, (states, span), 1) % states
    ).astype(bf16)
    diag = (
        lax.broadcasted_iota(jnp.int32, (t, span), 0) % STEP
        == lax.broadcasted_iota(jnp.int32, (t, span), 1) // states
    )
    ones_diag = diag[0:STEP].astype(bf16)
    b_low = proj[:, rank : rank + states].astype(bf16)
    c_low = proj[:, rank + states : rank + 2 * states].astype(bf16)
    bbd[...] = jnp.where(diag, mm(b_low, pick), 0.0).astype(bf16)
    cbd[...] = jnp.where(diag, mm(c_low, pick), 0.0).astype(bf16)

    rates = [-jnp.exp(alog[:, j * LANES : (j + 1) * LANES]) for j in range(tiles)]
    zeros = tuple(jnp.zeros((states, LANES), f32) for _ in range(tiles))
    tile = [slice(j * LANES, (j + 1) * LANES) for j in range(tiles)]

    def even_at(m):
        return pl.multiple_of(m * span, span)

    def odd_at(m):
        return pl.multiple_of(states + m * span, states)

    def state_block(ref, first, i):
        return ref.at[pl.ds(pl.multiple_of(first + i * states, states), states)]

    def scan_chunk(k, state, kept, first):
        rows = pl.ds(pl.multiple_of(k * STEP, STEP), STEP)
        b_here, dec, flow = bt[k], ddec.at[rows], u.at[rows]
        state = list(state)
        for i in range(STEP):
            b_wide = jnp.broadcast_to(b_here[:, i : i + 1], (states, LANES))
            dest = state_block(kept, first, i)
            for j, sl in enumerate(tile):
                decay = jnp.exp(dec[i : i + 1, sl] * rates[j])
                state[j] = decay * state[j] + flow[i : i + 1, sl] * b_wide
                dest[:, sl] = state[j].astype(bf16)
        return state

    def read_chunk(k, kept, first):
        rows = pl.ds(pl.multiple_of(k * STEP, STEP), STEP)
        du[rows, :] = mm(cbd[rows, :], kept[pl.ds(pl.multiple_of(first, states), span), :])


    def gated_block(b, carry):
        skip_own = lines[3:4, pl.ds(chan, w)]
        at = pl.ds(pl.multiple_of(b * STEP, STEP), STEP)
        for sl in halves:
            y = (du[at, sl] + skip_own[:, sl] * act[at, sl]).astype(bf16).astype(f32)
            g = gate[at, sl]
            sg = 1.0 / (1.0 + jnp.exp(-g))
            gt[at, sl] = (y * (g * sg)).astype(bf16)
            dgl[at, sl] = (dgated[at, sl] * y * (sg * (1.0 + g * (1.0 - sg)))).astype(bf16)
        return carry

    class Sum:
        def __init__(self, n, source):
            self.n, self.source, self.factors = n, source, []
            self.lines = zrows + (extra if n == 2 else 0)
            self.near, self.far, self.twin = [], [], []

        def send_factors(self, part):
            n, at = self.n, slice(part * tl, (part + 1) * tl)
            for sl in tile:
                turn[n, sl, at] = self.source[at, sl].T
            for s in range(1, PLANE):
                refs = lambda s=s: (
                    turn.at[n, block(plane_place[s], quarter), at],
                    fac.at[n, s - 1, :, at],
                )
                self.factors.append(Send(refs, plane_row[s], core))

        def rows(self, where, first, count):
            ref = (gout, ggate, gmix)[self.n]
            first = (core * PLANE + where) * DEPTH * self.lines + first
            return ref.at[pl.ds(pl.multiple_of(first, count), count), :]

        def shard(self, where, z):
            return self.rows(where, z * self.lines, self.lines)

        def partial(self):
            n = self.n
            for copy in self.factors:
                copy.wait_recv()
            kind = 1 if n == 0 else 0
            lefts = [turn[n, block(place, quarter), :]] + [fac[n, s] for s in range(PLANE - 1)]
            for sl in lane_tiles(d, 2 * LANES):
                total = mm(lefts[0], ng[kind, :, sl])
                for s in range(PLANE - 1):
                    total = total + mm(lefts[s + 1], ngh[s, kind, :, sl])
                pw[:, sl] = total
                pb[n, :, sl] = total.astype(bf16)
            pown[n] = pw[block(pz, zrows), :]
            self.depth = [
                Send(
                    lambda s=s: (pb.at[n, block(z_place[s], zrows), :], zr.at[n, s - 1]),
                    z_row[s],
                    core,
                )
                for s in range(1, DEPTH)
            ]

        def near_shard(self, z):
            part = pair_to(lambda: self.shard(place, z))
            self.near.append([Send(part, plane_row[s], core) for s in (1, 2)])

        def total(self):
            for copy in self.depth:
                copy.wait_recv()
            total = pown[self.n]
            for s in range(DEPTH - 1):
                total = total + zr[self.n, s].astype(f32)
            part = self.shard(place, pz)
            part[0:zrows, :] = total.astype(bf16)
            if self.n == 2:
                for copy in small_depth:
                    copy.wait_recv()
                total = sms[block(place * DEPTH + pz, extra), :]
                for s in range(DEPTH - 1):
                    total = total + szr[s].astype(f32)
                part[zrows:, 0:packed] = total.astype(bf16)
                part[zrows:, packed:] = jnp.zeros((extra, d - packed), bf16)
            own = pair_to(lambda: self.shard(place, pz))
            self.along = [Send(own, z_row[s], core) for s in (1, 2)]
            self.beyond = []
            self.near_shard(pz)

        def pass_on(self, s):
            if s < 3:
                self.along[s - 1].wait_recv()
                part = pair_to(lambda: self.shard(place, z_place[s]).at[:, halves[s - 1]])
                self.beyond.append(Send(part, z_row[3 - s], core))
            else:
                for copy in self.beyond:
                    copy.wait_recv()
            self.near_shard(z_place[s])
            if s == DEPTH - 1:
                self.to_twin(place)

        def pass_across(self, s):
            for copy in self.near[s]:
                copy.wait_recv()
            q = 1 + s % 2
            part = pair_to(lambda: self.shard(plane_place[q], z_place[s]))
            self.far.append(Send(part, plane_row[3 - q], core))
            if s == DEPTH - 1:
                for q in (1, 2):
                    self.to_twin(plane_place[q])

        def to_twin(self, where):
            self.twin.append(Send(pair_to(lambda: self.rows(where, 0, DEPTH * self.lines)), row, other))

        def finish(self):
            for copy in self.far:
                copy.wait_recv()
            self.to_twin(plane_place[3])

    sum_out, sum_gate, sum_in = Sum(0, gt), Sum(1, dgl), Sum(2, dil)

    def gated_half(part):
        lax.fori_loop(part * chunks // 2, (part + 1) * chunks // 2, gated_block, 0, unroll=4)
        sum_out.send_factors(part)

    pairs = chunks // 2
    odd[pl.ds(states, span), :] = jnp.zeros((span, w), bf16)

    def scan_pair(m, state):
        read_chunk(jnp.maximum(2 * m - 1, 0), odd, odd_at(jnp.maximum(m - 1, 0)))
        state = scan_chunk(2 * m, state, even, even_at(m))
        read_chunk(2 * m, even, even_at(m))
        state = scan_chunk(2 * m + 1, state, odd, odd_at(m))

        @pl.when(m == pairs // 2 - 1)
        def _():
            read_chunk(chunks // 2 - 1, odd, odd_at(pairs // 2 - 1))
            gated_half(0)
            share_on(0)

        return tuple(state)

    final = lax.fori_loop(0, pairs, scan_pair, zeros)
    read_chunk(chunks - 1, odd, odd_at(pairs - 1))
    gated_half(1)
    share_end(1)

    late = sum(dyf[t - 1 : t, sl] * final[j] for j, sl in enumerate(tile))
    lastc[...] = jnp.broadcast_to(jnp.sum(late, axis=1, keepdims=True), (states, LANES))

    def back_chunk(k, carry, kept, first, before, last, gbuf, qbuf, bbuf, cbuf):
        base = pl.multiple_of(k * STEP, STEP)
        rows = pl.ds(base, STEP)
        c_here, dec, dys, inflow = ct[k], ddec.at[rows], dyf.at[rows], u.at[rows]
        dys_before = dyf.at[pl.ds(pl.multiple_of(jnp.maximum(base - STEP, 0), STEP), STEP)]
        flow, acc = list(carry[0]), list(carry[1])
        for i in reversed(range(STEP)):
            c_wide = jnp.broadcast_to(c_here[:, i : i + 1], (states, LANES))
            at = slice(i * states, (i + 1) * states)
            old = state_block(kept, first, i - 1) if i else state_block(before, last, 0)
            dy_old = dys_before[STEP - 1 : STEP, :] if i == 0 else dys[i - 1 : i, :]
            for_b = for_c = None
            for j, sl in enumerate(tile):
                rate = dec[i : i + 1, sl]
                g = c_wide * dys[i : i + 1, sl] + flow[j]
                gbuf[at, sl] = g.astype(bf16)
                flow[j] = g * jnp.exp(rate * rates[j])
                h_old = old[:, sl].astype(f32)
                q = flow[j] * h_old
                acc[j] = acc[j] + q * rate
                qbuf[at, sl] = (q * rates[j]).astype(bf16)
                term_b, term_c = g * inflow[i : i + 1, sl], h_old * dy_old[:, sl]
                for_b = term_b if for_b is None else for_b + term_b
                for_c = term_c if for_c is None else for_c + term_c
            bbuf[at, :] = for_b.astype(bf16)
            cbuf[at, :] = for_c.astype(bf16)
        return flow, acc

    lane_of = lax.broadcasted_iota(jnp.int32, (states, LANES), 1)
    ones = jnp.ones((LANES, LANES), bf16)

    def back_sums(k, gbuf, qbuf, bbuf, cbuf):
        rows = pl.ds(pl.multiple_of(k * STEP, STEP), STEP)
        for parts, dest in ((bbuf, dbt), (cbuf, dct)):
            summed = mm(parts[...], ones)
            value = jnp.zeros((states, LANES), f32)
            for i in range(STEP):
                value = jnp.where(lane_of == i, summed[i * states : (i + 1) * states, :], value)
            dest[k] = value
        du[rows, :] = mm(bbd[rows, :], gbuf[...])
        sq[rows, :] = mm(ones_diag, qbuf[...])

    even_bufs, odd_bufs = (ga, qa, ba, ca), (gb, qb, bb, cc)

    def out_block(b, carry):
        at = pl.multiple_of(b * STEP, STEP)
        rows = pl.ds(at, STEP)
        total = outp[pl.ds(mine + at, STEP), :] + outr[rows, :]
        out[rows, :] = (ng[2, pl.ds(mine + at, STEP), :].astype(f32) + total).astype(bf16)
        return carry

    first = nproj + rank + states
    line_conv, line_cb, line_dtb, line_skip, line_gain = (
        first,
        first + taps,
        first + taps + 1,
        first + taps + 2,
        first + taps + 3,
    )
    tot_dtb, tot_skip, tot_conv = 0, 1, 2
    dproj_copies = {}

    def read_tot(n):
        return tuple(tot[n, :, sl] for sl in halves)

    def write_tot(n, values):
        for value, sl in zip(values, halves):
            tot[n, :, sl] = value

    def dpre_block(b, carry):
        at = pl.ds(pl.multiple_of(b * STEP, STEP), STEP)
        skip_own = lines[3:4, pl.ds(chan, w)]
        sums, gains = [], []
        for n, sl in enumerate(halves):
            flow, value, dy = du[at, sl], act[at, sl], dyf[at, sl]
            dpre = (sq[at, sl] + flow * value) * sig[at, sl]
            dpl[at, sl] = dpre.astype(bf16)
            s1[at, sl] = flow * s1[at, sl] + skip_own[:, sl] * dy
            both = dy * value
            sums.append(carry[0][n] + dpre[0:8] + dpre[8:16])
            gains.append(carry[1][n] + both[0:8] + both[8:16])
        return tuple(sums), tuple(gains)

    def projection_grads(part):
        at = slice(part * tl, (part + 1) * tl)
        span_of = (part * chunks // 2, (part + 1) * chunks // 2)
        sums, gains = lax.fori_loop(*span_of, dpre_block, (read_tot(tot_dtb), read_tot(tot_skip)), unroll=4)
        write_tot(tot_dtb, sums)
        write_tot(tot_skip, gains)
        for k in range(*span_of):
            cols = slice(k * STEP, (k + 1) * STEP)
            tsc[rank : rank + states, cols] = dbt[k][:, 0:STEP]
            tsc[rank + states : nproj, cols] = dct[k][:, 0:STEP]
        end = lastc[:, 0:1] if part else dct[chunks // 2][:, 0:1]
        shifted = pltpu.roll(tsc[rank + states : nproj, at], tl - 1, 1)
        at_end = lax.broadcasted_iota(jnp.int32, (states, tl), 1) == tl - 1
        tsc[rank + states : nproj, at] = jnp.where(at_end, end, shifted)
        pp2[at, :] = tsc[:, at].T
        pp2[at, 0:rank] = mm(dpl[at, :], dtw[...], NT)
        dproj_copies[part] = Send(lambda: (pp2.at[at, :], pq2.at[at, :]), row, other)

    def dconv_block(b, carry):
        at = pl.multiple_of(b * STEP, STEP)
        view = inner.at[pl.ds(at, STEP + 8)]
        rows = pl.ds(at, STEP)
        masks = mcol[rows, :]
        sums = [list(v) for v in carry]
        for n, sl in enumerate(halves):
            grad = (s1[rows, sl] + sq[rows, sl]) * dsilu[rows, sl]
            dconv[rows, sl] = grad
            terms = [grad, grad * view[8 : 8 + STEP, sl]]
            for j in range(1, taps):
                terms.append(grad * masks[:, j - 1 : j] * view[8 - j : 8 - j + STEP, sl])
            for m, term in enumerate(terms):
                sums[m][n] = sums[m][n] + term[0:8] + term[8:16]
        return tuple(tuple(v) for v in sums)

    def dinner_block(b, carry):
        at = pl.multiple_of(b * STEP, STEP)
        view = dconv.at[pl.ds(at, STEP + 8)]
        masks = mcol.at[pl.ds(at, STEP + 8)]
        cw_own = cw[...]
        for sl in halves:
            total = cw_own[taps - 1 : taps, sl] * view[0:STEP, sl]
            for j in range(1, taps):
                tap = cw_own[taps - 1 - j : taps - j, sl]
                total = total + tap * view[j : j + STEP, sl] * masks[j : j + STEP, j - 1 : j]
            dil[pl.ds(at, STEP), sl] = total.astype(bf16)
        return carry

    def inner_grads(part):
        at = slice(part * tl, (part + 1) * tl)
        span_of = (part * chunks // 2, (part + 1) * chunks // 2)
        dproj_copies[part].wait_recv()
        dproj = pp2[at, :] + pq2[at, :]
        pq2[at, :] = dproj
        dproj_low = dproj[:, 0:nproj].astype(bf16)
        for sl in lane_tiles(w, 2 * LANES):
            sq[at, sl] = mm(dproj_low, xw[:, sl])
        names = range(tot_conv, tot_conv + taps + 1)
        sums = lax.fori_loop(*span_of, dconv_block, tuple(read_tot(n) for n in names), unroll=4)
        for n, values in zip(names, sums):
            write_tot(n, values)
        lax.fori_loop(*span_of, dinner_block, 0, unroll=4)
        sum_in.send_factors(part)

    def late_half():
        back_sums(chunks // 2, *even_bufs)
        projection_grads(1)

    def out_sums():
        for copy in relays[1]:
            copy.wait_recv()
        sum_out.partial()

    def gate_factors():
        sum_gate.send_factors(0)
        sum_gate.send_factors(1)

    def gate_sums():
        for copy in relays[0]:
            copy.wait_recv()
        sum_gate.partial()

    def end_normed():
        share_end(0)

    def inner_late():
        inner_grads(1)

    events = (
        (1, out_sums, gate_factors), (2, end_normed), (3, late_half), (5, gate_sums, sum_out.total), (6, inner_late),
    )

    def back_pair(step, carry):
        m = pairs - 1 - step
        back_sums(jnp.minimum(2 * m + 2, chunks - 1), *even_bufs)
        carry = back_chunk(2 * m + 1, carry, odd, odd_at(m), even, even_at(m) + span - states, *odd_bufs)
        back_sums(2 * m + 1, *odd_bufs)
        flow, acc = back_chunk(2 * m, carry, even, even_at(m), odd, even_at(m), *even_bufs)
        for when, *steps in events:

            @pl.when(step == when * pairs // 8)
            def _():
                for event in steps:
                    event()

        return tuple(flow), tuple(acc)

    carry = lax.fori_loop(0, pairs, back_pair, (zeros, zeros))
    back_sums(0, *even_bufs)
    for j, sl in enumerate(tile):
        sm[nproj + rank : first, sl] = carry[1][j] * rates[j]
    projection_grads(0)
    for sl in lane_tiles(d, 2 * LANES):
        dn[:, sl] = mm(dgl[...], win_g[sl, :], NT)
    inner_grads(0)
    sum_gate.total()
    sum_out.pass_on(1)
    sum_out.pass_on(2)
    for sl in lane_tiles(d, 2 * LANES):
        dn[:, sl] = dn[:, sl] + mm(dil[...], win_i[sl, :], NT)
    dn_copy = Send(lambda: (dn.at[pl.ds(theirs, tl), :], dnr), row, other)
    dproj_turned = pq2[...].T[0:nproj, :].astype(bf16)
    for sl in lane_tiles(w, 2 * LANES):
        sm[0:nproj, sl] = mm(dproj_turned, actl[:, sl])
        sm[nproj : nproj + rank, sl] = mm(rank_turned, dpl[:, sl])

    def put_line(line, n):
        for value, sl in zip(read_tot(n), halves):
            sm[line : line + 1, sl] = jnp.sum(value, axis=0, keepdims=True)

    put_line(line_dtb, tot_dtb)
    put_line(line_skip, tot_skip)
    put_line(line_cb, tot_conv)
    for j in range(taps):
        put_line(line_conv + taps - 1 - j, tot_conv + 1 + j)
    def gain_block(b, carry):
        rows = pl.ds(pl.multiple_of(b * STEP, STEP), STEP)
        values = ng[2, rows, :].astype(f32)
        scale = lax.rsqrt(jnp.mean(values * values, axis=-1, keepdims=True) + EPS)
        both = dn[rows, :] * (values * scale)
        return carry + both[0:8] + both[8:16]

    total = lax.fori_loop(0, chunks, gain_block, jnp.zeros((8, d), f32), unroll=4)
    sm[line_gain : line_gain + 1, :] = jnp.sum(total, axis=0, keepdims=True)
    across_tiles = packed // LANES
    for n in range(sm.shape[0] // 16 * tiles):
        to = slice(n // across_tiles * 16, n // across_tiles * 16 + 16)
        to_lanes = tile[n % across_tiles]
        value = sm[n // tiles * 16 : n // tiles * 16 + 16, tile[n % tiles]]
        smb[to, to_lanes] = value.astype(bf16)
        sms[to, to_lanes] = value
    srows = DEPTH * extra
    over_plane = [
        Send(
            lambda s=s: (smb.at[block(plane_place[s], srows), :], sfac.at[s - 1]),
            plane_row[s],
            core,
        )
        for s in range(1, PLANE)
    ]
    sum_in.partial()
    sum_out.pass_on(3)
    sum_gate.pass_on(1)
    sum_gate.pass_on(2)
    sum_out.pass_across(0)
    for copy in over_plane:
        copy.wait_recv()
    total = sms[block(place, srows), :]
    for s in range(PLANE - 1):
        total = total + sfac[s].astype(f32)
    sms[block(place, srows), :] = total
    spb[...] = total.astype(bf16)
    small_depth = [
        Send(lambda s=s: (spb.at[block(z_place[s], extra), :], szr.at[s - 1]), z_row[s], core)
        for s in range(1, DEPTH)
    ]
    sum_out.pass_across(1)
    sum_out.pass_across(2)
    sum_out.pass_across(3)
    sum_gate.pass_on(3)

    sum_in.total()
    for sl in lane_tiles(d, 2 * LANES):
        outp[:, sl] = mm(gt[...], wo[:, sl])
    out_copy = Send(lambda: (outp.at[pl.ds(theirs, tl), :], outr), row, other)

    def norm_back(b, carry):
        at = pl.multiple_of(b * STEP, STEP)
        rows = pl.ds(at, STEP)
        values = ng[2, pl.ds(mine + at, STEP), :].astype(f32)
        scale = lax.rsqrt(jnp.mean(values * values, axis=-1, keepdims=True) + EPS)
        unit_rows = values * scale
        inside = (dn[pl.ds(mine + at, STEP), :] + dnr[rows, :]) * lines[0:1, 0:d]
        mean = jnp.mean(inside * unit_rows, axis=-1, keepdims=True)
        given = ng[1, pl.ds(mine + at, STEP), :].astype(f32)
        gtok[rows, :] = (given + scale * (inside - unit_rows * mean)).astype(bf16)
        return carry

    dn_copy.wait_recv()
    lax.fori_loop(0, tl // STEP, norm_back, 0, unroll=4)
    out_copy.wait_recv()
    lax.fori_loop(0, tl // STEP, out_block, 0, unroll=4)

    sum_gate.pass_across(0)
    sum_gate.pass_across(1)
    sum_out.finish()
    sum_in.pass_on(1)
    sum_in.pass_on(2)
    sum_gate.pass_across(2)
    sum_gate.pass_across(3)
    sum_in.pass_on(3)
    sum_in.pass_across(0)
    sum_gate.finish()
    for s in (1, 2, 3):
        sum_in.pass_across(s)
    sum_in.finish()
    for copy in sum_out.twin + sum_gate.twin + sum_in.twin:
        copy.wait_recv()
    for copy in pending:
        copy.wait_send()


def wide_kernel(packed, output, grad_tokens, gout, ggate, gmix, *refs):
    out_o, out_t, gin_f, gout_f, *rest = refs
    *rest, wide_in, wide_out, value, sems = rest
    finals, rows = rest[: len(rest) // 2], rest[len(rest) // 2 :]
    steps = wide_in.shape[0]
    cols, lines = wide_in.shape[2], wide_out.shape[1]
    copies = []

    def put(src, dst, *sem):
        copies.append(pltpu.make_async_copy(src, dst, sems.at[sem]))
        copies[-1].start()

    put(output, out_o, 2, 0)
    put(grad_tokens, out_t, 2, 1)
    e, d = ggate.shape
    blocks = e // cols
    shards = 2 * TEAM
    zrows, stride = e // shards, gmix.shape[0] // shards
    per = shards // blocks

    def inner_rows(i):
        parts = [gmix[n * stride : n * stride + zrows, :] for n in range(i * per, (i + 1) * per)]
        return jnp.concatenate(parts, axis=0)

    for i in range(steps):
        at = slice(i * lines, (i + 1) * lines)
        wide_out[i] = gout[at, :].astype(f32)
        put(wide_out.at[i], gout_f.at[at, :], 1, i)
        gate_rows = slice((i - blocks) * cols, (i - blocks + 1) * cols)
        turned = (inner_rows(i) if i < blocks else ggate[gate_rows, :]).T
        wide_in[i] = turned.astype(f32)
        put(wide_in.at[i], gin_f.at[:, i * cols : (i + 1) * cols], 0, i)

    matrices = [ref for ref in rows if len(ref.shape) == 2]
    vectors = [ref for ref in rows if len(ref.shape) == 1]
    gain = 0.0
    tiles, across = d // LANES, packed // LANES
    for core in range(2):
        for n in range(value.shape[0] // 16 * tiles):
            first = (core * TEAM + n // across) * stride + zrows
            at_row, at_lane, lane = n // tiles * 16, n % tiles * LANES, n % across * LANES
            value[at_row : at_row + 16, at_lane : at_lane + LANES] = gmix[
                first : first + 16, lane : lane + LANES
            ].astype(f32)
        at_lanes = slice(core * d, (core + 1) * d)
        at = 0
        for ref in matrices:
            ref[:, at_lanes] = value[at : at + ref.shape[0], :]
            at += ref.shape[0]
        for ref in vectors[:-1]:
            ref[at_lanes] = value[at : at + 1, :].reshape(d)
            at += 1
        gain = gain + value[at : at + 1, :]
    vectors[-1][...] = gain.reshape(d)
    for n, (src, dst) in enumerate(zip(rows, finals)):
        put(src, dst, 3, n)
    for copy in copies:
        copy.wait()


def local(
    tokens, marks, norm_gain, in_weight, conv_weight, conv_bias, x_weight, dt_weight,
    dt_bias, a_log, skip, out_weight, cotangent,
):
    tl, d = tokens.shape[1:]
    e = out_weight.shape[0]
    w = e // lax.axis_size("seq")
    t = tl * lax.axis_size("seq")
    states, rank, nproj, taps = a_log.shape[0], dt_weight.shape[0], x_weight.shape[0], conv_weight.shape[0]
    chunks, span = t // STEP, STEP * states
    quarter = w // PLANE
    zrows = quarter // DEPTH
    lines = -(-(nproj + rank + states + taps + 4) // 16) * 16
    packed = -(-(lines // 16) * (w // LANES) // TEAM) * LANES
    small = 16 * TEAM
    srows = zrows + 16
    vmem = pl.BlockSpec(memory_space=pltpu.VMEM)
    anywhere = pl.BlockSpec(memory_space=pl.ANY)
    wide = pltpu.VMEM((t, w), f32)
    low = pltpu.VMEM((t, w), bf16)
    one = pltpu.VMEM((t, LANES), f32)
    scratch = [
        pltpu.VMEM((d, w), bf16), pltpu.VMEM((d, w), bf16), pltpu.VMEM((w, d), bf16),
        pltpu.VMEM((d,), f32), pltpu.VMEM((taps, w), f32), pltpu.VMEM((e,), f32),
        pltpu.VMEM((nproj, w), bf16), pltpu.VMEM((rank, w), bf16), pltpu.VMEM((e,), f32),
        pltpu.VMEM((states, w), f32), pltpu.VMEM((e,), f32), pltpu.VMEM((8, tl), jnp.int32),
        pltpu.VMEM((3, t, d), bf16), pltpu.VMEM((PLANE - 1, 2, t, d), bf16),
        pltpu.VMEM((8, t), f32), pltpu.VMEM((t + 8, LANES), f32), pltpu.VMEM((8, e), f32),
        pltpu.VMEM((t + 8, w), f32), wide, wide, wide, wide, low, wide, wide, wide, wide, wide, wide, wide,
        one, one, one, one, pltpu.VMEM((LANES, t), f32),
        pltpu.VMEM((t * states // 2, w), bf16), pltpu.VMEM((t * states // 2 + states, w), bf16),
        pltpu.VMEM((chunks, states, LANES), f32), pltpu.VMEM((chunks, states, LANES), f32),
        pltpu.VMEM((t, span), bf16), pltpu.VMEM((t, span), bf16),
        *[pltpu.VMEM((span, w), bf16)] * 4, *[pltpu.VMEM((span, LANES), bf16)] * 4,
        *[pltpu.VMEM((chunks, states, LANES), f32)] * 2,
        pltpu.VMEM((states, LANES), f32), pltpu.VMEM((taps + 3, 8, w), f32),
        low, low, low, low, pltpu.VMEM((3, w, t), bf16), pltpu.VMEM((t + 8, w), f32),
        pltpu.VMEM((t, d), f32), pltpu.VMEM((tl, d), f32),
        pltpu.VMEM((t, d), f32), pltpu.VMEM((tl, d), f32),
        pltpu.VMEM((3, PLANE - 1, quarter, t), bf16), pltpu.VMEM((quarter, d), f32),
        pltpu.VMEM((3, zrows, d), f32), pltpu.VMEM((3, quarter, d), bf16),
        pltpu.VMEM((3, DEPTH - 1, zrows, d), bf16),
        pltpu.VMEM((lines, w), f32), pltpu.VMEM((small, packed), bf16), pltpu.VMEM((small, packed), f32),
        pltpu.VMEM((PLANE - 1, small // PLANE, packed), bf16), pltpu.VMEM((small // PLANE, packed), bf16),
        pltpu.VMEM((DEPTH - 1, 16, packed), bf16),
        pltpu.SemaphoreType.DMA((16,)),
        pltpu.SemaphoreType.DMA((128,)), pltpu.SemaphoreType.DMA((128,)),
    ]
    output, grad_tokens, gout, ggate, gmix = pl.pallas_call(
        body_kernel,
        out_shape=[
            pltpu.VMEM((tl, d), bf16),
            pltpu.VMEM((tl, d), bf16),
            pltpu.VMEM((e, d), bf16),
            pltpu.VMEM((e, d), bf16),
            pltpu.VMEM((2 * TEAM * srows, d), bf16),
        ],
        in_specs=[anywhere] * 13,
        out_specs=[vmem] * 5,
        scratch_shapes=scratch,
        compiler_params=pltpu.CompilerParams(
            collective_id=0, has_side_effects=True, vmem_limit_bytes=56 * 2**20
        ),
        name="block",
    )(
        tokens.reshape(tl, d), marks.reshape(1, tl), norm_gain, in_weight, conv_weight,
        conv_bias, x_weight, dt_weight, dt_bias, a_log, skip, out_weight, cotangent.reshape(tl, d),
    )

    steps = 8
    shapes = [(nproj, e), (rank, e), (states, e), (taps, e), (e,), (e,), (e,), (d,)]
    wide_shapes = [jax.ShapeDtypeStruct(s, f32) for s in [(d, 2 * e), (e, d)] + shapes]
    output, grad_tokens, *grads = pl.pallas_call(
        functools.partial(wide_kernel, packed),
        out_shape=[jax.ShapeDtypeStruct((tl, d), bf16)] * 2 + wide_shapes,
        in_specs=[vmem] * 5,
        out_specs=[anywhere] * (4 + len(shapes)),
        scratch_shapes=[pltpu.VMEM(s, f32) for s in shapes]
        + [
            pltpu.VMEM((steps, d, 2 * e // steps), f32),
            pltpu.VMEM((steps, e // steps, d), f32),
            pltpu.VMEM((lines, w), f32),
            pltpu.SemaphoreType.DMA((4, steps)),
        ],
        compiler_params=pltpu.CompilerParams(vmem_limit_bytes=40 * 2**20),
        name="widen",
    )(output, grad_tokens, gout, ggate, gmix)
    rows = lax.axis_size("rows")
    if rows > TEAM:
        grads = [v * (1.0 / TEAM) for v in lax.psum(grads, "rows")]
    grad_in, grad_out, grad_x, grad_dt, grad_log, grad_conv, g_cb, g_dtb, g_skip, g_gain = grads
    return (
        output[None], grad_tokens[None], g_gain, grad_in, grad_conv, g_cb, grad_x, grad_dt, g_dtb, grad_log,
        g_skip, grad_out,
    )


def solution(mesh):
    split = P("rows", "seq", None)
    whole = P()
    in_specs = (split, P("rows", "seq")) + (whole,) * 10 + (split,)
    out_specs = (split, split) + (whole,) * 10
    return jax.shard_map(local, mesh=mesh, in_specs=in_specs, out_specs=out_specs, check_vma=False)
```

```python
import jax
import jax.numpy as jnp
from jax import lax
from jax.experimental import pallas as pl
from jax.experimental.pallas import tpu as pltpu
from jax.sharding import PartitionSpec as P

f32 = jnp.float32
bf16 = jnp.bfloat16
EPS = 1e-05
LANES = 128
STEP = 16
PLANE = 4
DEPTH = 4
TEAM = PLANE * DEPTH
MESH = pl.DeviceIdType.MESH
NN = (((1,), (0,)), ((), ()))
NT = (((1,), (1,)), ((), ()))


def mm(a, b, dims=NN):
    return lax.dot_general(a, b, dims, preferred_element_type=f32)


def lane_tiles(width, size):
    return [slice(j, j + size) for j in range(0, width, size)]


def body_kernel(
    tok, marks, gain_in, win, cw_in, cb_in, xw_in, dtw_in, dtb_in, alog_in, skip_in, wout, cot,
    out, gtok, gout, ggate, ginner, small,
    win_i, win_g, wo, gain, cw, cb, xw, dtw, dtb, alog, skip, mkraw, ng, ngh, mk, mcol, lines,
    inner, gate, dgated, act, dsilu, actl, ddec, u, sig, dyf, du, s1, sq,
    pp, pq, pp2, pq2, tsc, even, odd, bt, ct, cbd, bbd, ga, gb, qa, qb, ba, bb, ca, cc, dbt, dct, lastc, tot,
    gt, dgl, dpl, dil, turn, dconv, dn, dnr, outp, outr,
    fac, pw, pown, pb, zr, sm, smb, sms, sfac, spb, szr,
    ls, ss, rs,
):
    row, core = lax.axis_index("rows"), lax.axis_index("seq")
    other = 1 - core
    team = row - row % TEAM
    px, py, pz = row % 2, (row // 2) % 2, (row // PLANE) % DEPTH
    tl, d = out.shape
    t = 2 * tl
    w = wo.shape[0]
    states = alog.shape[0]
    rank = dtw.shape[0]
    nproj = xw.shape[0]
    half = w // 2
    quarter = w // PLANE
    zrows = quarter // DEPTH
    extra, packed = smb.shape[0] // TEAM, smb.shape[1]
    place = row % PLANE
    chunks = t // STEP
    tiles = w // LANES
    mine = pl.multiple_of(core * tl, tl)
    theirs = pl.multiple_of(other * tl, tl)
    chan = pl.multiple_of(core * w, w)
    halves = lane_tiles(w, half)
    pending = []

    def flip(low, high, s):
        a, b = s % 2, s // 2
        return (high + b - 2 * b * high) * 2 + low + a - 2 * a * low

    plane_place = [flip(px, py, s) for s in range(PLANE)]
    plane_row = [team + pz * PLANE + plane_place[s] for s in range(PLANE)]
    z_place = [flip(pz % 2, pz // 2, s) for s in range(DEPTH)]
    z_row = [team + z_place[s] * PLANE + place for s in range(DEPTH)]
    ids = iter(range(10_000))

    class Send:
        def __init__(self, refs, to_row, to_core):
            self.refs, self.to, self.k = refs, (to_row, to_core), next(ids)
            self.copy().start()
            pending.append(self)

        def copy(self):
            src, dst = self.refs()
            return pltpu.make_async_remote_copy(
                src_ref=src,
                dst_ref=dst,
                send_sem=ss.at[self.k],
                recv_sem=rs.at[self.k],
                device_id=self.to,
                device_id_type=MESH,
            )

        def wait_recv(self):
            self.copy().wait_recv()

        def wait_send(self):
            self.copy().wait_send()

    def block(index, size):
        return pl.ds(pl.multiple_of(index * size, size), size)

    own = pl.ds(chan, w)
    sources = [
        (tok, ng.at[2, pl.ds(mine, tl), :]),
        (marks, mkraw.at[0:1]),
        (gain_in, gain),
        (win.at[:, own], win_i),
        (cw_in.at[:, own], cw),
        (cb_in, cb),
        (cot, ng.at[1, pl.ds(mine, tl), :]),
        (xw_in.at[:, own], xw),
        (win.at[:, pl.ds(pl.multiple_of(2 * w + core * w, w), w)], win_g),
        (wout.at[own, :], wo),
        (dtw_in.at[:, own], dtw),
        (dtb_in, dtb),
        (skip_in, skip),
        (alog_in.at[:, own], alog),
    ]
    loads = [pltpu.make_async_copy(src, dst, ls.at[n]) for n, (src, dst) in enumerate(sources)]
    for copy in loads:
        copy.start()

    barrier = pltpu.get_barrier_semaphore()
    partners = [(row, other)]
    partners += [(plane_row[s], core) for s in range(1, PLANE)]
    partners += [(z_row[s], core) for s in range(1, DEPTH)]
    for partner in partners:
        pl.semaphore_signal(barrier, inc=1, device_id=partner, device_id_type=MESH)
    pl.semaphore_wait(barrier, len(partners))

    def pair_to(ref):
        return lambda: (ref(), ref())

    def own_rows(kind):
        return ng.at[kind, pl.ds(mine, tl), :]

    def slot(s, kind, first=0, count=tl):
        return ngh.at[s - 1, kind, pl.ds(pl.multiple_of(mine + first, count), count), :]

    twin = [
        Send(lambda n=n, ref=ref: (ref, ng.at[n, pl.ds(mine, tl), :]), row, other)
        for n, ref in ((2, tok), (1, cot))
    ]
    twin.append(Send(lambda: (marks, mkraw.at[1:2]), row, other))
    early, across, relays = {}, {}, {0: [], 1: []}
    piece = tl // 2

    def share(kind):
        early[kind] = [
            Send(lambda s=s: (cot if kind else own_rows(kind), slot(s, kind)), plane_row[s], core)
            for s in (1, 2)
        ]

    def share_on(kind):
        across[kind] = []
        for s in (1, 2):
            early[kind][s - 1].wait_recv()
            first = (s - 1) * piece
            refs = lambda s=s, first=first: (slot(s, kind, first, piece), slot(3, kind, first, piece))
            across[kind].append(Send(refs, plane_row[3 - s], core))
            relays[kind].append(Send(pair_to(lambda s=s: slot(s, kind)), row, other))

    def share_end(kind):
        for s in (1, 2):
            across[kind][s - 1].wait_recv()
            refs = pair_to(lambda first=(s - 1) * piece: slot(3, kind, first, piece))
            relays[kind].append(Send(refs, row, other))

    share(1)

    for copy in loads[:3]:
        copy.wait()
    count = gain.shape[0]
    lines[0:1, 0:count] = gain[...].reshape(1, count)
    unit = 2 * STEP

    def norm_rows(first):
        gain_row = lines[0:1, 0:d]

        def norm_block(b, carry):
            at = pl.ds(pl.multiple_of(first + b * unit, unit), unit)
            rows = ng[2, at, :].astype(f32)
            scale = lax.rsqrt(jnp.mean(rows * rows, axis=-1, keepdims=True) + EPS)
            ng[0, at, :] = (rows * scale * gain_row).astype(bf16)
            return carry

        lax.fori_loop(0, tl // unit, norm_block, 0, unroll=4)

    norm_rows(mine)
    share(0)

    inner[0:8, :] = jnp.zeros((8, w), f32)
    dconv[t : t + 8, :] = jnp.zeros((8, w), f32)
    mcol[t : t + 8, :] = jnp.zeros((8, LANES), f32)
    odd[0:states, :] = jnp.zeros((states, w), bf16)
    tsc[...] = jnp.zeros(tsc.shape, f32)
    tot[...] = jnp.zeros(tot.shape, f32)
    smb[...] = jnp.zeros(smb.shape, bf16)
    sms[...] = jnp.zeros(sms.shape, f32)
    for ref in (ga, qa, ba, ca):
        ref[...] = jnp.zeros(ref.shape, bf16)
    sm[...] = jnp.zeros(sm.shape, f32)

    for copy in twin:
        copy.wait_recv()
    norm_rows(theirs)
    own_marks, twin_marks = mkraw[0:1, :].astype(f32), mkraw[1:2, :].astype(f32)
    mk[:, pl.ds(mine, tl)] = jnp.broadcast_to(own_marks, (8, tl))
    mk[:, pl.ds(theirs, tl)] = jnp.broadcast_to(twin_marks, (8, tl))
    for copy in loads[3:7]:
        copy.wait()

    for sl in lane_tiles(w, 2 * LANES):
        inner[8 : 8 + t, sl] = mm(ng[0], win_i[:, sl]).astype(bf16).astype(f32)

    lane = lax.broadcasted_iota(jnp.int32, (8, t), 1)
    mark = mk[...]
    keep = jnp.where(lane == 0, 0.0, 1.0 - mark)
    mask2 = keep * pltpu.roll(keep, 1, 1)
    mask3 = mask2 * pltpu.roll(keep, 2, 1)
    line = lax.broadcasted_iota(jnp.int32, (LANES, t), 0)

    def spread(v):
        return jnp.broadcast_to(v[0:1, :], (LANES, t))

    stacked = jnp.where(line == 0, spread(keep), 0.0)
    stacked = jnp.where(line == 1, spread(mask2), stacked)
    stacked = jnp.where(line == 2, spread(mask3), stacked)
    stacked = jnp.where(line == 3, spread(mark), stacked)
    mcol[0:t, :] = stacked.T

    for copy in loads[7:]:
        copy.wait()
    for n, ref in enumerate((gain, cb, dtb, skip)):
        count = ref.shape[0]
        lines[n : n + 1, 0:count] = ref[...].reshape(1, count)
    cw_own = cw[...]
    cb_own = lines[1:2, pl.ds(chan, w)]
    taps = cw.shape[0]

    def conv_block(b, carry):
        at = pl.multiple_of(b * STEP, STEP)
        view = inner.at[pl.ds(at, STEP + 8)]
        masks = mcol[pl.ds(at, STEP), :]
        for sl in halves:
            total = cb_own[:, sl] + cw_own[taps - 1 : taps, sl] * view[8 : 8 + STEP, sl]
            for j in range(1, taps):
                tap = cw_own[taps - 1 - j : taps - j, sl]
                total = total + tap * view[8 - j : 8 - j + STEP, sl] * masks[:, j - 1 : j]
            sg = 1.0 / (1.0 + jnp.exp(-total))
            value = total * sg
            act[pl.ds(at, STEP), sl] = value
            actl[pl.ds(at, STEP), sl] = value.astype(bf16)
            dsilu[pl.ds(at, STEP), sl] = sg * (1.0 + total * (1.0 - sg))
        return carry

    lax.fori_loop(0, chunks, conv_block, 0, unroll=4)
    xw_own = xw[...]
    pp[:, 0:nproj] = mm(actl[...], xw_own, NT)
    proj_copy = Send(lambda: (pp, pq), row, other)

    for sl in lane_tiles(w, 2 * LANES):
        gate[:, sl] = mm(ng[0], win_g[:, sl])
        dgated[:, sl] = mm(ng[1], wo[sl, :], NT)

    def dy_block(b, carry):
        at = pl.ds(pl.multiple_of(b * STEP, STEP), STEP)
        for sl in halves:
            g = gate[at, sl]
            low = (dgated[at, sl] * (g / (1.0 + jnp.exp(-g)))).astype(bf16)
            dyf[at, sl] = low.astype(f32)
        return carry

    lax.fori_loop(0, chunks, dy_block, 0, unroll=4)

    share_on(1)

    proj_copy.wait_recv()
    proj = pp[...] + pq[...]
    turned = proj.T
    for k in range(chunks):
        cols = slice(k * STEP, (k + 1) * STEP)
        bt[k, :, 0:STEP] = turned[rank : rank + states, cols]
        ct[k, :, 0:STEP] = turned[rank + states : rank + 2 * states, cols]
    rank_low = proj[:, 0:rank].astype(bf16)
    rank_turned = turned[0:rank, :].astype(bf16)
    dtw_own = dtw[...]
    dtb_own = lines[2:3, pl.ds(chan, w)]
    for sl in lane_tiles(w, 2 * LANES):
        sig[:, sl] = mm(rank_low, dtw_own[:, sl]) + dtb_own[:, sl]

    def delta_block(b, carry):
        at = pl.ds(pl.multiple_of(b * STEP, STEP), STEP)
        marked = mcol[at, :][:, 3:4] > 0.5
        for sl in halves:
            pre = sig[at, sl]
            e = jnp.exp(-jnp.abs(pre))
            one = 1.0 + e
            log1p = jnp.where(one == 1.0, e, jnp.log(one) * (e / (one - 1.0)))
            delta = jnp.maximum(pre, 0.0) + log1p
            sig[at, sl] = jnp.where(pre >= 0.0, 1.0, e) / one
            inflow = delta * act[at, sl]
            u[at, sl] = inflow
            s1[at, sl] = delta
            ddec[at, sl] = jnp.where(marked, 1e30, delta)
        return carry

    lax.fori_loop(0, chunks, delta_block, 0, unroll=4)

    span = STEP * states
    pick = (
        lax.broadcasted_iota(jnp.int32, (states, span), 0)
        == lax.broadcasted_iota(jnp.int32, (states, span), 1) % states
    ).astype(bf16)
    diag = (
        lax.broadcasted_iota(jnp.int32, (t, span), 0) % STEP
        == lax.broadcasted_iota(jnp.int32, (t, span), 1) // states
    )
    ones_diag = diag[0:STEP].astype(bf16)
    b_low = proj[:, rank : rank + states].astype(bf16)
    c_low = proj[:, rank + states : rank + 2 * states].astype(bf16)
    bbd[...] = jnp.where(diag, mm(b_low, pick), 0.0).astype(bf16)
    cbd[...] = jnp.where(diag, mm(c_low, pick), 0.0).astype(bf16)

    rates = [-jnp.exp(alog[:, j * LANES : (j + 1) * LANES]) for j in range(tiles)]
    zeros = tuple(jnp.zeros((states, LANES), f32) for _ in range(tiles))
    tile = [slice(j * LANES, (j + 1) * LANES) for j in range(tiles)]

    def even_at(m):
        return pl.multiple_of(m * span, span)

    def odd_at(m):
        return pl.multiple_of(states + m * span, states)

    def state_block(ref, first, i):
        return ref.at[pl.ds(pl.multiple_of(first + i * states, states), states)]

    def scan_chunk(k, state, kept, first):
        rows = pl.ds(pl.multiple_of(k * STEP, STEP), STEP)
        b_here, dec, flow = bt[k], ddec.at[rows], u.at[rows]
        state = list(state)
        for i in range(STEP):
            b_wide = jnp.broadcast_to(b_here[:, i : i + 1], (states, LANES))
            dest = state_block(kept, first, i)
            for j, sl in enumerate(tile):
                decay = jnp.exp(dec[i : i + 1, sl] * rates[j])
                state[j] = decay * state[j] + flow[i : i + 1, sl] * b_wide
                dest[:, sl] = state[j].astype(bf16)
        return state

    def read_chunk(k, kept, first):
        rows = pl.ds(pl.multiple_of(k * STEP, STEP), STEP)
        du[rows, :] = mm(cbd[rows, :], kept[pl.ds(pl.multiple_of(first, states), span), :])


    def gated_block(b, carry):
        skip_own = lines[3:4, pl.ds(chan, w)]
        at = pl.ds(pl.multiple_of(b * STEP, STEP), STEP)
        for sl in halves:
            y = (du[at, sl] + skip_own[:, sl] * act[at, sl]).astype(bf16).astype(f32)
            g = gate[at, sl]
            sg = 1.0 / (1.0 + jnp.exp(-g))
            gt[at, sl] = (y * (g * sg)).astype(bf16)
            dgl[at, sl] = (dgated[at, sl] * y * (sg * (1.0 + g * (1.0 - sg)))).astype(bf16)
        return carry

    class Sum:
        def __init__(self, n, source):
            self.n, self.source, self.factors = n, source, []
            self.near, self.far, self.twin = [], [], []

        def send_factors(self, part):
            n, at = self.n, slice(part * tl, (part + 1) * tl)
            for sl in tile:
                turn[n, sl, at] = self.source[at, sl].T
            for s in range(1, PLANE):
                refs = lambda s=s: (
                    turn.at[n, block(plane_place[s], quarter), at],
                    fac.at[n, s - 1, :, at],
                )
                self.factors.append(Send(refs, plane_row[s], core))

        def rows(self, where, first, count):
            ref = (gout, ggate, ginner)[self.n]
            first = chan + where * quarter + first
            return ref.at[pl.ds(pl.multiple_of(first, count), count), :]

        def shard(self, where, z):
            return self.rows(where, z * zrows, zrows)

        def partial(self):
            n = self.n
            for copy in self.factors:
                copy.wait_recv()
            kind = 1 if n == 0 else 0
            lefts = [turn[n, block(place, quarter), :]] + [fac[n, s] for s in range(PLANE - 1)]
            for sl in lane_tiles(d, 2 * LANES):
                total = mm(lefts[0], ng[kind, :, sl])
                for s in range(PLANE - 1):
                    total = total + mm(lefts[s + 1], ngh[s, kind, :, sl])
                pw[:, sl] = total
                pb[n, :, sl] = total.astype(bf16)
            pown[n] = pw[block(pz, zrows), :]
            self.depth = [
                Send(
                    lambda s=s: (pb.at[n, block(z_place[s], zrows), :], zr.at[n, s - 1]),
                    z_row[s],
                    core,
                )
                for s in range(1, DEPTH)
            ]

        def near_shard(self, z):
            part = pair_to(lambda: self.shard(place, z))
            self.near.append([Send(part, plane_row[s], core) for s in (1, 2)])

        def total(self):
            for copy in self.depth:
                copy.wait_recv()
            total = pown[self.n]
            for s in range(DEPTH - 1):
                total = total + zr[self.n, s].astype(f32)
            part = self.shard(place, pz)
            part[...] = total.astype(bf16)
            own = pair_to(lambda: self.shard(place, pz))
            self.along = [Send(own, z_row[s], core) for s in (1, 2)]
            self.beyond = []
            self.near_shard(pz)

        def pass_on(self, s):
            if s < 3:
                self.along[s - 1].wait_recv()
                part = pair_to(lambda: self.shard(place, z_place[s]).at[:, halves[s - 1]])
                self.beyond.append(Send(part, z_row[3 - s], core))
            else:
                for copy in self.beyond:
                    copy.wait_recv()
            self.near_shard(z_place[s])
            if s == DEPTH - 1:
                self.to_twin(place)

        def pass_across(self, s):
            for copy in self.near[s]:
                copy.wait_recv()
            far = []
            for q in (1, 2):
                part = pair_to(lambda q=q: self.shard(plane_place[q], z_place[s]).at[:, halves[q - 1]])
                far.append(Send(part, plane_row[3 - q], core))
            self.far.append(far)
            if s == DEPTH - 1:
                for q in (1, 2):
                    self.to_twin(plane_place[q])

        def to_twin(self, where):
            self.twin.append(Send(pair_to(lambda: self.rows(where, 0, quarter)), row, other))

        def finish(self):
            for s, far in enumerate(self.far):
                for copy in far:
                    copy.wait_recv()
                part = pair_to(lambda s=s: self.shard(plane_place[3], z_place[s]))
                self.twin.append(Send(part, row, other))

    sum_out, sum_gate, sum_in = Sum(0, gt), Sum(1, dgl), Sum(2, dil)

    def gated_half(part):
        lax.fori_loop(part * chunks // 2, (part + 1) * chunks // 2, gated_block, 0, unroll=4)
        sum_out.send_factors(part)

    pairs = chunks // 2
    odd[pl.ds(states, span), :] = jnp.zeros((span, w), bf16)

    def scan_pair(m, state):
        read_chunk(jnp.maximum(2 * m - 1, 0), odd, odd_at(jnp.maximum(m - 1, 0)))
        state = scan_chunk(2 * m, state, even, even_at(m))
        read_chunk(2 * m, even, even_at(m))
        state = scan_chunk(2 * m + 1, state, odd, odd_at(m))

        @pl.when(m == pairs // 2 - 1)
        def _():
            read_chunk(chunks // 2 - 1, odd, odd_at(pairs // 2 - 1))
            gated_half(0)
            share_on(0)

        return tuple(state)

    final = lax.fori_loop(0, pairs, scan_pair, zeros)
    read_chunk(chunks - 1, odd, odd_at(pairs - 1))
    gated_half(1)
    share_end(1)

    late = sum(dyf[t - 1 : t, sl] * final[j] for j, sl in enumerate(tile))
    lastc[...] = jnp.broadcast_to(jnp.sum(late, axis=1, keepdims=True), (states, LANES))

    def back_chunk(k, carry, kept, first, before, last, gbuf, qbuf, bbuf, cbuf):
        base = pl.multiple_of(k * STEP, STEP)
        rows = pl.ds(base, STEP)
        c_here, dec, dys, inflow = ct[k], ddec.at[rows], dyf.at[rows], u.at[rows]
        dys_before = dyf.at[pl.ds(pl.multiple_of(jnp.maximum(base - STEP, 0), STEP), STEP)]
        flow, acc = list(carry[0]), list(carry[1])
        for i in reversed(range(STEP)):
            c_wide = jnp.broadcast_to(c_here[:, i : i + 1], (states, LANES))
            at = slice(i * states, (i + 1) * states)
            old = state_block(kept, first, i - 1) if i else state_block(before, last, 0)
            dy_old = dys_before[STEP - 1 : STEP, :] if i == 0 else dys[i - 1 : i, :]
            for_b = for_c = None
            for j, sl in enumerate(tile):
                rate = dec[i : i + 1, sl]
                g = c_wide * dys[i : i + 1, sl] + flow[j]
                gbuf[at, sl] = g.astype(bf16)
                flow[j] = g * jnp.exp(rate * rates[j])
                h_old = old[:, sl].astype(f32)
                q = flow[j] * h_old
                acc[j] = acc[j] + q * rate
                qbuf[at, sl] = (q * rates[j]).astype(bf16)
                term_b, term_c = g * inflow[i : i + 1, sl], h_old * dy_old[:, sl]
                for_b = term_b if for_b is None else for_b + term_b
                for_c = term_c if for_c is None else for_c + term_c
            bbuf[at, :] = for_b.astype(bf16)
            cbuf[at, :] = for_c.astype(bf16)
        return flow, acc

    lane_of = lax.broadcasted_iota(jnp.int32, (states, LANES), 1)
    ones = jnp.ones((LANES, LANES), bf16)

    def back_sums(k, gbuf, qbuf, bbuf, cbuf):
        rows = pl.ds(pl.multiple_of(k * STEP, STEP), STEP)
        for parts, dest in ((bbuf, dbt), (cbuf, dct)):
            summed = mm(parts[...], ones)
            value = jnp.zeros((states, LANES), f32)
            for i in range(STEP):
                value = jnp.where(lane_of == i, summed[i * states : (i + 1) * states, :], value)
            dest[k] = value
        du[rows, :] = mm(bbd[rows, :], gbuf[...])
        sq[rows, :] = mm(ones_diag, qbuf[...])

    even_bufs, odd_bufs = (ga, qa, ba, ca), (gb, qb, bb, cc)

    def out_block(b, carry):
        at = pl.multiple_of(b * STEP, STEP)
        rows = pl.ds(at, STEP)
        total = outp[pl.ds(mine + at, STEP), :] + outr[rows, :]
        out[rows, :] = (ng[2, pl.ds(mine + at, STEP), :].astype(f32) + total).astype(bf16)
        return carry

    first = nproj + rank + states
    line_conv, line_cb, line_dtb, line_skip, line_gain = (
        first,
        first + taps,
        first + taps + 1,
        first + taps + 2,
        first + taps + 3,
    )
    tot_dtb, tot_skip, tot_conv = 0, 1, 2
    dproj_copies = {}

    def read_tot(n):
        return tuple(tot[n, :, sl] for sl in halves)

    def write_tot(n, values):
        for value, sl in zip(values, halves):
            tot[n, :, sl] = value

    def dpre_block(b, carry):
        at = pl.ds(pl.multiple_of(b * STEP, STEP), STEP)
        skip_own = lines[3:4, pl.ds(chan, w)]
        sums, gains = [], []
        for n, sl in enumerate(halves):
            flow, value, dy = du[at, sl], act[at, sl], dyf[at, sl]
            dpre = (sq[at, sl] + flow * value) * sig[at, sl]
            dpl[at, sl] = dpre.astype(bf16)
            s1[at, sl] = flow * s1[at, sl] + skip_own[:, sl] * dy
            both = dy * value
            sums.append(carry[0][n] + dpre[0:8] + dpre[8:16])
            gains.append(carry[1][n] + both[0:8] + both[8:16])
        return tuple(sums), tuple(gains)

    def projection_grads(part):
        at = slice(part * tl, (part + 1) * tl)
        span_of = (part * chunks // 2, (part + 1) * chunks // 2)
        sums, gains = lax.fori_loop(*span_of, dpre_block, (read_tot(tot_dtb), read_tot(tot_skip)), unroll=4)
        write_tot(tot_dtb, sums)
        write_tot(tot_skip, gains)
        for k in range(*span_of):
            cols = slice(k * STEP, (k + 1) * STEP)
            tsc[rank : rank + states, cols] = dbt[k][:, 0:STEP]
            tsc[rank + states : nproj, cols] = dct[k][:, 0:STEP]
        end = lastc[:, 0:1] if part else dct[chunks // 2][:, 0:1]
        shifted = pltpu.roll(tsc[rank + states : nproj, at], tl - 1, 1)
        at_end = lax.broadcasted_iota(jnp.int32, (states, tl), 1) == tl - 1
        tsc[rank + states : nproj, at] = jnp.where(at_end, end, shifted)
        pp2[at, :] = tsc[:, at].T
        pp2[at, 0:rank] = mm(dpl[at, :], dtw[...], NT)
        dproj_copies[part] = Send(lambda: (pp2.at[at, :], pq2.at[at, :]), row, other)

    def dconv_block(b, carry):
        at = pl.multiple_of(b * STEP, STEP)
        view = inner.at[pl.ds(at, STEP + 8)]
        rows = pl.ds(at, STEP)
        masks = mcol[rows, :]
        sums = [list(v) for v in carry]
        for n, sl in enumerate(halves):
            grad = (s1[rows, sl] + sq[rows, sl]) * dsilu[rows, sl]
            dconv[rows, sl] = grad
            terms = [grad, grad * view[8 : 8 + STEP, sl]]
            for j in range(1, taps):
                terms.append(grad * masks[:, j - 1 : j] * view[8 - j : 8 - j + STEP, sl])
            for m, term in enumerate(terms):
                sums[m][n] = sums[m][n] + term[0:8] + term[8:16]
        return tuple(tuple(v) for v in sums)

    def dinner_block(b, carry):
        at = pl.multiple_of(b * STEP, STEP)
        view = dconv.at[pl.ds(at, STEP + 8)]
        masks = mcol.at[pl.ds(at, STEP + 8)]
        cw_own = cw[...]
        for sl in halves:
            total = cw_own[taps - 1 : taps, sl] * view[0:STEP, sl]
            for j in range(1, taps):
                tap = cw_own[taps - 1 - j : taps - j, sl]
                total = total + tap * view[j : j + STEP, sl] * masks[j : j + STEP, j - 1 : j]
            dil[pl.ds(at, STEP), sl] = total.astype(bf16)
        return carry

    def inner_grads(part):
        at = slice(part * tl, (part + 1) * tl)
        span_of = (part * chunks // 2, (part + 1) * chunks // 2)
        dproj_copies[part].wait_recv()
        dproj = pp2[at, :] + pq2[at, :]
        pq2[at, :] = dproj
        dproj_low = dproj[:, 0:nproj].astype(bf16)
        for sl in lane_tiles(w, 2 * LANES):
            sq[at, sl] = mm(dproj_low, xw[:, sl])
        names = range(tot_conv, tot_conv + taps + 1)
        sums = lax.fori_loop(*span_of, dconv_block, tuple(read_tot(n) for n in names), unroll=4)
        for n, values in zip(names, sums):
            write_tot(n, values)
        lax.fori_loop(*span_of, dinner_block, 0, unroll=4)
        sum_in.send_factors(part)

    def late_half():
        back_sums(chunks // 2, *even_bufs)
        projection_grads(1)

    def out_sums():
        for copy in relays[1]:
            copy.wait_recv()
        sum_out.partial()

    def gate_factors():
        sum_gate.send_factors(0)
        sum_gate.send_factors(1)

    def gate_sums():
        for copy in relays[0]:
            copy.wait_recv()
        sum_gate.partial()

    def end_normed():
        share_end(0)

    def inner_late():
        inner_grads(1)

    events = (
        (1, out_sums, gate_factors), (2, end_normed), (3, late_half), (5, gate_sums, sum_out.total), (6, inner_late),
    )

    def back_pair(step, carry):
        m = pairs - 1 - step
        back_sums(jnp.minimum(2 * m + 2, chunks - 1), *even_bufs)
        carry = back_chunk(2 * m + 1, carry, odd, odd_at(m), even, even_at(m) + span - states, *odd_bufs)
        back_sums(2 * m + 1, *odd_bufs)
        flow, acc = back_chunk(2 * m, carry, even, even_at(m), odd, even_at(m), *even_bufs)
        for when, *steps in events:

            @pl.when(step == when * pairs // 8)
            def _():
                for event in steps:
                    event()

        return tuple(flow), tuple(acc)

    carry = lax.fori_loop(0, pairs, back_pair, (zeros, zeros))
    back_sums(0, *even_bufs)
    for j, sl in enumerate(tile):
        sm[nproj + rank : first, sl] = carry[1][j] * rates[j]
    projection_grads(0)
    for sl in lane_tiles(d, 2 * LANES):
        dn[:, sl] = mm(dgl[...], win_g[sl, :], NT)
    inner_grads(0)
    sum_gate.total()
    sum_out.pass_on(1)
    sum_out.pass_on(2)
    for sl in lane_tiles(d, 2 * LANES):
        dn[:, sl] = dn[:, sl] + mm(dil[...], win_i[sl, :], NT)
    dn_copy = Send(lambda: (dn.at[pl.ds(theirs, tl), :], dnr), row, other)
    dproj_turned = pq2[...].T[0:nproj, :].astype(bf16)
    for sl in lane_tiles(w, 2 * LANES):
        sm[0:nproj, sl] = mm(dproj_turned, actl[:, sl])
        sm[nproj : nproj + rank, sl] = mm(rank_turned, dpl[:, sl])

    def put_line(line, n):
        for value, sl in zip(read_tot(n), halves):
            sm[line : line + 1, sl] = jnp.sum(value, axis=0, keepdims=True)

    put_line(line_dtb, tot_dtb)
    put_line(line_skip, tot_skip)
    put_line(line_cb, tot_conv)
    for j in range(taps):
        put_line(line_conv + taps - 1 - j, tot_conv + 1 + j)
    def gain_block(b, carry):
        rows = pl.ds(pl.multiple_of(b * STEP, STEP), STEP)
        values = ng[2, rows, :].astype(f32)
        scale = lax.rsqrt(jnp.mean(values * values, axis=-1, keepdims=True) + EPS)
        both = dn[rows, :] * (values * scale)
        return carry + both[0:8] + both[8:16]

    total = lax.fori_loop(0, chunks, gain_block, jnp.zeros((8, d), f32), unroll=4)
    sm[line_gain : line_gain + 1, :] = jnp.sum(total, axis=0, keepdims=True)
    across_tiles = packed // LANES
    for n in range(sm.shape[0] // 16 * tiles):
        to = slice(n // across_tiles * 16, n // across_tiles * 16 + 16)
        to_lanes = tile[n % across_tiles]
        value = sm[n // tiles * 16 : n // tiles * 16 + 16, tile[n % tiles]]
        smb[to, to_lanes] = value.astype(bf16)
        sms[to, to_lanes] = value
    srows = DEPTH * extra
    over_plane = [
        Send(
            lambda s=s: (smb.at[block(plane_place[s], srows), :], sfac.at[s - 1]),
            plane_row[s],
            core,
        )
        for s in range(1, PLANE)
    ]
    sum_in.partial()
    sum_out.pass_on(3)
    sum_gate.pass_on(1)
    sum_gate.pass_on(2)
    sum_out.pass_across(0)
    for copy in over_plane:
        copy.wait_recv()
    total = sms[block(place, srows), :]
    for s in range(PLANE - 1):
        total = total + sfac[s].astype(f32)
    sms[block(place, srows), :] = total
    spb[...] = total.astype(bf16)
    small_depth = [
        Send(lambda s=s: (spb.at[block(z_place[s], extra), :], szr.at[s - 1]), z_row[s], core)
        for s in range(1, DEPTH)
    ]
    sum_out.pass_across(1)
    sum_out.pass_across(2)
    sum_out.pass_across(3)
    for copy in small_depth:
        copy.wait_recv()

    def small_rows(first, count):
        first = (core * TEAM + first) * extra
        return small.at[pl.ds(pl.multiple_of(first, count * extra), count * extra), :]

    own_small = place * DEPTH + pz
    total = sms[block(own_small, extra), :]
    for s in range(DEPTH - 1):
        total = total + szr[s].astype(f32)
    small_rows(own_small, 1)[...] = total.astype(bf16)
    refs = pair_to(lambda: small_rows(own_small, 1))
    small_along = [Send(refs, z_row[s], core) for s in range(1, DEPTH)]
    sum_gate.pass_on(3)
    sum_in.total()

    for sl in lane_tiles(d, 2 * LANES):
        outp[:, sl] = mm(gt[...], wo[:, sl])
    out_copy = Send(lambda: (outp.at[pl.ds(theirs, tl), :], outr), row, other)

    def norm_back(b, carry):
        at = pl.multiple_of(b * STEP, STEP)
        rows = pl.ds(at, STEP)
        values = ng[2, pl.ds(mine + at, STEP), :].astype(f32)
        scale = lax.rsqrt(jnp.mean(values * values, axis=-1, keepdims=True) + EPS)
        unit_rows = values * scale
        inside = (dn[pl.ds(mine + at, STEP), :] + dnr[rows, :]) * lines[0:1, 0:d]
        mean = jnp.mean(inside * unit_rows, axis=-1, keepdims=True)
        given = ng[1, pl.ds(mine + at, STEP), :].astype(f32)
        gtok[rows, :] = (given + scale * (inside - unit_rows * mean)).astype(bf16)
        return carry

    dn_copy.wait_recv()
    lax.fori_loop(0, tl // STEP, norm_back, 0, unroll=4)
    out_copy.wait_recv()
    lax.fori_loop(0, tl // STEP, out_block, 0, unroll=4)

    sum_gate.pass_across(0)
    sum_gate.pass_across(1)
    for copy in small_along:
        copy.wait_recv()
    refs = pair_to(lambda: small_rows(place * DEPTH, DEPTH))
    small_near = [Send(refs, plane_row[s], core) for s in range(1, PLANE)]
    sum_out.finish()
    sum_in.pass_on(1)
    sum_in.pass_on(2)
    sum_gate.pass_across(2)
    sum_gate.pass_across(3)
    sum_in.pass_on(3)
    sum_in.pass_across(0)
    for copy in small_near:
        copy.wait_recv()
    twin_small = Send(pair_to(lambda: small_rows(0, TEAM)), row, other)
    sum_gate.finish()
    for s in (1, 2, 3):
        sum_in.pass_across(s)
    sum_in.finish()
    for copy in sum_out.twin + sum_gate.twin + [twin_small] + sum_in.twin:
        copy.wait_recv()
    for copy in pending:
        copy.wait_send()


def wide_kernel(output, grad_tokens, gout, ggate, ginner, small, *refs):
    out_o, out_t, gin_f, gout_f, *rest = refs
    *rest, wide_in, wide_out, value, sems = rest
    finals, rows = rest[: len(rest) // 2], rest[len(rest) // 2 :]
    steps = wide_in.shape[0]
    cols, lines = wide_in.shape[2], wide_out.shape[1]
    copies = []

    def put(src, dst, *sem):
        copies.append(pltpu.make_async_copy(src, dst, sems.at[sem]))
        copies[-1].start()

    put(output, out_o, 2, 0)
    put(grad_tokens, out_t, 2, 1)
    e, d = ggate.shape
    blocks = e // cols
    for i in range(steps):
        at = slice(i * lines, (i + 1) * lines)
        wide_out[i] = gout[at, :].astype(f32)
        put(wide_out.at[i], gout_f.at[at, :], 1, i)
        source = ginner if i < blocks else ggate
        first = i % blocks * cols
        wide_in[i] = source[first : first + cols, :].T.astype(f32)
        put(wide_in.at[i], gin_f.at[:, i * cols : (i + 1) * cols], 0, i)

    matrices = [ref for ref in rows if len(ref.shape) == 2]
    vectors = [ref for ref in rows if len(ref.shape) == 1]
    gain = 0.0
    tiles, across = d // LANES, small.shape[1] // LANES
    for core in range(2):
        for n in range(value.shape[0] // 16 * tiles):
            first = (core * TEAM + n // across) * 16
            at_row, at_lane, lane = n // tiles * 16, n % tiles * LANES, n % across * LANES
            value[at_row : at_row + 16, at_lane : at_lane + LANES] = small[
                first : first + 16, lane : lane + LANES
            ].astype(f32)
        at_lanes = slice(core * d, (core + 1) * d)
        at = 0
        for ref in matrices:
            ref[:, at_lanes] = value[at : at + ref.shape[0], :]
            at += ref.shape[0]
        for ref in vectors[:-1]:
            ref[at_lanes] = value[at : at + 1, :].reshape(d)
            at += 1
        gain = gain + value[at : at + 1, :]
    vectors[-1][...] = gain.reshape(d)
    for n, (src, dst) in enumerate(zip(rows, finals)):
        put(src, dst, 3, n)
    for copy in copies:
        copy.wait()


def local(
    tokens, marks, norm_gain, in_weight, conv_weight, conv_bias, x_weight, dt_weight,
    dt_bias, a_log, skip, out_weight, cotangent,
):
    tl, d = tokens.shape[1:]
    e = out_weight.shape[0]
    w = e // lax.axis_size("seq")
    t = tl * lax.axis_size("seq")
    states, rank, nproj, taps = a_log.shape[0], dt_weight.shape[0], x_weight.shape[0], conv_weight.shape[0]
    chunks, span = t // STEP, STEP * states
    quarter = w // PLANE
    zrows = quarter // DEPTH
    lines = -(-(nproj + rank + states + taps + 4) // 16) * 16
    packed = -(-(lines // 16) * (w // LANES) // TEAM) * LANES
    pieces = 16 * TEAM
    vmem = pl.BlockSpec(memory_space=pltpu.VMEM)
    anywhere = pl.BlockSpec(memory_space=pl.ANY)
    wide = pltpu.VMEM((t, w), f32)
    low = pltpu.VMEM((t, w), bf16)
    one = pltpu.VMEM((t, LANES), f32)
    scratch = [
        pltpu.VMEM((d, w), bf16), pltpu.VMEM((d, w), bf16), pltpu.VMEM((w, d), bf16),
        pltpu.VMEM((d,), f32), pltpu.VMEM((taps, w), f32), pltpu.VMEM((e,), f32),
        pltpu.VMEM((nproj, w), bf16), pltpu.VMEM((rank, w), bf16), pltpu.VMEM((e,), f32),
        pltpu.VMEM((states, w), f32), pltpu.VMEM((e,), f32), pltpu.VMEM((8, tl), jnp.int32),
        pltpu.VMEM((3, t, d), bf16), pltpu.VMEM((PLANE - 1, 2, t, d), bf16),
        pltpu.VMEM((8, t), f32), pltpu.VMEM((t + 8, LANES), f32), pltpu.VMEM((8, e), f32),
        pltpu.VMEM((t + 8, w), f32), wide, wide, wide, wide, low, wide, wide, wide, wide, wide, wide, wide,
        one, one, one, one, pltpu.VMEM((LANES, t), f32),
        pltpu.VMEM((t * states // 2, w), bf16), pltpu.VMEM((t * states // 2 + states, w), bf16),
        pltpu.VMEM((chunks, states, LANES), f32), pltpu.VMEM((chunks, states, LANES), f32),
        pltpu.VMEM((t, span), bf16), pltpu.VMEM((t, span), bf16),
        *[pltpu.VMEM((span, w), bf16)] * 4, *[pltpu.VMEM((span, LANES), bf16)] * 4,
        *[pltpu.VMEM((chunks, states, LANES), f32)] * 2,
        pltpu.VMEM((states, LANES), f32), pltpu.VMEM((taps + 3, 8, w), f32),
        low, low, low, low, pltpu.VMEM((3, w, t), bf16), pltpu.VMEM((t + 8, w), f32),
        pltpu.VMEM((t, d), f32), pltpu.VMEM((tl, d), f32),
        pltpu.VMEM((t, d), f32), pltpu.VMEM((tl, d), f32),
        pltpu.VMEM((3, PLANE - 1, quarter, t), bf16), pltpu.VMEM((quarter, d), f32),
        pltpu.VMEM((3, zrows, d), f32), pltpu.VMEM((3, quarter, d), bf16),
        pltpu.VMEM((3, DEPTH - 1, zrows, d), bf16),
        pltpu.VMEM((lines, w), f32), pltpu.VMEM((pieces, packed), bf16), pltpu.VMEM((pieces, packed), f32),
        pltpu.VMEM((PLANE - 1, pieces // PLANE, packed), bf16), pltpu.VMEM((pieces // PLANE, packed), bf16),
        pltpu.VMEM((DEPTH - 1, 16, packed), bf16),
        pltpu.SemaphoreType.DMA((16,)),
        pltpu.SemaphoreType.DMA((160,)), pltpu.SemaphoreType.DMA((160,)),
    ]
    output, grad_tokens, gout, ggate, ginner, small = pl.pallas_call(
        body_kernel,
        out_shape=[
            pltpu.VMEM((tl, d), bf16),
            pltpu.VMEM((tl, d), bf16),
            pltpu.VMEM((e, d), bf16),
            pltpu.VMEM((e, d), bf16),
            pltpu.VMEM((e, d), bf16),
            pltpu.VMEM((2 * TEAM * 16, packed), bf16),
        ],
        in_specs=[anywhere] * 13,
        out_specs=[vmem] * 6,
        scratch_shapes=scratch,
        compiler_params=pltpu.CompilerParams(
            collective_id=0, has_side_effects=True, vmem_limit_bytes=56 * 2**20
        ),
        name="block",
    )(
        tokens.reshape(tl, d), marks.reshape(1, tl), norm_gain, in_weight, conv_weight,
        conv_bias, x_weight, dt_weight, dt_bias, a_log, skip, out_weight, cotangent.reshape(tl, d),
    )

    steps = 8
    shapes = [(nproj, e), (rank, e), (states, e), (taps, e), (e,), (e,), (e,), (d,)]
    wide_shapes = [jax.ShapeDtypeStruct(s, f32) for s in [(d, 2 * e), (e, d)] + shapes]
    output, grad_tokens, *grads = pl.pallas_call(
        wide_kernel,
        out_shape=[jax.ShapeDtypeStruct((tl, d), bf16)] * 2 + wide_shapes,
        in_specs=[vmem] * 6,
        out_specs=[anywhere] * (4 + len(shapes)),
        scratch_shapes=[pltpu.VMEM(s, f32) for s in shapes]
        + [
            pltpu.VMEM((steps, d, 2 * e // steps), f32),
            pltpu.VMEM((steps, e // steps, d), f32),
            pltpu.VMEM((lines, w), f32),
            pltpu.SemaphoreType.DMA((4, steps)),
        ],
        compiler_params=pltpu.CompilerParams(vmem_limit_bytes=40 * 2**20),
        name="widen",
    )(output, grad_tokens, gout, ggate, ginner, small)
    rows = lax.axis_size("rows")
    if rows > TEAM:
        grads = [v * (1.0 / TEAM) for v in lax.psum(grads, "rows")]
    grad_in, grad_out, grad_x, grad_dt, grad_log, grad_conv, g_cb, g_dtb, g_skip, g_gain = grads
    return (
        output[None], grad_tokens[None], g_gain, grad_in, grad_conv, g_cb, grad_x, grad_dt, g_dtb, grad_log,
        g_skip, grad_out,
    )


def solution(mesh):
    split = P("rows", "seq", None)
    whole = P()
    in_specs = (split, P("rows", "seq")) + (whole,) * 10 + (split,)
    out_specs = (split, split) + (whole,) * 10
    return jax.shard_map(local, mesh=mesh, in_specs=in_specs, out_specs=out_specs, check_vma=False)
```

```python
import jax
import jax.numpy as jnp
from jax import lax
from jax.experimental import pallas as pl
from jax.experimental.pallas import tpu as pltpu
from jax.sharding import PartitionSpec as P

f32 = jnp.float32
bf16 = jnp.bfloat16
EPS = 1e-05
LANES = 128
STEP = 16
PLANE = 4
DEPTH = 4
TEAM = PLANE * DEPTH
MESH = pl.DeviceIdType.MESH
NN = (((1,), (0,)), ((), ()))
NT = (((1,), (1,)), ((), ()))


def mm(a, b, dims=NN):
    return lax.dot_general(a, b, dims, preferred_element_type=f32)


def lane_tiles(width, size):
    return [slice(j, j + size) for j in range(0, width, size)]


def body_kernel(
    tok, marks, gain_in, win, cw_in, cb_in, xw_in, dtw_in, dtb_in, alog_in, skip_in, wout, cot,
    out, gtok, gout, ggate, ginner, small,
    win_i, win_g, wo, gain, cw, cb, xw, dtw, dtb, alog, skip, mkraw, ng, ngh, mk, mcol, lines,
    inner, gate, dgated, act, dsilu, actl, ddec, u, sig, dyf, du, s1, sq,
    pp, pq, pp2, pq2, tsc, even, odd, bt, ct, cbd, bbd, ga, gb, qa, qb, ba, bb, ca, cc, dbt, dct, lastc, tot,
    gt, dgl, dpl, dil, turn, dconv, dn, dnr, outp, outr,
    fac, pw, pown, pb, zr, sm, smb, sms, sfac, spb, szr,
    ls, ss, rs,
):
    row, core = lax.axis_index("rows"), lax.axis_index("seq")
    other = 1 - core
    team = row - row % TEAM
    px, py, pz = row % 2, (row // 2) % 2, (row // PLANE) % DEPTH
    tl, d = out.shape
    t = 2 * tl
    w = wo.shape[0]
    states = alog.shape[0]
    rank = dtw.shape[0]
    nproj = xw.shape[0]
    half = w // 2
    quarter = w // PLANE
    zrows = quarter // DEPTH
    extra, packed = smb.shape[0] // TEAM, smb.shape[1]
    place = row % PLANE
    chunks = t // STEP
    tiles = w // LANES
    mine = pl.multiple_of(core * tl, tl)
    theirs = pl.multiple_of(other * tl, tl)
    chan = pl.multiple_of(core * w, w)
    halves = lane_tiles(w, half)
    pending = []

    def flip(low, high, s):
        a, b = s % 2, s // 2
        return (high + b - 2 * b * high) * 2 + low + a - 2 * a * low

    plane_place = [flip(px, py, s) for s in range(PLANE)]
    plane_row = [team + pz * PLANE + plane_place[s] for s in range(PLANE)]
    z_place = [flip(pz % 2, pz // 2, s) for s in range(DEPTH)]
    z_row = [team + z_place[s] * PLANE + place for s in range(DEPTH)]
    ids = iter(range(10_000))

    class Send:
        def __init__(self, refs, to_row, to_core):
            self.refs, self.to, self.k = refs, (to_row, to_core), next(ids)
            self.copy().start()
            pending.append(self)

        def copy(self):
            src, dst = self.refs()
            return pltpu.make_async_remote_copy(
                src_ref=src,
                dst_ref=dst,
                send_sem=ss.at[self.k],
                recv_sem=rs.at[self.k],
                device_id=self.to,
                device_id_type=MESH,
            )

        def wait_recv(self):
            self.copy().wait_recv()

        def wait_send(self):
            self.copy().wait_send()

    def block(index, size):
        return pl.ds(pl.multiple_of(index * size, size), size)

    own = pl.ds(chan, w)
    sources = [
        (tok, ng.at[2, pl.ds(mine, tl), :]),
        (marks, mkraw.at[0:1]),
        (gain_in, gain),
        (win.at[:, own], win_i),
        (cw_in.at[:, own], cw),
        (cb_in, cb),
        (cot, ng.at[1, pl.ds(mine, tl), :]),
        (xw_in.at[:, own], xw),
        (win.at[:, pl.ds(pl.multiple_of(2 * w + core * w, w), w)], win_g),
        (wout.at[own, :], wo),
        (dtw_in.at[:, own], dtw),
        (dtb_in, dtb),
        (skip_in, skip),
        (alog_in.at[:, own], alog),
    ]
    loads = [pltpu.make_async_copy(src, dst, ls.at[n]) for n, (src, dst) in enumerate(sources)]
    for copy in loads:
        copy.start()

    barrier = pltpu.get_barrier_semaphore()
    partners = [(row, other)]
    partners += [(plane_row[s], core) for s in range(1, PLANE)]
    partners += [(z_row[s], core) for s in range(1, DEPTH)]
    for partner in partners:
        pl.semaphore_signal(barrier, inc=1, device_id=partner, device_id_type=MESH)
    pl.semaphore_wait(barrier, len(partners))

    def pair_to(ref):
        return lambda: (ref(), ref())

    def own_rows(kind):
        return ng.at[kind, pl.ds(mine, tl), :]

    def slot(s, kind, first=0, count=tl):
        return ngh.at[s - 1, kind, pl.ds(pl.multiple_of(mine + first, count), count), :]

    twin = [
        Send(lambda n=n, ref=ref: (ref, ng.at[n, pl.ds(mine, tl), :]), row, other)
        for n, ref in ((2, tok), (1, cot))
    ]
    twin.append(Send(lambda: (marks, mkraw.at[1:2]), row, other))
    early, across, relays = {}, {}, {0: [], 1: []}
    piece = tl // 2

    def share(kind):
        early[kind] = [
            Send(lambda s=s: (cot if kind else own_rows(kind), slot(s, kind)), plane_row[s], core)
            for s in (1, 2)
        ]

    def share_on(kind):
        across[kind] = []
        for s in (1, 2):
            early[kind][s - 1].wait_recv()
            first = (s - 1) * piece
            refs = lambda s=s, first=first: (slot(s, kind, first, piece), slot(3, kind, first, piece))
            across[kind].append(Send(refs, plane_row[3 - s], core))
            relays[kind].append(Send(pair_to(lambda s=s: slot(s, kind)), row, other))

    def share_end(kind):
        for s in (1, 2):
            across[kind][s - 1].wait_recv()
            refs = pair_to(lambda first=(s - 1) * piece: slot(3, kind, first, piece))
            relays[kind].append(Send(refs, row, other))

    share(1)

    for copy in loads[:3]:
        copy.wait()
    count = gain.shape[0]
    lines[0:1, 0:count] = gain[...].reshape(1, count)
    unit = 2 * STEP

    def norm_rows(first):
        gain_row = lines[0:1, 0:d]

        def norm_block(b, carry):
            at = pl.ds(pl.multiple_of(first + b * unit, unit), unit)
            rows = ng[2, at, :].astype(f32)
            scale = lax.rsqrt(jnp.mean(rows * rows, axis=-1, keepdims=True) + EPS)
            ng[0, at, :] = (rows * scale * gain_row).astype(bf16)
            return carry

        lax.fori_loop(0, tl // unit, norm_block, 0, unroll=4)

    norm_rows(mine)
    share(0)

    inner[0:8, :] = jnp.zeros((8, w), f32)
    dconv[t : t + 8, :] = jnp.zeros((8, w), f32)
    mcol[t : t + 8, :] = jnp.zeros((8, LANES), f32)
    odd[0:states, :] = jnp.zeros((states, w), bf16)
    tsc[...] = jnp.zeros(tsc.shape, f32)
    tot[...] = jnp.zeros(tot.shape, f32)
    smb[...] = jnp.zeros(smb.shape, bf16)
    sms[...] = jnp.zeros(sms.shape, f32)
    for ref in (ga, qa, ba, ca):
        ref[...] = jnp.zeros(ref.shape, bf16)
    sm[...] = jnp.zeros(sm.shape, f32)

    for copy in twin:
        copy.wait_recv()
    norm_rows(theirs)
    own_marks, twin_marks = mkraw[0:1, :].astype(f32), mkraw[1:2, :].astype(f32)
    mk[:, pl.ds(mine, tl)] = jnp.broadcast_to(own_marks, (8, tl))
    mk[:, pl.ds(theirs, tl)] = jnp.broadcast_to(twin_marks, (8, tl))
    for copy in loads[3:7]:
        copy.wait()

    for sl in lane_tiles(w, 2 * LANES):
        inner[8 : 8 + t, sl] = mm(ng[0], win_i[:, sl]).astype(bf16).astype(f32)

    lane = lax.broadcasted_iota(jnp.int32, (8, t), 1)
    mark = mk[...]
    keep = jnp.where(lane == 0, 0.0, 1.0 - mark)
    mask2 = keep * pltpu.roll(keep, 1, 1)
    mask3 = mask2 * pltpu.roll(keep, 2, 1)
    line = lax.broadcasted_iota(jnp.int32, (LANES, t), 0)

    def spread(v):
        return jnp.broadcast_to(v[0:1, :], (LANES, t))

    stacked = jnp.where(line == 0, spread(keep), 0.0)
    stacked = jnp.where(line == 1, spread(mask2), stacked)
    stacked = jnp.where(line == 2, spread(mask3), stacked)
    stacked = jnp.where(line == 3, spread(mark), stacked)
    mcol[0:t, :] = stacked.T

    for copy in loads[7:]:
        copy.wait()
    for n, ref in enumerate((gain, cb, dtb, skip)):
        count = ref.shape[0]
        lines[n : n + 1, 0:count] = ref[...].reshape(1, count)
    cw_own = cw[...]
    cb_own = lines[1:2, pl.ds(chan, w)]
    taps = cw.shape[0]

    def conv_block(b, carry):
        at = pl.multiple_of(b * STEP, STEP)
        view = inner.at[pl.ds(at, STEP + 8)]
        masks = mcol[pl.ds(at, STEP), :]
        for sl in halves:
            total = cb_own[:, sl] + cw_own[taps - 1 : taps, sl] * view[8 : 8 + STEP, sl]
            for j in range(1, taps):
                tap = cw_own[taps - 1 - j : taps - j, sl]
                total = total + tap * view[8 - j : 8 - j + STEP, sl] * masks[:, j - 1 : j]
            sg = 1.0 / (1.0 + jnp.exp(-total))
            value = total * sg
            act[pl.ds(at, STEP), sl] = value
            actl[pl.ds(at, STEP), sl] = value.astype(bf16)
            dsilu[pl.ds(at, STEP), sl] = sg * (1.0 + total * (1.0 - sg))
        return carry

    lax.fori_loop(0, chunks, conv_block, 0, unroll=4)
    xw_own = xw[...]
    pp[:, 0:nproj] = mm(actl[...], xw_own, NT)
    proj_copy = Send(lambda: (pp, pq), row, other)

    for sl in lane_tiles(w, 2 * LANES):
        gate[:, sl] = mm(ng[0], win_g[:, sl])
        dgated[:, sl] = mm(ng[1], wo[sl, :], NT)

    def dy_block(b, carry):
        at = pl.ds(pl.multiple_of(b * STEP, STEP), STEP)
        for sl in halves:
            g = gate[at, sl]
            low = (dgated[at, sl] * (g / (1.0 + jnp.exp(-g)))).astype(bf16)
            dyf[at, sl] = low.astype(f32)
        return carry

    lax.fori_loop(0, chunks, dy_block, 0, unroll=4)

    share_on(1)

    proj_copy.wait_recv()
    proj = pp[...] + pq[...]
    turned = proj.T
    for k in range(chunks):
        cols = slice(k * STEP, (k + 1) * STEP)
        bt[k, :, 0:STEP] = turned[rank : rank + states, cols]
        ct[k, :, 0:STEP] = turned[rank + states : rank + 2 * states, cols]
    rank_low = proj[:, 0:rank].astype(bf16)
    rank_turned = turned[0:rank, :].astype(bf16)
    dtw_own = dtw[...]
    dtb_own = lines[2:3, pl.ds(chan, w)]
    for sl in lane_tiles(w, 2 * LANES):
        sig[:, sl] = mm(rank_low, dtw_own[:, sl]) + dtb_own[:, sl]

    def delta_block(b, carry):
        at = pl.ds(pl.multiple_of(b * STEP, STEP), STEP)
        marked = mcol[at, :][:, 3:4] > 0.5
        for sl in halves:
            pre = sig[at, sl]
            e = jnp.exp(-jnp.abs(pre))
            one = 1.0 + e
            log1p = jnp.where(one == 1.0, e, jnp.log(one) * (e / (one - 1.0)))
            delta = jnp.maximum(pre, 0.0) + log1p
            sig[at, sl] = jnp.where(pre >= 0.0, 1.0, e) / one
            inflow = delta * act[at, sl]
            u[at, sl] = inflow
            s1[at, sl] = delta
            ddec[at, sl] = jnp.where(marked, 1e30, delta)
        return carry

    lax.fori_loop(0, chunks, delta_block, 0, unroll=4)

    span = STEP * states
    pick = (
        lax.broadcasted_iota(jnp.int32, (states, span), 0)
        == lax.broadcasted_iota(jnp.int32, (states, span), 1) % states
    ).astype(bf16)
    diag = (
        lax.broadcasted_iota(jnp.int32, (t, span), 0) % STEP
        == lax.broadcasted_iota(jnp.int32, (t, span), 1) // states
    )
    ones_diag = diag[0:STEP].astype(bf16)
    b_low = proj[:, rank : rank + states].astype(bf16)
    c_low = proj[:, rank + states : rank + 2 * states].astype(bf16)
    bbd[...] = jnp.where(diag, mm(b_low, pick), 0.0).astype(bf16)
    cbd[...] = jnp.where(diag, mm(c_low, pick), 0.0).astype(bf16)

    rates = [-jnp.exp(alog[:, j * LANES : (j + 1) * LANES]) for j in range(tiles)]
    zeros = tuple(jnp.zeros((states, LANES), f32) for _ in range(tiles))
    tile = [slice(j * LANES, (j + 1) * LANES) for j in range(tiles)]

    def even_at(m):
        return pl.multiple_of(m * span, span)

    def odd_at(m):
        return pl.multiple_of(states + m * span, states)

    def state_block(ref, first, i):
        return ref.at[pl.ds(pl.multiple_of(first + i * states, states), states)]

    def scan_chunk(k, state, kept, first):
        rows = pl.ds(pl.multiple_of(k * STEP, STEP), STEP)
        b_here, dec, flow = bt[k], ddec.at[rows], u.at[rows]
        state = list(state)
        for i in range(STEP):
            b_wide = jnp.broadcast_to(b_here[:, i : i + 1], (states, LANES))
            dest = state_block(kept, first, i)
            for j, sl in enumerate(tile):
                decay = jnp.exp(dec[i : i + 1, sl] * rates[j])
                state[j] = decay * state[j] + flow[i : i + 1, sl] * b_wide
                dest[:, sl] = state[j].astype(bf16)
        return state

    def read_chunk(k, kept, first):
        rows = pl.ds(pl.multiple_of(k * STEP, STEP), STEP)
        du[rows, :] = mm(cbd[rows, :], kept[pl.ds(pl.multiple_of(first, states), span), :])


    def gated_block(b, carry):
        skip_own = lines[3:4, pl.ds(chan, w)]
        at = pl.ds(pl.multiple_of(b * STEP, STEP), STEP)
        for sl in halves:
            y = (du[at, sl] + skip_own[:, sl] * act[at, sl]).astype(bf16).astype(f32)
            g = gate[at, sl]
            sg = 1.0 / (1.0 + jnp.exp(-g))
            gt[at, sl] = (y * (g * sg)).astype(bf16)
            dgl[at, sl] = (dgated[at, sl] * y * (sg * (1.0 + g * (1.0 - sg)))).astype(bf16)
        return carry

    class Sum:
        def __init__(self, n, source):
            self.n, self.source, self.factors = n, source, []
            self.near, self.far, self.twin = [], [], []

        def send_factors(self, part):
            n, at = self.n, slice(part * tl, (part + 1) * tl)
            for sl in tile:
                turn[n, sl, at] = self.source[at, sl].T
            for s in range(1, PLANE):
                refs = lambda s=s: (
                    turn.at[n, block(plane_place[s], quarter), at],
                    fac.at[n, s - 1, :, at],
                )
                self.factors.append(Send(refs, plane_row[s], core))

        def rows(self, where, first, count):
            ref = (gout, ggate, ginner)[self.n]
            first = chan + where * quarter + first
            return ref.at[pl.ds(pl.multiple_of(first, count), count), :]

        def shard(self, where, z):
            return self.rows(where, z * zrows, zrows)

        def partial(self):
            n = self.n
            for copy in self.factors:
                copy.wait_recv()
            kind = 1 if n == 0 else 0
            lefts = [turn[n, block(place, quarter), :]] + [fac[n, s] for s in range(PLANE - 1)]
            for sl in lane_tiles(d, 2 * LANES):
                total = mm(lefts[0], ng[kind, :, sl])
                for s in range(PLANE - 1):
                    total = total + mm(lefts[s + 1], ngh[s, kind, :, sl])
                pw[:, sl] = total
                pb[n, :, sl] = total.astype(bf16)
            pown[n] = pw[block(pz, zrows), :]
            self.depth = [
                Send(
                    lambda s=s: (pb.at[n, block(z_place[s], zrows), :], zr.at[n, s - 1]),
                    z_row[s],
                    core,
                )
                for s in range(1, DEPTH)
            ]

        def near_shard(self, z):
            part = pair_to(lambda: self.shard(place, z))
            self.near.append([Send(part, plane_row[s], core) for s in (1, 2)])

        def total(self):
            for copy in self.depth:
                copy.wait_recv()
            total = pown[self.n]
            for s in range(DEPTH - 1):
                total = total + zr[self.n, s].astype(f32)
            part = self.shard(place, pz)
            part[...] = total.astype(bf16)
            own = pair_to(lambda: self.shard(place, pz))
            self.along = [Send(own, z_row[s], core) for s in (1, 2)]
            self.beyond = []
            self.near_shard(pz)

        def pass_on(self, s):
            if s < 3:
                self.along[s - 1].wait_recv()
                part = pair_to(lambda: self.shard(place, z_place[s]).at[:, halves[s - 1]])
                self.beyond.append(Send(part, z_row[3 - s], core))
            else:
                for copy in self.beyond:
                    copy.wait_recv()
            self.near_shard(z_place[s])
            if s == DEPTH - 1:
                self.to_twin(place)

        def pass_across(self, s):
            for copy in self.near[s]:
                copy.wait_recv()
            far = []
            for q in (1, 2):
                part = pair_to(lambda q=q: self.shard(plane_place[q], z_place[s]).at[:, halves[q - 1]])
                far.append(Send(part, plane_row[3 - q], core))
            self.far.append(far)
            if s == DEPTH - 1:
                for q in (1, 2):
                    self.to_twin(plane_place[q])

        def to_twin(self, where):
            self.twin.append(Send(pair_to(lambda: self.rows(where, 0, quarter)), row, other))

        def finish(self):
            for s, far in enumerate(self.far):
                for copy in far:
                    copy.wait_recv()
                part = pair_to(lambda s=s: self.shard(plane_place[3], z_place[s]))
                self.twin.append(Send(part, row, other))

    sum_out, sum_gate, sum_in = Sum(0, gt), Sum(1, dgl), Sum(2, dil)

    def gated_half(part):
        lax.fori_loop(part * chunks // 2, (part + 1) * chunks // 2, gated_block, 0, unroll=4)
        sum_out.send_factors(part)

    pairs = chunks // 2
    odd[pl.ds(states, span), :] = jnp.zeros((span, w), bf16)

    def scan_pair(m, state):
        read_chunk(jnp.maximum(2 * m - 1, 0), odd, odd_at(jnp.maximum(m - 1, 0)))
        state = scan_chunk(2 * m, state, even, even_at(m))
        read_chunk(2 * m, even, even_at(m))
        state = scan_chunk(2 * m + 1, state, odd, odd_at(m))

        @pl.when(m == pairs // 2 - 1)
        def _():
            read_chunk(chunks // 2 - 1, odd, odd_at(pairs // 2 - 1))
            gated_half(0)
            share_on(0)

        return tuple(state)

    final = lax.fori_loop(0, pairs, scan_pair, zeros)
    read_chunk(chunks - 1, odd, odd_at(pairs - 1))
    gated_half(1)
    share_end(1)

    late = sum(dyf[t - 1 : t, sl] * final[j] for j, sl in enumerate(tile))
    lastc[...] = jnp.broadcast_to(jnp.sum(late, axis=1, keepdims=True), (states, LANES))

    def back_chunk(k, carry, kept, first, before, last, gbuf, qbuf, bbuf, cbuf):
        base = pl.multiple_of(k * STEP, STEP)
        rows = pl.ds(base, STEP)
        c_here, dec, dys, inflow = ct[k], ddec.at[rows], dyf.at[rows], u.at[rows]
        dys_before = dyf.at[pl.ds(pl.multiple_of(jnp.maximum(base - STEP, 0), STEP), STEP)]
        flow, acc = list(carry[0]), list(carry[1])
        for i in reversed(range(STEP)):
            c_wide = jnp.broadcast_to(c_here[:, i : i + 1], (states, LANES))
            at = slice(i * states, (i + 1) * states)
            old = state_block(kept, first, i - 1) if i else state_block(before, last, 0)
            dy_old = dys_before[STEP - 1 : STEP, :] if i == 0 else dys[i - 1 : i, :]
            for_b = for_c = None
            for j, sl in enumerate(tile):
                rate = dec[i : i + 1, sl]
                g = c_wide * dys[i : i + 1, sl] + flow[j]
                gbuf[at, sl] = g.astype(bf16)
                flow[j] = g * jnp.exp(rate * rates[j])
                h_old = old[:, sl].astype(f32)
                q = flow[j] * h_old
                acc[j] = acc[j] + q * rate
                qbuf[at, sl] = (q * rates[j]).astype(bf16)
                term_b, term_c = g * inflow[i : i + 1, sl], h_old * dy_old[:, sl]
                for_b = term_b if for_b is None else for_b + term_b
                for_c = term_c if for_c is None else for_c + term_c
            bbuf[at, :] = for_b.astype(bf16)
            cbuf[at, :] = for_c.astype(bf16)
        return flow, acc

    lane_of = lax.broadcasted_iota(jnp.int32, (states, LANES), 1)
    ones = jnp.ones((LANES, LANES), bf16)

    def back_sums(k, gbuf, qbuf, bbuf, cbuf):
        rows = pl.ds(pl.multiple_of(k * STEP, STEP), STEP)
        for parts, dest in ((bbuf, dbt), (cbuf, dct)):
            summed = mm(parts[...], ones)
            value = jnp.zeros((states, LANES), f32)
            for i in range(STEP):
                value = jnp.where(lane_of == i, summed[i * states : (i + 1) * states, :], value)
            dest[k] = value
        du[rows, :] = mm(bbd[rows, :], gbuf[...])
        sq[rows, :] = mm(ones_diag, qbuf[...])

    even_bufs, odd_bufs = (ga, qa, ba, ca), (gb, qb, bb, cc)

    def out_block(b, carry):
        at = pl.multiple_of(b * STEP, STEP)
        rows = pl.ds(at, STEP)
        total = outp[pl.ds(mine + at, STEP), :] + outr[rows, :]
        out[rows, :] = (ng[2, pl.ds(mine + at, STEP), :].astype(f32) + total).astype(bf16)
        return carry

    first = nproj + rank + states
    line_conv, line_cb, line_dtb, line_skip, line_gain = (
        first,
        first + taps,
        first + taps + 1,
        first + taps + 2,
        first + taps + 3,
    )
    tot_dtb, tot_skip, tot_conv = 0, 1, 2
    dproj_copies = {}

    def read_tot(n):
        return tuple(tot[n, :, sl] for sl in halves)

    def write_tot(n, values):
        for value, sl in zip(values, halves):
            tot[n, :, sl] = value

    def dpre_block(b, carry):
        at = pl.ds(pl.multiple_of(b * STEP, STEP), STEP)
        skip_own = lines[3:4, pl.ds(chan, w)]
        sums, gains = [], []
        for n, sl in enumerate(halves):
            flow, value, dy = du[at, sl], act[at, sl], dyf[at, sl]
            dpre = (sq[at, sl] + flow * value) * sig[at, sl]
            dpl[at, sl] = dpre.astype(bf16)
            s1[at, sl] = flow * s1[at, sl] + skip_own[:, sl] * dy
            both = dy * value
            sums.append(carry[0][n] + dpre[0:8] + dpre[8:16])
            gains.append(carry[1][n] + both[0:8] + both[8:16])
        return tuple(sums), tuple(gains)

    def projection_grads(part):
        at = slice(part * tl, (part + 1) * tl)
        span_of = (part * chunks // 2, (part + 1) * chunks // 2)
        sums, gains = lax.fori_loop(*span_of, dpre_block, (read_tot(tot_dtb), read_tot(tot_skip)), unroll=4)
        write_tot(tot_dtb, sums)
        write_tot(tot_skip, gains)
        for k in range(*span_of):
            cols = slice(k * STEP, (k + 1) * STEP)
            tsc[rank : rank + states, cols] = dbt[k][:, 0:STEP]
            tsc[rank + states : nproj, cols] = dct[k][:, 0:STEP]
        end = lastc[:, 0:1] if part else dct[chunks // 2][:, 0:1]
        shifted = pltpu.roll(tsc[rank + states : nproj, at], tl - 1, 1)
        at_end = lax.broadcasted_iota(jnp.int32, (states, tl), 1) == tl - 1
        tsc[rank + states : nproj, at] = jnp.where(at_end, end, shifted)
        pp2[at, :] = tsc[:, at].T
        pp2[at, 0:rank] = mm(dpl[at, :], dtw[...], NT)
        dproj_copies[part] = Send(lambda: (pp2.at[at, :], pq2.at[at, :]), row, other)

    def dconv_block(b, carry):
        at = pl.multiple_of(b * STEP, STEP)
        view = inner.at[pl.ds(at, STEP + 8)]
        rows = pl.ds(at, STEP)
        masks = mcol[rows, :]
        sums = [list(v) for v in carry]
        for n, sl in enumerate(halves):
            grad = (s1[rows, sl] + sq[rows, sl]) * dsilu[rows, sl]
            dconv[rows, sl] = grad
            terms = [grad, grad * view[8 : 8 + STEP, sl]]
            for j in range(1, taps):
                terms.append(grad * masks[:, j - 1 : j] * view[8 - j : 8 - j + STEP, sl])
            for m, term in enumerate(terms):
                sums[m][n] = sums[m][n] + term[0:8] + term[8:16]
        return tuple(tuple(v) for v in sums)

    def dinner_block(b, carry):
        at = pl.multiple_of(b * STEP, STEP)
        view = dconv.at[pl.ds(at, STEP + 8)]
        masks = mcol.at[pl.ds(at, STEP + 8)]
        cw_own = cw[...]
        for sl in halves:
            total = cw_own[taps - 1 : taps, sl] * view[0:STEP, sl]
            for j in range(1, taps):
                tap = cw_own[taps - 1 - j : taps - j, sl]
                total = total + tap * view[j : j + STEP, sl] * masks[j : j + STEP, j - 1 : j]
            dil[pl.ds(at, STEP), sl] = total.astype(bf16)
        return carry

    def inner_grads(part):
        at = slice(part * tl, (part + 1) * tl)
        span_of = (part * chunks // 2, (part + 1) * chunks // 2)
        dproj_copies[part].wait_recv()
        dproj = pp2[at, :] + pq2[at, :]
        pq2[at, :] = dproj
        dproj_low = dproj[:, 0:nproj].astype(bf16)
        for sl in lane_tiles(w, 2 * LANES):
            sq[at, sl] = mm(dproj_low, xw[:, sl])
        names = range(tot_conv, tot_conv + taps + 1)
        sums = lax.fori_loop(*span_of, dconv_block, tuple(read_tot(n) for n in names), unroll=4)
        for n, values in zip(names, sums):
            write_tot(n, values)
        lax.fori_loop(*span_of, dinner_block, 0, unroll=4)
        sum_in.send_factors(part)

    def late_half():
        back_sums(chunks // 2, *even_bufs)
        projection_grads(1)

    def out_sums():
        for copy in relays[1]:
            copy.wait_recv()
        sum_out.partial()

    def gate_factors():
        sum_gate.send_factors(0)
        sum_gate.send_factors(1)

    def gate_sums():
        for copy in relays[0]:
            copy.wait_recv()
        sum_gate.partial()

    def end_normed():
        share_end(0)

    def inner_late():
        inner_grads(1)

    events = (
        (1, out_sums, gate_factors), (2, end_normed), (3, late_half), (5, gate_sums, sum_out.total), (6, inner_late),
    )

    def back_pair(step, carry):
        m = pairs - 1 - step
        back_sums(jnp.minimum(2 * m + 2, chunks - 1), *even_bufs)
        carry = back_chunk(2 * m + 1, carry, odd, odd_at(m), even, even_at(m) + span - states, *odd_bufs)
        back_sums(2 * m + 1, *odd_bufs)
        flow, acc = back_chunk(2 * m, carry, even, even_at(m), odd, even_at(m), *even_bufs)
        for when, *steps in events:

            @pl.when(step == when * pairs // 8)
            def _():
                for event in steps:
                    event()

        return tuple(flow), tuple(acc)

    carry = lax.fori_loop(0, pairs, back_pair, (zeros, zeros))
    back_sums(0, *even_bufs)
    for j, sl in enumerate(tile):
        sm[nproj + rank : first, sl] = carry[1][j] * rates[j]
    projection_grads(0)
    for sl in lane_tiles(d, 2 * LANES):
        dn[:, sl] = mm(dgl[...], win_g[sl, :], NT)
    inner_grads(0)
    sum_gate.total()
    sum_out.pass_on(1)
    sum_out.pass_on(2)
    for sl in lane_tiles(d, 2 * LANES):
        dn[:, sl] = dn[:, sl] + mm(dil[...], win_i[sl, :], NT)
    dn_copy = Send(lambda: (dn.at[pl.ds(theirs, tl), :], dnr), row, other)
    dproj_turned = pq2[...].T[0:nproj, :].astype(bf16)
    for sl in lane_tiles(w, 2 * LANES):
        sm[0:nproj, sl] = mm(dproj_turned, actl[:, sl])
        sm[nproj : nproj + rank, sl] = mm(rank_turned, dpl[:, sl])

    def put_line(line, n):
        for value, sl in zip(read_tot(n), halves):
            sm[line : line + 1, sl] = jnp.sum(value, axis=0, keepdims=True)

    put_line(line_dtb, tot_dtb)
    put_line(line_skip, tot_skip)
    put_line(line_cb, tot_conv)
    for j in range(taps):
        put_line(line_conv + taps - 1 - j, tot_conv + 1 + j)
    def gain_block(b, carry):
        rows = pl.ds(pl.multiple_of(b * STEP, STEP), STEP)
        values = ng[2, rows, :].astype(f32)
        scale = lax.rsqrt(jnp.mean(values * values, axis=-1, keepdims=True) + EPS)
        both = dn[rows, :] * (values * scale)
        return carry + both[0:8] + both[8:16]

    total = lax.fori_loop(0, chunks, gain_block, jnp.zeros((8, d), f32), unroll=4)
    sm[line_gain : line_gain + 1, :] = jnp.sum(total, axis=0, keepdims=True)
    across_tiles = packed // LANES
    for n in range(sm.shape[0] // 16 * tiles):
        to = slice(n // across_tiles * 16, n // across_tiles * 16 + 16)
        to_lanes = tile[n % across_tiles]
        value = sm[n // tiles * 16 : n // tiles * 16 + 16, tile[n % tiles]]
        smb[to, to_lanes] = value.astype(bf16)
        sms[to, to_lanes] = value
    srows = DEPTH * extra
    over_plane = [
        Send(
            lambda s=s: (smb.at[block(plane_place[s], srows), :], sfac.at[s - 1]),
            plane_row[s],
            core,
        )
        for s in range(1, PLANE)
    ]
    sum_in.partial()
    sum_out.pass_on(3)
    sum_gate.pass_on(1)
    sum_gate.pass_on(2)
    sum_out.pass_across(0)
    for copy in over_plane:
        copy.wait_recv()
    total = sms[block(place, srows), :]
    for s in range(PLANE - 1):
        total = total + sfac[s].astype(f32)
    sms[block(place, srows), :] = total
    spb[...] = total.astype(bf16)
    small_depth = [
        Send(lambda s=s: (spb.at[block(z_place[s], extra), :], szr.at[s - 1]), z_row[s], core)
        for s in range(1, DEPTH)
    ]
    sum_out.pass_across(1)
    sum_out.pass_across(2)
    sum_out.pass_across(3)
    for copy in small_depth:
        copy.wait_recv()

    def small_rows(first, count):
        first = (core * TEAM + first) * extra
        return small.at[pl.ds(pl.multiple_of(first, count * extra), count * extra), :]

    own_small = place * DEPTH + pz
    total = sms[block(own_small, extra), :]
    for s in range(DEPTH - 1):
        total = total + szr[s].astype(f32)
    small_rows(own_small, 1)[...] = total.astype(bf16)
    refs = pair_to(lambda: small_rows(own_small, 1))
    small_along = [Send(refs, z_row[s], core) for s in range(1, DEPTH)]
    sum_gate.pass_on(3)
    sum_in.total()

    for sl in lane_tiles(d, 2 * LANES):
        outp[:, sl] = mm(gt[...], wo[:, sl])
    out_copy = Send(lambda: (outp.at[pl.ds(theirs, tl), :], outr), row, other)

    def norm_back(b, carry):
        at = pl.multiple_of(b * STEP, STEP)
        rows = pl.ds(at, STEP)
        values = ng[2, pl.ds(mine + at, STEP), :].astype(f32)
        scale = lax.rsqrt(jnp.mean(values * values, axis=-1, keepdims=True) + EPS)
        unit_rows = values * scale
        inside = (dn[pl.ds(mine + at, STEP), :] + dnr[rows, :]) * lines[0:1, 0:d]
        mean = jnp.mean(inside * unit_rows, axis=-1, keepdims=True)
        given = ng[1, pl.ds(mine + at, STEP), :].astype(f32)
        gtok[rows, :] = (given + scale * (inside - unit_rows * mean)).astype(bf16)
        return carry

    dn_copy.wait_recv()
    lax.fori_loop(0, tl // STEP, norm_back, 0, unroll=4)
    out_copy.wait_recv()
    lax.fori_loop(0, tl // STEP, out_block, 0, unroll=4)

    sum_gate.pass_across(0)
    sum_gate.pass_across(1)
    for copy in small_along:
        copy.wait_recv()
    refs = pair_to(lambda: small_rows(place * DEPTH, DEPTH))
    small_near = [Send(refs, plane_row[s], core) for s in range(1, PLANE)]
    sum_out.finish()
    sum_in.pass_on(1)
    sum_in.pass_on(2)
    sum_gate.pass_across(2)
    sum_gate.pass_across(3)
    sum_in.pass_on(3)
    sum_in.pass_across(0)
    for copy in small_near:
        copy.wait_recv()
    twin_small = Send(pair_to(lambda: small_rows(0, TEAM)), row, other)
    sum_gate.finish()
    for s in (1, 2, 3):
        sum_in.pass_across(s)
    sum_in.finish()
    for copy in sum_out.twin + sum_gate.twin + [twin_small] + sum_in.twin:
        copy.wait_recv()
    for copy in pending:
        copy.wait_send()


def wide_kernel(output, grad_tokens, gout, ggate, ginner, small, *refs):
    out_o, out_t, gin_f, gout_f, *rest = refs
    *rest, wide_in, wide_out, value, sems = rest
    finals, rows = rest[: len(rest) // 2], rest[len(rest) // 2 :]
    steps = wide_in.shape[0]
    cols, lines = wide_in.shape[2], wide_out.shape[1]
    copies = []

    def put(src, dst, *sem):
        copies.append(pltpu.make_async_copy(src, dst, sems.at[sem]))
        copies[-1].start()

    put(output, out_o, 2, 0)
    put(grad_tokens, out_t, 2, 1)
    e, d = ggate.shape
    blocks = e // cols
    for i in range(steps):
        at = slice(i * lines, (i + 1) * lines)
        wide_out[i] = gout[at, :].astype(f32)
        put(wide_out.at[i], gout_f.at[at, :], 1, i)
    for i in range(steps):
        source = ginner if i < blocks else ggate
        first = i % blocks * cols
        wide_in[i] = source[first : first + cols, :].T.astype(f32)
        put(wide_in.at[i], gin_f.at[:, i * cols : (i + 1) * cols], 0, i)

    matrices = [ref for ref in rows if len(ref.shape) == 2]
    vectors = [ref for ref in rows if len(ref.shape) == 1]
    gain = 0.0
    tiles, across = d // LANES, small.shape[1] // LANES
    for core in range(2):
        for n in range(value.shape[0] // 16 * tiles):
            first = (core * TEAM + n // across) * 16
            at_row, at_lane, lane = n // tiles * 16, n % tiles * LANES, n % across * LANES
            value[at_row : at_row + 16, at_lane : at_lane + LANES] = small[
                first : first + 16, lane : lane + LANES
            ].astype(f32)
        at_lanes = slice(core * d, (core + 1) * d)
        at = 0
        for ref in matrices:
            ref[:, at_lanes] = value[at : at + ref.shape[0], :]
            at += ref.shape[0]
        for ref in vectors[:-1]:
            ref[at_lanes] = value[at : at + 1, :].reshape(d)
            at += 1
        gain = gain + value[at : at + 1, :]
    vectors[-1][...] = gain.reshape(d)
    for n, (src, dst) in enumerate(zip(rows, finals)):
        put(src, dst, 3, n)
    for copy in copies:
        copy.wait()


def local(
    tokens, marks, norm_gain, in_weight, conv_weight, conv_bias, x_weight, dt_weight,
    dt_bias, a_log, skip, out_weight, cotangent,
):
    tl, d = tokens.shape[1:]
    e = out_weight.shape[0]
    w = e // lax.axis_size("seq")
    t = tl * lax.axis_size("seq")
    states, rank, nproj, taps = a_log.shape[0], dt_weight.shape[0], x_weight.shape[0], conv_weight.shape[0]
    chunks, span = t // STEP, STEP * states
    quarter = w // PLANE
    zrows = quarter // DEPTH
    lines = -(-(nproj + rank + states + taps + 4) // 16) * 16
    packed = -(-(lines // 16) * (w // LANES) // TEAM) * LANES
    pieces = 16 * TEAM
    vmem = pl.BlockSpec(memory_space=pltpu.VMEM)
    anywhere = pl.BlockSpec(memory_space=pl.ANY)
    wide = pltpu.VMEM((t, w), f32)
    low = pltpu.VMEM((t, w), bf16)
    one = pltpu.VMEM((t, LANES), f32)
    scratch = [
        pltpu.VMEM((d, w), bf16), pltpu.VMEM((d, w), bf16), pltpu.VMEM((w, d), bf16),
        pltpu.VMEM((d,), f32), pltpu.VMEM((taps, w), f32), pltpu.VMEM((e,), f32),
        pltpu.VMEM((nproj, w), bf16), pltpu.VMEM((rank, w), bf16), pltpu.VMEM((e,), f32),
        pltpu.VMEM((states, w), f32), pltpu.VMEM((e,), f32), pltpu.VMEM((8, tl), jnp.int32),
        pltpu.VMEM((3, t, d), bf16), pltpu.VMEM((PLANE - 1, 2, t, d), bf16),
        pltpu.VMEM((8, t), f32), pltpu.VMEM((t + 8, LANES), f32), pltpu.VMEM((8, e), f32),
        pltpu.VMEM((t + 8, w), f32), wide, wide, wide, wide, low, wide, wide, wide, wide, wide, wide, wide,
        one, one, one, one, pltpu.VMEM((LANES, t), f32),
        pltpu.VMEM((t * states // 2, w), bf16), pltpu.VMEM((t * states // 2 + states, w), bf16),
        pltpu.VMEM((chunks, states, LANES), f32), pltpu.VMEM((chunks, states, LANES), f32),
        pltpu.VMEM((t, span), bf16), pltpu.VMEM((t, span), bf16),
        *[pltpu.VMEM((span, w), bf16)] * 4, *[pltpu.VMEM((span, LANES), bf16)] * 4,
        *[pltpu.VMEM((chunks, states, LANES), f32)] * 2,
        pltpu.VMEM((states, LANES), f32), pltpu.VMEM((taps + 3, 8, w), f32),
        low, low, low, low, pltpu.VMEM((3, w, t), bf16), pltpu.VMEM((t + 8, w), f32),
        pltpu.VMEM((t, d), f32), pltpu.VMEM((tl, d), f32),
        pltpu.VMEM((t, d), f32), pltpu.VMEM((tl, d), f32),
        pltpu.VMEM((3, PLANE - 1, quarter, t), bf16), pltpu.VMEM((quarter, d), f32),
        pltpu.VMEM((3, zrows, d), f32), pltpu.VMEM((3, quarter, d), bf16),
        pltpu.VMEM((3, DEPTH - 1, zrows, d), bf16),
        pltpu.VMEM((lines, w), f32), pltpu.VMEM((pieces, packed), bf16), pltpu.VMEM((pieces, packed), f32),
        pltpu.VMEM((PLANE - 1, pieces // PLANE, packed), bf16), pltpu.VMEM((pieces // PLANE, packed), bf16),
        pltpu.VMEM((DEPTH - 1, 16, packed), bf16),
        pltpu.SemaphoreType.DMA((16,)),
        pltpu.SemaphoreType.DMA((160,)), pltpu.SemaphoreType.DMA((160,)),
    ]
    output, grad_tokens, gout, ggate, ginner, small = pl.pallas_call(
        body_kernel,
        out_shape=[
            pltpu.VMEM((tl, d), bf16),
            pltpu.VMEM((tl, d), bf16),
            pltpu.VMEM((e, d), bf16),
            pltpu.VMEM((e, d), bf16),
            pltpu.VMEM((e, d), bf16),
            pltpu.VMEM((2 * TEAM * 16, packed), bf16),
        ],
        in_specs=[anywhere] * 13,
        out_specs=[vmem] * 6,
        scratch_shapes=scratch,
        compiler_params=pltpu.CompilerParams(
            collective_id=0, has_side_effects=True, vmem_limit_bytes=56 * 2**20
        ),
        name="block",
    )(
        tokens.reshape(tl, d), marks.reshape(1, tl), norm_gain, in_weight, conv_weight,
        conv_bias, x_weight, dt_weight, dt_bias, a_log, skip, out_weight, cotangent.reshape(tl, d),
    )

    steps = 8
    shapes = [(nproj, e), (rank, e), (states, e), (taps, e), (e,), (e,), (e,), (d,)]
    wide_shapes = [jax.ShapeDtypeStruct(s, f32) for s in [(d, 2 * e), (e, d)] + shapes]
    output, grad_tokens, *grads = pl.pallas_call(
        wide_kernel,
        out_shape=[jax.ShapeDtypeStruct((tl, d), bf16)] * 2 + wide_shapes,
        in_specs=[vmem] * 6,
        out_specs=[anywhere] * (4 + len(shapes)),
        scratch_shapes=[pltpu.VMEM(s, f32) for s in shapes]
        + [
            pltpu.VMEM((steps, d, 2 * e // steps), f32),
            pltpu.VMEM((steps, e // steps, d), f32),
            pltpu.VMEM((lines, w), f32),
            pltpu.SemaphoreType.DMA((4, steps)),
        ],
        compiler_params=pltpu.CompilerParams(vmem_limit_bytes=40 * 2**20),
        name="widen",
    )(output, grad_tokens, gout, ggate, ginner, small)
    rows = lax.axis_size("rows")
    if rows > TEAM:
        grads = [v * (1.0 / TEAM) for v in lax.psum(grads, "rows")]
    grad_in, grad_out, grad_x, grad_dt, grad_log, grad_conv, g_cb, g_dtb, g_skip, g_gain = grads
    return (
        output[None], grad_tokens[None], g_gain, grad_in, grad_conv, g_cb, grad_x, grad_dt, g_dtb, grad_log,
        g_skip, grad_out,
    )


def solution(mesh):
    split = P("rows", "seq", None)
    whole = P()
    in_specs = (split, P("rows", "seq")) + (whole,) * 10 + (split,)
    out_specs = (split, split) + (whole,) * 10
    return jax.shard_map(local, mesh=mesh, in_specs=in_specs, out_specs=out_specs, check_vma=False)
```
